32 devices in a mesh: tm: 8 (over z, x), row: 4 (over y, core).
Axes of the slice: x: 2, y: 2, z: 4, core: 2. Of those that a mesh axis runs over, the one named last changes fastest.
Arguments:
- inputs: bfloat16 [1, 512, 16, 16, 256], P(None, 'tm', 'row'), may hold values from -6 to 6
- decays: float32 [512, 256], P('tm'), may hold values from 0.4 to 0.999999, as said below
- in_kernel: bfloat16 [3, 3, 256, 256], replicated, may hold values from -0.125 to 0.125
- out_kernel: bfloat16 [3, 3, 256, 256], replicated, may hold values from -0.125 to 0.125
- skip: float32 [256], replicated, may hold values from -1 to 1
- cotangent: bfloat16 [1, 512, 16, 16, 256], P(None, 'tm', 'row'), may hold values from -6 to 6
Outputs:
- outputs: bfloat16 [1, 512, 16, 16, 256], P(None, 'tm', 'row')
- in_kernel_grad: float32 [3, 3, 256, 256], replicated
- out_kernel_grad: float32 [3, 3, 256, 256], replicated
The draws below stay inside these ranges and needn't reach their ends.
Inputs may be any that keep to these rules, and one draw needn't show every extreme that they name: `decays`: strictly below one.
All inputs are finite; a program needn't handle non-finite values.
Results may differ from the reference program's by a relative error of at most 0.0043.
Values may be sent and summed in bfloat16 or wider, within the bound.
No kernel may reach another device: no remote copies, remote signals or barrier semaphores. Data moves between devices by JAX's collectives and lax.ppermute only.
A program may use at most 128 MiB of HBM per device.

```python
import math
import jax
import jax.numpy as jnp
from jax import lax

C = 256
P_SIZE = 256
WD = 16
CLIPS = 1
SEGMENT_LENGTH = 512
H = 16


def draw_decays(key, part):
    sampler_seeds = jax.random.split(key, 6)
    slow_share = 0.55
    is_slow = jax.random.bernoulli(sampler_seeds[0], slow_share, (P_SIZE,))
    slower_decay_rate = jax.random.uniform(sampler_seeds[1], (P_SIZE,), jnp.float32, 0.1, 0.6) / SEGMENT_LENGTH
    fast_rate = jnp.exp(jax.random.uniform(sampler_seeds[2], (P_SIZE,), jnp.float32, math.log(0.02), math.log(0.1)))
    base_rate = jnp.where(is_slow, slower_decay_rate, fast_rate)
    modulation = jnp.exp(jax.random.uniform(sampler_seeds[3], (SEGMENT_LENGTH, 1), jnp.float32, math.log(0.5), math.log(2.0)))
    spike_indices = jax.random.randint(sampler_seeds[4], (3,), 0, SEGMENT_LENGTH)
    marked_timesteps = jnp.any(jnp.arange(SEGMENT_LENGTH)[:, None] == spike_indices[None, :], axis=1)
    spike_amplitude = jax.random.uniform(sampler_seeds[5], (SEGMENT_LENGTH, 1), jnp.float32, 0.6, 0.85)
    gain_factor = jnp.where(marked_timesteps[:, None], spike_amplitude, 1.0)
    return jnp.minimum(jnp.exp(-base_rate[None, :] * modulation) * gain_factor, 0.999999)


def shard_levels(key, shape, cuts, low, largest):
    def one(dim, blocks):
        draws = jax.random.uniform(jax.random.fold_in(jax.random.fold_in(key, 6), dim), (blocks,), jnp.float32, low / len(cuts), largest / len(cuts))
        return jnp.repeat(jnp.exp(draws), shape[dim] // blocks).reshape((-1,) + (1,) * (len(shape) - dim - 1))

    gain = one(*cuts[0])
    for cut in cuts[1:]:
        gain = gain * one(*cut)
    return gain


def normal_values(rng, dims, scale, bound, cuts=(), held_as=jnp.bfloat16):
    values = jax.random.normal(rng, dims, jnp.float32) * scale
    if len(cuts) > 0:
        values = shard_levels(rng, dims, cuts, -0.22, 0.18) * values
    return jnp.clip(values, min=-bound, max=bound).astype(held_as)


def setup_inputs(seed: int = 0) -> dict:
    key_list = jax.random.split(jax.random.key(seed), 7)
    return {
        "inputs": normal_values(key_list[0], (CLIPS, SEGMENT_LENGTH, H, WD, C), 1.0, 6.0, ((1, 8), (2, 4))),
        "decays": draw_decays(jax.random.fold_in(key_list[6], 71), 0),
        "in_kernel": normal_values(key_list[2], (3, 3, C, P_SIZE), (9 * C) ** -0.5, 0.125),
        "out_kernel": normal_values(key_list[3], (3, 3, P_SIZE, C), (9 * P_SIZE) ** -0.5, 0.125),
        "skip": jnp.clip(jax.random.uniform(key_list[4], (C,), jnp.float32, -1.0, 1.0), -1.0, 1.0),
        "cotangent": normal_values(key_list[5], (CLIPS, SEGMENT_LENGTH, H, WD, C), 1.0, 6.0, ((1, 8), (2, 4))),
    }


def conv_same(field, kernel):
    return lax.conv_general_dilated(field.astype(jnp.float32), kernel.astype(jnp.float32), (1, 1), ((1, 1), (1, 1)), dimension_numbers=('NHWC', 'HWIO', 'NHWC'), precision=lax.Precision.HIGHEST)

def tap_grads(field, cotan_field):
    height = cotan_field.shape[1]
    width = cotan_field.shape[2]
    padded = jnp.pad(field.astype(jnp.float32), ((0, 0), (1, 1), (1, 1), (0, 0)))
    cotan_wide = cotan_field.astype(jnp.float32)
    collected = []
    for tap_row in range(3):
        for tap_col in range(3):
            window = padded[:, tap_row:tap_row + height, tap_col:tap_col + width, :]
            collected.append(jnp.einsum('bhwi,bhwo->io', window, cotan_wide, precision=lax.Precision.HIGHEST))
    return jnp.stack(collected).reshape(3, 3, field.shape[3], cotan_field.shape[3])

def reference(inputs, decays, in_kernel, out_kernel, skip, cotangent):
    batch_rows = CLIPS * SEGMENT_LENGTH
    flat_in = inputs.reshape(batch_rows, H, WD, C)
    drive = conv_same(flat_in, in_kernel).reshape(CLIPS, SEGMENT_LENGTH, H, WD, P_SIZE)
    scale_in = jnp.sqrt((1.0 - decays) * (1.0 + decays))

    def forward_step(carry, entries):
        decay_row, scale_row, drive_row = entries
        updated = decay_row * carry + scale_row * drive_row
        return (updated, updated)
    start = jnp.zeros((CLIPS, H, WD, P_SIZE), jnp.float32)
    _, states = lax.scan(forward_step, start, (decays, scale_in, jnp.moveaxis(drive, 1, 0)))
    states = jnp.moveaxis(states, 0, 1)
    state_low = states.astype(jnp.bfloat16)
    flat_state = state_low.reshape(batch_rows, H, WD, P_SIZE)
    mixed_out = conv_same(flat_state, out_kernel).reshape(CLIPS, SEGMENT_LENGTH, H, WD, C)
    outputs = (mixed_out + skip * inputs.astype(jnp.float32)).astype(jnp.bfloat16)
    grad_scale = 1.0 / math.sqrt(CLIPS * SEGMENT_LENGTH * H * WD)
    flat_cot = cotangent.reshape(batch_rows, H, WD, C)
    out_kernel_grad = tap_grads(flat_state, flat_cot) * grad_scale
    flipped = jnp.transpose(jnp.flip(out_kernel, (0, 1)), (0, 1, 3, 2))
    state_cot = conv_same(flat_cot, flipped).reshape(CLIPS, SEGMENT_LENGTH, H, WD, P_SIZE)
    next_decay = jnp.concatenate([decays[1:], jnp.ones_like(decays[:1])], axis=0)

    def backward_step(carry, entries):
        decay_row, cot_row = entries
        updated = cot_row + decay_row * carry
        return (updated, updated)
    _, adjoint = lax.scan(backward_step, start, (next_decay, jnp.moveaxis(state_cot, 1, 0)), reverse=True)
    adjoint = jnp.moveaxis(adjoint, 0, 1)
    drive_cot = (scale_in[None, :, None, None, :] * adjoint).astype(jnp.bfloat16)
    in_kernel_grad = tap_grads(flat_in, drive_cot.reshape(batch_rows, H, WD, P_SIZE)) * grad_scale
    return (outputs, in_kernel_grad, out_kernel_grad)
```

```python
import functools
import math

import jax
import jax.numpy as jnp
from jax import lax
from jax.experimental import pallas as pl
from jax.experimental.pallas import tpu as pltpu
from jax.sharding import PartitionSpec as P

BF16 = jnp.bfloat16
F32 = jnp.float32


def params(mib=44):
    return pltpu.CompilerParams(
        dimension_semantics=("arbitrary",), vmem_limit_bytes=mib * 1024 * 1024
    )


def cost(flops, nbytes):
    return pl.CostEstimate(flops=int(flops), bytes_accessed=int(nbytes), transcendentals=0)


def shifted(cells, width):
    count = cells.shape[0]
    wide = cells.astype(F32)
    column = lax.broadcasted_iota(jnp.int32, (count, 1), 0) % width
    left = jnp.where(column == 0, 0.0, pltpu.roll(wide, 1, 0))
    right = jnp.where(column == width - 1, 0.0, pltpu.roll(wide, count - 1, 0))
    return jnp.concatenate([left.astype(BF16), cells, right.astype(BF16)], axis=1)


def flat(block):
    return block.reshape(-1, block.shape[-1])


def dot(a, b):
    return jnp.dot(a, b, preferred_element_type=F32)


def interior_body(x_ref, w_ref, out_ref, s_ref):
    frames, rows, width, _ = x_ref.shape
    lines = frames * width
    for r in range(rows):
        s_ref[r] = shifted(flat(x_ref[:, r]), width)

    def conv(first, count, taps):
        lhs = jnp.concatenate(
            [flat(s_ref[first + i - 1 : first + i - 1 + count]) for i in taps], axis=1
        )
        rhs = w_ref[taps[0] : taps[-1] + 1].reshape(len(taps) * w_ref.shape[1], w_ref.shape[2])
        out_ref[first : first + count] = dot(lhs, rhs).reshape(count, frames, width, -1)

    conv(1, rows - 2, (0, 1, 2))
    conv(0, 1, (1, 2))
    conv(rows - 1, 1, (0, 1))


def interior_plain_kernel(x_ref, w_ref, out_ref, s_ref):
    interior_body(x_ref, w_ref, out_ref, s_ref)


def interior_flipped_kernel(x_ref, w_ref, out_ref, wt_ref, s_ref):
    @pl.when(pl.program_id(0) == 0)
    def _():
        for i in range(3):
            for j in range(3):
                c = w_ref.shape[3]
                wt_ref[i, j * c : (j + 1) * c, :] = w_ref[2 - i, 2 - j].T

    interior_body(x_ref, wt_ref, out_ref, s_ref)


def interior_conv(x, w, flipped, block):
    frames, rows, width, c = x.shape
    p = w.shape[2] if flipped else w.shape[3]
    part_shape = jax.ShapeDtypeStruct((rows, frames, width, p), F32)
    part_spec = pl.BlockSpec((rows, block, width, p), lambda b: (0, b, 0, 0))
    x_spec = pl.BlockSpec((block, rows, width, c), lambda b: (b, 0, 0, 0))
    scratch = [pltpu.VMEM((rows, block * width, 3 * c), BF16)]
    estimate = cost(2 * frames * rows * width * 9 * c * p, 8 * 2**20)
    taps_spec = pl.BlockSpec((3, 3 * c, p), lambda b: (0, 0, 0))
    if flipped:
        return pl.pallas_call(
            interior_flipped_kernel,
            grid=(frames // block,),
            in_specs=[x_spec, pl.BlockSpec(w.shape, lambda b: (0, 0, 0, 0))],
            out_specs=[part_spec, taps_spec],
            out_shape=[part_shape, jax.ShapeDtypeStruct((3, 3 * c, p), BF16)],
            scratch_shapes=scratch,
            compiler_params=params(),
            cost_estimate=estimate,
            name="interior_cot",
        )(x, w)
    taps = w.reshape(3, 3 * c, p)
    part = pl.pallas_call(
        interior_plain_kernel,
        grid=(frames // block,),
        in_specs=[x_spec, taps_spec],
        out_specs=part_spec,
        out_shape=part_shape,
        scratch_shapes=scratch,
        compiler_params=params(),
        cost_estimate=estimate,
        name="interior_in",
    )(x, taps)
    return part, taps


def scan_kernel(backward, part_ref, up_ref, down_ref, w_ref, decay_ref, local_ref, product_ref, end_ref, carry_ref, run_ref):
    rows, frames, width, p = part_ref.shape
    lines = rows * width

    @pl.when(pl.program_id(0) == 0)
    def _():
        carry_ref[...] = jnp.zeros_like(carry_ref)
        run_ref[...] = jnp.ones_like(run_ref)

    top = dot(shifted(flat(up_ref[...]), width), w_ref[0]).reshape(frames, width, p)
    low = dot(shifted(flat(down_ref[...]), width), w_ref[2]).reshape(frames, width, p)
    decay = decay_ref[...]
    scale = jnp.sqrt((1.0 - decay) * (1.0 + decay))
    state = [carry_ref[r * width : (r + 1) * width] for r in range(rows)]
    run = run_ref[0:1]
    for step in range(frames):
        t = frames - 1 - step if backward else step
        factor = decay[t : t + 1]
        gain = scale[t : t + 1]
        if backward:
            product_ref[t : t + 1] = run
        run = run * factor
        if not backward:
            product_ref[t : t + 1] = run
        for r in range(rows):
            term = part_ref[r, t]
            if r == 0:
                term = term + top[t]
            if r == rows - 1:
                term = term + low[t]
            if backward:
                full = term + state[r]
                local_ref[r, t] = full
                state[r] = factor * full
            else:
                state[r] = factor * state[r] + gain * term
                local_ref[r, t] = state[r]
    for r in range(rows):
        carry_ref[r * width : (r + 1) * width] = state[r]
        end_ref[r * width : (r + 1) * width] = state[r]
    run_ref[...] = jnp.broadcast_to(run, run_ref.shape)
    end_ref[lines : lines + 8] = jnp.broadcast_to(run, (8, p))


def local_scan(part, up, down, taps, decays, backward, block):
    rows, frames, width, p = part.shape
    c = up.shape[-1]
    blocks = frames // block
    at = (lambda b: blocks - 1 - b) if backward else (lambda b: b)
    halo_spec = pl.BlockSpec((block, width, c), lambda b: (at(b), 0, 0))
    part_spec = pl.BlockSpec((rows, block, width, p), lambda b: (0, at(b), 0, 0))
    frame_spec = pl.BlockSpec((block, p), lambda b: (at(b), 0))
    lines = rows * width + 8
    return pl.pallas_call(
        functools.partial(scan_kernel, backward),
        grid=(blocks,),
        in_specs=[
            part_spec,
            halo_spec,
            halo_spec,
            pl.BlockSpec(taps.shape, lambda b: (0, 0, 0)),
            frame_spec,
        ],
        out_specs=[part_spec, frame_spec, pl.BlockSpec((lines, p), lambda b: (0, 0))],
        out_shape=[
            jax.ShapeDtypeStruct(part.shape, F32),
            jax.ShapeDtypeStruct((frames, p), F32),
            jax.ShapeDtypeStruct((lines, p), F32),
        ],
        scratch_shapes=[pltpu.VMEM((rows * width, p), F32), pltpu.VMEM((8, p), F32)],
        compiler_params=params(),
        cost_estimate=cost(4 * frames * width * 3 * c * p, 12 * 2**20),
        name="scan_back" if backward else "scan_fwd",
    )(part, up, down, taps, decays)


def combine(place_ref, ends_ref, total_ref, backward):
    place = place_ref[0]
    count = ends_ref.shape[0]
    lines = total_ref.shape[0]
    total = jnp.zeros(total_ref.shape, F32)
    order = range(count - 1, -1, -1) if backward else range(count)
    for k in order:
        passed = ends_ref[k, lines : lines + 1] * total + ends_ref[k, 0:lines]
        total = jnp.where(k > place if backward else k < place, passed, total)
    total_ref[...] = total


def fill_rim(s_ref, up_ref, x_ref, down_ref):
    _, rows, width, _ = x_ref.shape
    s_ref[0] = shifted(flat(up_ref[...]), width)
    for r in range(rows):
        s_ref[r + 1] = shifted(flat(x_ref[:, r]), width)
    s_ref[rows + 1] = shifted(flat(down_ref[...]), width)


def out_grad_kernel(place_ref, ends_ref, local_ref, product_ref, cot_ref, up_ref, down_ref, low_ref, grad_ref, s_ref, total_ref):
    rows, frames, width, p = local_ref.shape
    c = cot_ref.shape[-1]

    @pl.when(pl.program_id(0) == 0)
    def _():
        combine(place_ref, ends_ref, total_ref, False)
        grad_ref[...] = jnp.zeros_like(grad_ref)

    fill_rim(s_ref, up_ref, cot_ref, down_ref)
    product = product_ref[...]
    turned = []
    for r in range(rows):
        state = local_ref[r] + product[:, None, :] * total_ref[r * width : (r + 1) * width][None]
        low = state.astype(BF16)
        low_ref[r] = low
        turned.append(flat(low).T)
    turned = jnp.concatenate(turned, axis=1)
    for i in range(3):
        gain = dot(turned, flat(s_ref[2 - i : 2 - i + rows]))
        for j in range(3):
            grad_ref[3 * i + j] += gain[:, (2 - j) * c : (3 - j) * c]


def in_grad_kernel(place_ref, ends_ref, local_ref, product_ref, decay_ref, x_ref, up_ref, down_ref, grad_ref, s_ref, total_ref, sum_ref):
    rows, frames, width, p = local_ref.shape
    c = x_ref.shape[-1]

    @pl.when(pl.program_id(0) == 0)
    def _():
        combine(place_ref, ends_ref, total_ref, True)
        sum_ref[...] = jnp.zeros_like(sum_ref)

    fill_rim(s_ref, up_ref, x_ref, down_ref)
    product = product_ref[...]
    decay = decay_ref[...]
    scale = jnp.sqrt((1.0 - decay) * (1.0 + decay))[:, None, :]
    turned = []
    for r in range(rows):
        adjoint = local_ref[r] + product[:, None, :] * total_ref[r * width : (r + 1) * width][None]
        turned.append(flat((scale * adjoint).astype(BF16)).T)
    turned = jnp.concatenate(turned, axis=1)
    for i in range(3):
        sum_ref[i] += dot(turned, flat(s_ref[i : i + rows]))

    @pl.when(pl.program_id(0) == pl.num_programs(0) - 1)
    def _():
        for i in range(3):
            for j in range(3):
                grad_ref[3 * i + j] = sum_ref[i, :, j * c : (j + 1) * c].T


def kernel_grads(place, ends, local, product, x, up, down, decays, block):
    rows, frames, width, p = local.shape
    c = x.shape[-1]
    halo_spec = pl.BlockSpec((block, width, c), lambda b: (b, 0, 0))
    local_spec = pl.BlockSpec((rows, block, width, p), lambda b: (0, b, 0, 0))
    frame_spec = pl.BlockSpec((block, p), lambda b: (b, 0))
    x_spec = pl.BlockSpec((block, rows, width, c), lambda b: (b, 0, 0, 0))
    lead = [
        pl.BlockSpec(memory_space=pltpu.SMEM),
        pl.BlockSpec(ends.shape, lambda b: (0, 0, 0)),
        local_spec,
        frame_spec,
    ]
    tail = [x_spec, halo_spec, halo_spec]
    scratch = [
        pltpu.VMEM((rows + 2, block * width, 3 * c), BF16),
        pltpu.VMEM((rows * width, p), F32),
    ]
    estimate = cost(2 * frames * rows * width * 9 * c * p, 10 * 2**20)
    if decays is None:
        return pl.pallas_call(
            out_grad_kernel,
            grid=(frames // block,),
            in_specs=lead + tail,
            out_specs=[local_spec, pl.BlockSpec((9, p, c), lambda b: (0, 0, 0))],
            out_shape=[
                jax.ShapeDtypeStruct(local.shape, BF16),
                jax.ShapeDtypeStruct((9, p, c), F32),
            ],
            scratch_shapes=scratch,
            compiler_params=params(),
            cost_estimate=estimate,
            name="out_grad",
        )(place, ends, local, product, x, up, down)
    return pl.pallas_call(
        in_grad_kernel,
        grid=(frames // block,),
        in_specs=lead + [frame_spec] + tail,
        out_specs=pl.BlockSpec((9, c, p), lambda b: (0, 0, 0)),
        out_shape=jax.ShapeDtypeStruct((9, c, p), F32),
        scratch_shapes=scratch + [pltpu.VMEM((3, p, 3 * c), F32)],
        compiler_params=params(),
        cost_estimate=estimate,
        name="in_grad",
    )(place, ends, local, product, decays, x, up, down)


def outputs_kernel(low_ref, up_ref, down_ref, w_ref, x_ref, skip_ref, out_ref, s_ref):
    rows, frames, width, p = low_ref.shape
    s_ref[0] = shifted(flat(up_ref[...]), width)
    for r in range(rows):
        s_ref[r + 1] = shifted(flat(low_ref[r]), width)
    s_ref[rows + 1] = shifted(flat(down_ref[...]), width)
    lhs = jnp.concatenate([flat(s_ref[i : i + rows]) for i in range(3)], axis=1)
    mixed = dot(lhs, flat(w_ref[...])).reshape(rows, frames, width, -1)
    skip = skip_ref[...][0:1].reshape(1, 1, -1)
    for r in range(rows):
        out_ref[:, r] = (mixed[r] + skip * x_ref[:, r].astype(F32)).astype(BF16)


def outputs_conv(low, up, down, taps, x, skip, block):
    rows, frames, width, p = low.shape
    c = x.shape[-1]
    halo_spec = pl.BlockSpec((block, width, p), lambda b: (b, 0, 0))
    x_spec = pl.BlockSpec((block, rows, width, c), lambda b: (b, 0, 0, 0))
    return pl.pallas_call(
        outputs_kernel,
        grid=(frames // block,),
        in_specs=[
            pl.BlockSpec((rows, block, width, p), lambda b: (0, b, 0, 0)),
            halo_spec,
            halo_spec,
            pl.BlockSpec(taps.shape, lambda b: (0, 0, 0)),
            x_spec,
            pl.BlockSpec((1, c), lambda b: (0, 0)),
        ],
        out_specs=x_spec,
        out_shape=jax.ShapeDtypeStruct(x.shape, BF16),
        scratch_shapes=[pltpu.VMEM((rows + 2, block * width, 3 * p), BF16)],
        compiler_params=params(),
        cost_estimate=cost(2 * frames * rows * width * 9 * c * p, 8 * 2**20),
        name="outputs_conv",
    )(low, up, down, taps, x, skip)


def row_halo(first, last):
    count = lax.axis_size("row")
    up = lax.ppermute(last, "row", [(i, i + 1) for i in range(count - 1)])
    down = lax.ppermute(first, "row", [(i + 1, i) for i in range(count - 1)])
    return up, down


def reduced_share(grad, scale):
    place = lax.axis_index("row")
    bit = 1
    while bit < lax.axis_size("row"):
        half = grad.shape[0] // 2
        side = (place // bit) % 2
        sent = lax.dynamic_slice_in_dim(grad, (1 - side) * half, half, 0).astype(BF16)
        kept = lax.dynamic_slice_in_dim(grad, side * half, half, 0)
        pairs = [(i, i ^ bit) for i in range(lax.axis_size("row"))]
        grad = kept + lax.ppermute(sent, "row", pairs).astype(F32)
        bit *= 2
    count = lax.axis_size("tm")
    parts = grad.astype(BF16).reshape(count, grad.shape[0] // count, grad.shape[1])
    parts = lax.all_to_all(parts, "tm", 0, 0)
    return (jnp.sum(parts.astype(F32), axis=0) * scale).astype(BF16)


def gathered(share):
    whole = lax.all_gather(share, "tm", axis=0, tiled=True)
    place = lax.axis_index("row")
    bit = lax.axis_size("row") // 2
    while bit >= 1:
        side = (place // bit) % 2
        pairs = [(i, i ^ bit) for i in range(lax.axis_size("row"))]
        other = lax.ppermute(whole, "row", pairs)
        whole = jnp.where(
            side == 0,
            jnp.concatenate([whole, other], axis=0),
            jnp.concatenate([other, whole], axis=0),
        )
        bit //= 2
    return whole.astype(F32)


def per_device(inputs, decays, in_kernel, out_kernel, skip, cotangent):
    clips, frames, rows, width, c = inputs.shape
    p = in_kernel.shape[3]
    block = 16
    grad_scale = 1.0 / math.sqrt(
        clips * frames * lax.axis_size("tm") * rows * lax.axis_size("row") * width
    )
    x = inputs.reshape(frames, rows, width, c)
    cot = cotangent.reshape(frames, rows, width, c)
    place = lax.axis_index("tm").astype(jnp.int32).reshape(1)

    cot_up, cot_down = row_halo(cot[:, 0], cot[:, rows - 1])
    x_up, x_down = row_halo(x[:, 0], x[:, rows - 1])

    cot_part, cot_taps = interior_conv(cot, out_kernel, True, block)
    x_part, x_taps = interior_conv(x, in_kernel, False, block)

    states, running, ends = local_scan(x_part, x_up, x_down, x_taps, decays, False, block)
    all_ends = lax.all_gather(ends, "tm")
    adjoint, trailing, starts = local_scan(
        cot_part, cot_up, cot_down, cot_taps, decays, True, block
    )
    all_starts = lax.all_gather(starts, "tm")

    low, out_grad = kernel_grads(
        place, all_ends, states, running, cot, cot_up, cot_down, None, block
    )
    low_up, low_down = row_halo(low[0], low[rows - 1])
    out_share = reduced_share(out_grad.reshape(-1, c), grad_scale)
    in_grad = kernel_grads(
        place, all_starts, adjoint, trailing, x, x_up, x_down, decays, block
    )
    in_share = reduced_share(in_grad.reshape(-1, p), grad_scale)

    outputs = outputs_conv(
        low, low_up, low_down, out_kernel.reshape(3, 3 * p, c), x, skip.reshape(1, c), block
    )
    return (
        outputs.reshape(inputs.shape),
        gathered(in_share).reshape(in_kernel.shape),
        gathered(out_share).reshape(out_kernel.shape),
    )


def solution(mesh):
    return jax.shard_map(
        per_device,
        mesh=mesh,
        in_specs=(
            P(None, "tm", "row", None, None),
            P("tm", None),
            P(),
            P(),
            P(),
            P(None, "tm", "row", None, None),
        ),
        out_specs=(P(None, "tm", "row", None, None), P(), P()),
        check_vma=False,
    )
```

```python
import functools
import math

import jax
import jax.numpy as jnp
from jax import lax
from jax.experimental import pallas as pl
from jax.experimental.pallas import tpu as pltpu
from jax.sharding import PartitionSpec as P

BF16 = jnp.bfloat16
F32 = jnp.float32


def params(mib=20):
    return pltpu.CompilerParams(
        dimension_semantics=("arbitrary",), vmem_limit_bytes=mib * 1024 * 1024
    )


def cost(flops, nbytes):
    return pl.CostEstimate(flops=int(flops), bytes_accessed=int(nbytes), transcendentals=0)


def shifted(cells, width):
    count = cells.shape[0]
    wide = cells.astype(F32)
    column = lax.broadcasted_iota(jnp.int32, (count, 1), 0) % width
    left = jnp.where(column == 0, 0.0, pltpu.roll(wide, 1, 0))
    right = jnp.where(column == width - 1, 0.0, pltpu.roll(wide, count - 1, 0))
    return jnp.concatenate([left.astype(BF16), cells, right.astype(BF16)], axis=1)


def flat(block):
    return block.reshape(-1, block.shape[-1])


def dot(a, b):
    return jnp.dot(a, b, preferred_element_type=F32)


def interior_body(x_ref, w_ref, out_ref, s_ref):
    frames, rows, width, _ = x_ref.shape
    lines = frames * width
    for r in range(rows):
        s_ref[r] = shifted(flat(x_ref[:, r]), width)

    def conv(first, count, taps):
        lhs = jnp.concatenate(
            [flat(s_ref[first + i - 1 : first + i - 1 + count]) for i in taps], axis=1
        )
        rhs = w_ref[taps[0] : taps[-1] + 1].reshape(len(taps) * w_ref.shape[1], w_ref.shape[2])
        out_ref[first : first + count] = dot(lhs, rhs).reshape(count, frames, width, -1)

    conv(1, rows - 2, (0, 1, 2))
    conv(0, 1, (1, 2))
    conv(rows - 1, 1, (0, 1))


def interior_plain_kernel(x_ref, w_ref, out_ref, s_ref):
    interior_body(x_ref, w_ref, out_ref, s_ref)


def interior_flipped_kernel(x_ref, w_ref, after_ref, out_ref, wt_ref, s_ref):
    @pl.when(pl.program_id(0) == 0)
    def _():
        for i in range(3):
            for j in range(3):
                c = w_ref.shape[3]
                wt_ref[i, j * c : (j + 1) * c, :] = w_ref[2 - i, 2 - j].T

    interior_body(x_ref, wt_ref, out_ref, s_ref)


def interior_conv(x, w, flipped, block, after=None):
    frames, rows, width, c = x.shape
    p = w.shape[2] if flipped else w.shape[3]
    part_shape = jax.ShapeDtypeStruct((rows, frames, width, p), F32)
    part_spec = pl.BlockSpec((rows, block, width, p), lambda b: (0, b, 0, 0))
    x_spec = pl.BlockSpec((block, rows, width, c), lambda b: (b, 0, 0, 0))
    scratch = [pltpu.VMEM((rows, block * width, 3 * c), BF16)]
    estimate = cost(2 * frames * rows * width * 9 * c * p, 8 * 2**20)
    taps_spec = pl.BlockSpec((3, 3 * c, p), lambda b: (0, 0, 0))
    if flipped:
        return pl.pallas_call(
            interior_flipped_kernel,
            grid=(frames // block,),
            in_specs=[
                x_spec,
                pl.BlockSpec(w.shape, lambda b: (0, 0, 0, 0)),
                pl.BlockSpec(memory_space=pl.ANY),
            ],
            out_specs=[part_spec, taps_spec],
            out_shape=[part_shape, jax.ShapeDtypeStruct((3, 3 * c, p), BF16)],
            scratch_shapes=scratch,
            compiler_params=params(),
            cost_estimate=estimate,
            name="interior_cot",
        )(x, w, after)
    taps = w.reshape(3, 3 * c, p)
    part = pl.pallas_call(
        interior_plain_kernel,
        grid=(frames // block,),
        in_specs=[x_spec, taps_spec],
        out_specs=part_spec,
        out_shape=part_shape,
        scratch_shapes=scratch,
        compiler_params=params(),
        cost_estimate=estimate,
        name="interior_in",
    )(x, taps)
    return part, taps


def scan_kernel(backward, part_ref, up_ref, down_ref, w_ref, decay_ref, local_ref, product_ref, end_ref, carry_ref, run_ref):
    rows, frames, width, p = part_ref.shape
    lines = rows * width

    @pl.when(pl.program_id(0) == 0)
    def _():
        carry_ref[...] = jnp.zeros_like(carry_ref)
        run_ref[...] = jnp.ones_like(run_ref)

    top = dot(shifted(flat(up_ref[...]), width), w_ref[0]).reshape(frames, width, p)
    low = dot(shifted(flat(down_ref[...]), width), w_ref[2]).reshape(frames, width, p)
    decay = decay_ref[...]
    scale = jnp.sqrt((1.0 - decay) * (1.0 + decay))
    state = [carry_ref[r * width : (r + 1) * width] for r in range(rows)]
    run = run_ref[0:1]
    for step in range(frames):
        t = frames - 1 - step if backward else step
        factor = decay[t : t + 1]
        gain = scale[t : t + 1]
        if backward:
            product_ref[t : t + 1] = run
        run = run * factor
        if not backward:
            product_ref[t : t + 1] = run
        for r in range(rows):
            term = part_ref[r, t]
            if r == 0:
                term = term + top[t]
            if r == rows - 1:
                term = term + low[t]
            if backward:
                full = term + state[r]
                local_ref[r, t] = full
                state[r] = factor * full
            else:
                state[r] = factor * state[r] + gain * term
                local_ref[r, t] = state[r]
    for r in range(rows):
        carry_ref[r * width : (r + 1) * width] = state[r]
        end_ref[r * width : (r + 1) * width] = state[r]
    run_ref[...] = jnp.broadcast_to(run, run_ref.shape)
    end_ref[lines : lines + 8] = jnp.broadcast_to(run, (8, p))


def local_scan(part, up, down, taps, decays, backward, block):
    rows, frames, width, p = part.shape
    c = up.shape[-1]
    blocks = frames // block
    at = (lambda b: blocks - 1 - b) if backward else (lambda b: b)
    halo_spec = pl.BlockSpec((block, width, c), lambda b: (at(b), 0, 0))
    part_spec = pl.BlockSpec((rows, block, width, p), lambda b: (0, at(b), 0, 0))
    frame_spec = pl.BlockSpec((block, p), lambda b: (at(b), 0))
    lines = rows * width + 8
    return pl.pallas_call(
        functools.partial(scan_kernel, backward),
        grid=(blocks,),
        in_specs=[
            part_spec,
            halo_spec,
            halo_spec,
            pl.BlockSpec(taps.shape, lambda b: (0, 0, 0)),
            frame_spec,
        ],
        out_specs=[part_spec, frame_spec, pl.BlockSpec((lines, p), lambda b: (0, 0))],
        out_shape=[
            jax.ShapeDtypeStruct(part.shape, F32),
            jax.ShapeDtypeStruct((frames, p), F32),
            jax.ShapeDtypeStruct((lines, p), F32),
        ],
        scratch_shapes=[pltpu.VMEM((rows * width, p), F32), pltpu.VMEM((8, p), F32)],
        compiler_params=params(),
        cost_estimate=cost(4 * frames * width * 3 * c * p, 12 * 2**20),
        name="scan_back" if backward else "scan_fwd",
    )(part, up, down, taps, decays)


def combine(place_ref, ends_ref, total_ref, backward):
    place = place_ref[0]
    count = ends_ref.shape[0]
    lines = total_ref.shape[0]
    total = jnp.zeros(total_ref.shape, F32)
    order = range(count - 1, -1, -1) if backward else range(count)
    for k in order:
        passed = ends_ref[k, lines : lines + 1] * total + ends_ref[k, 0:lines]
        total = jnp.where(k > place if backward else k < place, passed, total)
    total_ref[...] = total


def fill_rim(s_ref, up_ref, x_ref, down_ref):
    _, rows, width, _ = x_ref.shape
    s_ref[0] = shifted(flat(up_ref[...]), width)
    for r in range(rows):
        s_ref[r + 1] = shifted(flat(x_ref[:, r]), width)
    s_ref[rows + 1] = shifted(flat(down_ref[...]), width)


def out_grad_kernel(place_ref, ends_ref, local_ref, product_ref, cot_ref, up_ref, down_ref, low_ref, first_ref, last_ref, grad_ref, s_ref, total_ref):
    rows, frames, width, p = local_ref.shape
    c = cot_ref.shape[-1]

    @pl.when(pl.program_id(0) == 0)
    def _():
        combine(place_ref, ends_ref, total_ref, False)
        grad_ref[...] = jnp.zeros_like(grad_ref)

    fill_rim(s_ref, up_ref, cot_ref, down_ref)
    product = product_ref[...]
    turned = []
    for r in range(rows):
        state = local_ref[r] + product[:, None, :] * total_ref[r * width : (r + 1) * width][None]
        low = state.astype(BF16)
        low_ref[r] = low
        if r == 0:
            first_ref[...] = low
        if r == rows - 1:
            last_ref[...] = low
        turned.append(flat(low).T)
    turned = jnp.concatenate(turned, axis=1)
    for i in range(3):
        gain = dot(turned, flat(s_ref[2 - i : 2 - i + rows]))
        for j in range(3):
            grad_ref[3 * i + j] += gain[:, (2 - j) * c : (3 - j) * c]


def in_grad_kernel(place_ref, ends_ref, local_ref, product_ref, decay_ref, x_ref, up_ref, down_ref, after_ref, grad_ref, s_ref, total_ref, sum_ref):
    rows, frames, width, p = local_ref.shape
    c = x_ref.shape[-1]

    @pl.when(pl.program_id(0) == 0)
    def _():
        combine(place_ref, ends_ref, total_ref, True)
        sum_ref[...] = jnp.zeros_like(sum_ref)

    fill_rim(s_ref, up_ref, x_ref, down_ref)
    product = product_ref[...]
    decay = decay_ref[...]
    scale = jnp.sqrt((1.0 - decay) * (1.0 + decay))[:, None, :]
    turned = []
    for r in range(rows):
        adjoint = local_ref[r] + product[:, None, :] * total_ref[r * width : (r + 1) * width][None]
        turned.append(flat((scale * adjoint).astype(BF16)).T)
    turned = jnp.concatenate(turned, axis=1)
    for i in range(3):
        sum_ref[i] += dot(turned, flat(s_ref[i : i + rows]))

    @pl.when(pl.program_id(0) == pl.num_programs(0) - 1)
    def _():
        for i in range(3):
            for j in range(3):
                grad_ref[3 * i + j] = sum_ref[i, :, j * c : (j + 1) * c].T


def kernel_grads(place, ends, local, product, x, up, down, decays, block, after=None):
    rows, frames, width, p = local.shape
    c = x.shape[-1]
    halo_spec = pl.BlockSpec((block, width, c), lambda b: (b, 0, 0))
    local_spec = pl.BlockSpec((rows, block, width, p), lambda b: (0, b, 0, 0))
    frame_spec = pl.BlockSpec((block, p), lambda b: (b, 0))
    x_spec = pl.BlockSpec((block, rows, width, c), lambda b: (b, 0, 0, 0))
    lead = [
        pl.BlockSpec(memory_space=pltpu.SMEM),
        pl.BlockSpec(ends.shape, lambda b: (0, 0, 0)),
        local_spec,
        frame_spec,
    ]
    tail = [x_spec, halo_spec, halo_spec]
    scratch = [
        pltpu.VMEM((rows + 2, block * width, 3 * c), BF16),
        pltpu.VMEM((rows * width, p), F32),
    ]
    estimate = cost(2 * frames * rows * width * 9 * c * p, 10 * 2**20)
    if decays is None:
        return pl.pallas_call(
            out_grad_kernel,
            grid=(frames // block,),
            in_specs=lead + tail,
            out_specs=[
                local_spec,
                pl.BlockSpec((block, width, p), lambda b: (b, 0, 0)),
                pl.BlockSpec((block, width, p), lambda b: (b, 0, 0)),
                pl.BlockSpec((9, p, c), lambda b: (0, 0, 0)),
            ],
            out_shape=[
                jax.ShapeDtypeStruct(local.shape, BF16),
                jax.ShapeDtypeStruct((frames, width, p), BF16),
                jax.ShapeDtypeStruct((frames, width, p), BF16),
                jax.ShapeDtypeStruct((9, p, c), F32),
            ],
            scratch_shapes=scratch,
            compiler_params=params(),
            cost_estimate=estimate,
            name="out_grad",
        )(place, ends, local, product, x, up, down)
    return pl.pallas_call(
        in_grad_kernel,
        grid=(frames // block,),
        in_specs=lead + [frame_spec] + tail + [pl.BlockSpec(memory_space=pl.ANY)],
        out_specs=pl.BlockSpec((9, c, p), lambda b: (0, 0, 0)),
        out_shape=jax.ShapeDtypeStruct((9, c, p), F32),
        scratch_shapes=scratch + [pltpu.VMEM((3, p, 3 * c), F32)],
        compiler_params=params(),
        cost_estimate=estimate,
        name="in_grad",
    )(place, ends, local, product, decays, x, up, down, after)


def outputs_kernel(low_ref, up_ref, down_ref, w_ref, x_ref, skip_ref, out_ref, s_ref):
    rows, frames, width, p = low_ref.shape
    s_ref[0] = shifted(flat(up_ref[...]), width)
    for r in range(rows):
        s_ref[r + 1] = shifted(flat(low_ref[r]), width)
    s_ref[rows + 1] = shifted(flat(down_ref[...]), width)
    lhs = jnp.concatenate([flat(s_ref[i : i + rows]) for i in range(3)], axis=1)
    mixed = dot(lhs, flat(w_ref[...])).reshape(rows, frames, width, -1)
    skip = skip_ref[...][0:1].reshape(1, 1, -1)
    for r in range(rows):
        out_ref[:, r] = (mixed[r] + skip * x_ref[:, r].astype(F32)).astype(BF16)


def outputs_conv(low, up, down, taps, x, skip, block):
    rows, frames, width, p = low.shape
    c = x.shape[-1]
    halo_spec = pl.BlockSpec((block, width, p), lambda b: (b, 0, 0))
    x_spec = pl.BlockSpec((block, rows, width, c), lambda b: (b, 0, 0, 0))
    return pl.pallas_call(
        outputs_kernel,
        grid=(frames // block,),
        in_specs=[
            pl.BlockSpec((rows, block, width, p), lambda b: (0, b, 0, 0)),
            halo_spec,
            halo_spec,
            pl.BlockSpec(taps.shape, lambda b: (0, 0, 0)),
            x_spec,
            pl.BlockSpec((1, c), lambda b: (0, 0)),
        ],
        out_specs=x_spec,
        out_shape=jax.ShapeDtypeStruct(x.shape, BF16),
        scratch_shapes=[pltpu.VMEM((rows + 2, block * width, 3 * p), BF16)],
        compiler_params=params(),
        cost_estimate=cost(2 * frames * rows * width * 9 * c * p, 8 * 2**20),
        name="outputs_conv",
    )(low, up, down, taps, x, skip)


def edge_rows_kernel(x_ref, after_ref, first_ref, last_ref, sems):
    rows = x_ref.shape[1]
    first = pltpu.make_async_copy(x_ref.at[:, 0], first_ref, sems.at[0])
    last = pltpu.make_async_copy(x_ref.at[:, rows - 1], last_ref, sems.at[1])
    first.start()
    last.start()
    first.wait()
    last.wait()


def edge_rows(x, after):
    frames, rows, width, c = x.shape
    anywhere = pl.BlockSpec(memory_space=pl.ANY)
    line = jax.ShapeDtypeStruct((frames, width, c), x.dtype)
    return pl.pallas_call(
        edge_rows_kernel,
        in_specs=[anywhere, anywhere],
        out_specs=[anywhere, anywhere],
        out_shape=[line, line],
        scratch_shapes=[pltpu.SemaphoreType.DMA((2,))],
        compiler_params=pltpu.CompilerParams(vmem_limit_bytes=2**20),
        cost_estimate=cost(0, 2**21),
        name="edge_rows",
    )(x, after)


def row_halo(first, last):
    axes = ("y", "core")
    count = lax.axis_size("y") * lax.axis_size("core")
    up = lax.ppermute(last, axes, [(i, i + 1) for i in range(count - 1)])
    down = lax.ppermute(first, axes, [(i + 1, i) for i in range(count - 1)])
    return up, down


def spread(block, axes):
    count = math.prod(lax.axis_size(name) for name in axes)
    return lax.all_to_all(jnp.broadcast_to(block[None], (count,) + block.shape), axes, 0, 0)


def scattered_sum(part, axes):
    count = math.prod(lax.axis_size(name) for name in axes)
    parts = part.astype(BF16).reshape(count, part.shape[0] // count, part.shape[1])
    return jnp.sum(lax.all_to_all(parts, axes, 0, 0).astype(F32), axis=0)


CORES = [(0, 1), (1, 0)]


def reduced_share(grad, scale):
    side = lax.axis_index("core")
    half = grad.shape[0] // 2
    sent = lax.dynamic_slice_in_dim(grad, (1 - side) * half, half, 0).astype(BF16)
    kept = lax.dynamic_slice_in_dim(grad, side * half, half, 0)
    part = kept + lax.ppermute(sent, "core", CORES).astype(F32)
    part = scattered_sum(part, ("x", "y"))
    part = scattered_sum(part, ("a",))
    return (part * scale).astype(BF16)


def merge_kernel(side_ref, own_ref, other_ref, out_ref):
    @pl.when(pl.program_id(0) == 0)
    def _():
        out_ref[...] = own_ref[...].astype(F32)

    @pl.when(pl.program_id(0) == 1)
    def _():
        out_ref[...] = other_ref[...].astype(F32)


def gathered(share):
    part = flat(spread(share, ("a",)))
    own = flat(spread(part, ("x", "y")))
    other = lax.ppermute(own, "core", CORES)
    side = lax.axis_index("core").astype(jnp.int32).reshape(1)
    half, c = own.shape
    part_spec = pl.BlockSpec((half, c), lambda g, side: (0, 0))
    return pl.pallas_call(
        merge_kernel,
        grid_spec=pltpu.PrefetchScalarGridSpec(
            num_scalar_prefetch=1,
            grid=(2,),
            in_specs=[part_spec, part_spec],
            out_specs=pl.BlockSpec((half, c), lambda g, side: (jnp.bitwise_xor(g, side[0]), 0)),
        ),
        out_shape=jax.ShapeDtypeStruct((2 * half, c), F32),
        compiler_params=params(8),
        cost_estimate=cost(0, 10 * half * c),
        name="merge",
    )(side, own, other)


def per_device(inputs, decays, in_kernel, out_kernel, skip, cotangent):
    clips, frames, rows, width, c = inputs.shape
    p = in_kernel.shape[3]
    block = 16
    devices = math.prod(lax.axis_size(name) for name in ("a", "x", "y", "core"))
    grad_scale = 1.0 / math.sqrt(clips * frames * rows * width * devices)
    x = inputs.reshape(frames, rows, width, c)
    cot = cotangent.reshape(frames, rows, width, c)
    place = lax.axis_index(("a", "x")).astype(jnp.int32).reshape(1)

    x_up, x_down = row_halo(*edge_rows(x, decays))
    x_part, x_taps = interior_conv(x, in_kernel, False, block)
    cot_up, cot_down = row_halo(*edge_rows(cot, x_part))
    states, running, ends = local_scan(x_part, x_up, x_down, x_taps, decays, False, block)
    all_ends = spread(ends, ("a", "x"))
    cot_part, cot_taps = interior_conv(cot, out_kernel, True, block, ends)
    adjoint, trailing, starts = local_scan(
        cot_part, cot_up, cot_down, cot_taps, decays, True, block
    )
    all_starts = spread(starts, ("a", "x"))

    low, low_first, low_last, out_grad = kernel_grads(
        place, all_ends, states, running, cot, cot_up, cot_down, None, block
    )
    out_share = reduced_share(out_grad.reshape(-1, c), grad_scale)
    low_up, low_down = row_halo(low_first, low_last)
    in_grad = kernel_grads(
        place, all_starts, adjoint, trailing, x, x_up, x_down, decays, block, low_first
    )
    in_share = reduced_share(in_grad.reshape(-1, p), grad_scale)

    outputs = outputs_conv(
        low, low_up, low_down, out_kernel.reshape(3, 3 * p, c), x, skip.reshape(1, c), block
    )
    return (
        outputs.reshape(inputs.shape),
        gathered(in_share).reshape(in_kernel.shape),
        gathered(out_share).reshape(out_kernel.shape),
    )


def solution(mesh):
    frames = mesh.shape["tm"]
    rows = mesh.shape["row"]
    fine = jax.sharding.Mesh(
        mesh.devices.reshape(frames // 2, 2, rows // 2, 2), ("a", "x", "y", "core")
    )
    cells = P(None, ("a", "x"), ("y", "core"), None, None)
    return jax.shard_map(
        per_device,
        mesh=fine,
        in_specs=(cells, P(("a", "x"), None), P(), P(), P(), cells),
        out_specs=(cells, P(), P()),
        check_vma=False,
    )
```

```python
import functools
import math

import jax
import jax.numpy as jnp
from jax import lax
from jax.experimental import pallas as pl
from jax.experimental.pallas import tpu as pltpu
from jax.sharding import PartitionSpec as P

BF16 = jnp.bfloat16
F32 = jnp.float32


SCALARS = pl.BlockSpec(memory_space=pltpu.SMEM)
ANYWHERE = pl.BlockSpec(memory_space=pl.ANY)
TOKEN = jax.ShapeDtypeStruct((8, 128), F32)
TOKEN_SPEC = pl.BlockSpec((8, 128), lambda *b: (0, 0))


def params(mib=20):
    return pltpu.CompilerParams(
        dimension_semantics=("arbitrary",), vmem_limit_bytes=mib * 1024 * 1024
    )


def cost(flops, nbytes):
    return pl.CostEstimate(flops=int(flops), bytes_accessed=int(nbytes), transcendentals=0)


def shifted(cells, width):
    count = cells.shape[0]
    wide = cells.astype(F32)
    column = lax.broadcasted_iota(jnp.int32, (count, 1), 0) % width
    left = jnp.where(column == 0, 0.0, pltpu.roll(wide, 1, 0))
    right = jnp.where(column == width - 1, 0.0, pltpu.roll(wide, count - 1, 0))
    return jnp.concatenate([left.astype(BF16), cells, right.astype(BF16)], axis=1)


def flat(block):
    return block.reshape(-1, block.shape[-1])


def dot(a, b):
    return jnp.dot(a, b, preferred_element_type=F32)


def interior_body(x_ref, w_ref, out_ref, s_ref):
    frames, rows, width, _ = x_ref.shape
    lines = frames * width
    for r in range(rows):
        s_ref[r] = shifted(flat(x_ref[:, r]), width)

    def conv(first, count, taps):
        lhs = jnp.concatenate(
            [flat(s_ref[first + i - 1 : first + i - 1 + count]) for i in taps], axis=1
        )
        rhs = w_ref[taps[0] : taps[-1] + 1].reshape(len(taps) * w_ref.shape[1], w_ref.shape[2])
        out_ref[first : first + count] = dot(lhs, rhs).reshape(count, frames, width, -1)

    conv(1, rows - 2, (0, 1, 2))
    conv(0, 1, (1, 2))
    conv(rows - 1, 1, (0, 1))


def interior_plain_kernel(x_ref, w_ref, out_ref, s_ref):
    interior_body(x_ref, w_ref, out_ref, s_ref)


def interior_flipped_kernel(x_ref, w_ref, out_ref, wt_ref, s_ref):
    @pl.when(pl.program_id(0) == 0)
    def _():
        for i in range(3):
            for j in range(3):
                c = w_ref.shape[3]
                wt_ref[i, j * c : (j + 1) * c, :] = w_ref[2 - i, 2 - j].T

    interior_body(x_ref, wt_ref, out_ref, s_ref)


def interior_conv(x, w, flipped, block):
    frames, rows, width, c = x.shape
    p = w.shape[2] if flipped else w.shape[3]
    part_shape = jax.ShapeDtypeStruct((rows, frames, width, p), F32)
    part_spec = pl.BlockSpec((rows, block, width, p), lambda b: (0, b, 0, 0))
    x_spec = pl.BlockSpec((block, rows, width, c), lambda b: (b, 0, 0, 0))
    scratch = [pltpu.VMEM((rows, block * width, 3 * c), BF16)]
    estimate = cost(2 * frames * rows * width * 9 * c * p, 8 * 2**20)
    taps_spec = pl.BlockSpec((3, 3 * c, p), lambda b: (0, 0, 0))
    if flipped:
        return pl.pallas_call(
            interior_flipped_kernel,
            grid=(frames // block,),
            in_specs=[
                x_spec,
                pl.BlockSpec(w.shape, lambda b: (0, 0, 0, 0)),
            ],
            out_specs=[part_spec, taps_spec],
            out_shape=[part_shape, jax.ShapeDtypeStruct((3, 3 * c, p), BF16)],
            scratch_shapes=scratch,
            compiler_params=params(),
            cost_estimate=estimate,
            name="interior_cot",
        )(x, w)
    taps = w.reshape(3, 3 * c, p)
    part = pl.pallas_call(
        interior_plain_kernel,
        grid=(frames // block,),
        in_specs=[x_spec, taps_spec],
        out_specs=part_spec,
        out_shape=part_shape,
        scratch_shapes=scratch,
        compiler_params=params(),
        cost_estimate=estimate,
        name="interior_in",
    )(x, taps)
    return part, taps


def scan_kernel(backward, part_ref, up_ref, down_ref, w_ref, decay_ref, *refs):
    if backward:
        place_ref, ahead_ref, local_ref, product_ref, end_ref, carry_ref, run_ref = refs
    else:
        local_ref, product_ref, end_ref, carry_ref, run_ref = refs
    rows, frames, width, p = part_ref.shape
    lines = rows * width

    @pl.when(pl.program_id(0) == 0)
    def _():
        carry_ref[...] = jnp.zeros_like(carry_ref)
        run_ref[...] = jnp.ones_like(run_ref)

    top = dot(shifted(flat(up_ref[...]), width), w_ref[0]).reshape(frames, width, p)
    low = dot(shifted(flat(down_ref[...]), width), w_ref[2]).reshape(frames, width, p)
    decay = decay_ref[...]
    scale = jnp.sqrt((1.0 - decay) * (1.0 + decay))
    state = [carry_ref[r * width : (r + 1) * width] for r in range(rows)]
    run = run_ref[0:1]
    for step in range(frames):
        t = frames - 1 - step if backward else step
        factor = decay[t : t + 1]
        gain = scale[t : t + 1]
        if backward:
            product_ref[t : t + 1] = run
        run = run * factor
        if not backward:
            product_ref[t : t + 1] = run
        for r in range(rows):
            term = part_ref[r, t]
            if r == 0:
                term = term + top[t]
            if r == rows - 1:
                term = term + low[t]
            if backward:
                full = term + state[r]
                local_ref[r, t] = full
                state[r] = factor * full
            else:
                state[r] = factor * state[r] + gain * term
                local_ref[r, t] = state[r]
    for r in range(rows):
        carry_ref[r * width : (r + 1) * width] = state[r]
    run_ref[...] = jnp.broadcast_to(run, run_ref.shape)

    @pl.when(pl.program_id(0) == pl.num_programs(0) - 1)
    def _():
        if not backward:
            end_ref[...] = jnp.concatenate(state, axis=0)
        else:
            high = run.astype(BF16).astype(F32)
            products = [jnp.broadcast_to(high, (8, p)), jnp.broadcast_to(run - high, (8, p))]
            leading = jnp.concatenate(state + products, axis=0).astype(BF16)
            ending = jnp.concatenate([ahead_ref[...]] + products, axis=0).astype(BF16)
            for k in range(end_ref.shape[0]):
                end_ref[k] = jnp.where(k > place_ref[0], ending, leading)


def local_scan(part, up, down, half, taps, decays, block, places=None, ahead=None):
    backward = ahead is not None
    rows, frames, width, p = part.shape
    c = up.shape[-1]
    blocks = frames // block
    at = (lambda b: blocks - 1 - b) if backward else (lambda b: b)
    halo_spec = pl.BlockSpec((None, block, width, c), lambda b: (half, at(b), 0, 0))
    part_spec = pl.BlockSpec((rows, block, width, p), lambda b: (0, at(b), 0, 0))
    frame_spec = pl.BlockSpec((block, p), lambda b: (at(b), 0))
    lines = rows * width
    in_specs = [
        part_spec,
        halo_spec,
        halo_spec,
        pl.BlockSpec(taps.shape, lambda b: (0, 0, 0)),
        frame_spec,
    ]
    operands = [part, up, down, taps, decays]
    if backward:
        count = lax.axis_size("a") * lax.axis_size("x")
        in_specs += [SCALARS, pl.BlockSpec((lines, p), lambda b: (0, 0))]
        operands += [places, ahead]
        end_spec = pl.BlockSpec((count, lines + 16, p), lambda b: (0, 0, 0))
        end_shape = jax.ShapeDtypeStruct((count, lines + 16, p), BF16)
    else:
        end_spec = pl.BlockSpec((lines, p), lambda b: (0, 0))
        end_shape = jax.ShapeDtypeStruct((lines, p), F32)
    return pl.pallas_call(
        functools.partial(scan_kernel, backward),
        grid=(blocks,),
        in_specs=in_specs,
        out_specs=[part_spec, frame_spec, end_spec],
        out_shape=[
            jax.ShapeDtypeStruct(part.shape, F32),
            jax.ShapeDtypeStruct((frames, p), F32),
            end_shape,
        ],
        scratch_shapes=[pltpu.VMEM((lines, p), F32), pltpu.VMEM((8, p), F32)],
        compiler_params=params(),
        cost_estimate=cost(4 * frames * width * 3 * c * p, 12 * 2**20),
        name="scan_back" if backward else "scan_fwd",
    )(*operands)


def combine(place_ref, ends_ref, total_ref, backward):
    place = place_ref[0]
    count = ends_ref.shape[0]
    lines = total_ref.shape[0]
    total = jnp.zeros(total_ref.shape, F32)
    order = range(count - 1, -1, -1) if backward else range(count)
    for k in order:
        block = ends_ref[k].astype(F32)
        product = block[lines : lines + 1] + block[lines + 8 : lines + 9]
        passed = product * total + block[0:lines]
        total = jnp.where(k > place if backward else k < place, passed, total)
    total_ref[...] = total


def split_halves(place_ref, sum_ref, sent_ref, kept_ref):
    half = kept_ref.shape[0]
    side = place_ref[1]
    sent_ref[...] = sum_ref[pl.ds(pl.multiple_of((1 - side) * half, 8), half)].astype(BF16)
    kept_ref[...] = sum_ref[pl.ds(pl.multiple_of(side * half, 8), half)]


def fill_rim(s_ref, up_ref, x_ref, down_ref):
    _, rows, width, _ = x_ref.shape
    s_ref[0] = shifted(flat(up_ref[...]), width)
    for r in range(rows):
        s_ref[r + 1] = shifted(flat(x_ref[:, r]), width)
    s_ref[rows + 1] = shifted(flat(down_ref[...]), width)


def out_grad_kernel(place_ref, ends_ref, local_ref, product_ref, cot_ref, up_ref, down_ref, low_ref, first_ref, last_ref, sent_ref, kept_ref, token_ref, s_ref, total_ref, sum_ref):
    rows, frames, width, p = local_ref.shape
    c = cot_ref.shape[-1]

    @pl.when(pl.program_id(0) == 0)
    def _():
        combine(place_ref, ends_ref, total_ref, False)
        sum_ref[...] = jnp.zeros_like(sum_ref)
        token_ref[...] = jnp.zeros_like(token_ref)

    fill_rim(s_ref, up_ref, cot_ref, down_ref)
    product = product_ref[...]
    turned = []
    for r in range(rows):
        state = local_ref[r] + product[:, None, :] * total_ref[r * width : (r + 1) * width][None]
        low = state.astype(BF16)
        low_ref[r] = low
        if r == 0:
            first_ref[...] = low
        if r == rows - 1:
            last_ref[...] = low
        turned.append(flat(low).T)
    turned = jnp.concatenate(turned, axis=1)
    for i in range(3):
        gain = dot(turned, flat(s_ref[2 - i : 2 - i + rows]))
        for j in range(3):
            tap = 3 * i + j
            sum_ref[tap * p : (tap + 1) * p] += gain[:, (2 - j) * c : (3 - j) * c]

    @pl.when(pl.program_id(0) == pl.num_programs(0) - 1)
    def _():
        split_halves(place_ref, sum_ref, sent_ref, kept_ref)


def in_grad_kernel(place_ref, ends_ref, local_ref, product_ref, decay_ref, x_ref, up_ref, down_ref, after_ref, sent_ref, kept_ref, token_ref, s_ref, total_ref, sum_ref, flat_ref):
    rows, frames, width, p = local_ref.shape
    c = x_ref.shape[-1]

    @pl.when(pl.program_id(0) == 0)
    def _():
        combine(place_ref, ends_ref, total_ref, True)
        sum_ref[...] = jnp.zeros_like(sum_ref)
        token_ref[...] = jnp.zeros_like(token_ref)

    fill_rim(s_ref, up_ref, x_ref, down_ref)
    product = product_ref[...]
    decay = decay_ref[...]
    scale = jnp.sqrt((1.0 - decay) * (1.0 + decay))[:, None, :]
    turned = []
    for r in range(rows):
        adjoint = local_ref[r] + product[:, None, :] * total_ref[r * width : (r + 1) * width][None]
        turned.append(flat((scale * adjoint).astype(BF16)).T)
    turned = jnp.concatenate(turned, axis=1)
    for i in range(3):
        sum_ref[i] += dot(turned, flat(s_ref[i : i + rows]))

    @pl.when(pl.program_id(0) == pl.num_programs(0) - 1)
    def _():
        for i in range(3):
            for j in range(3):
                tap = 3 * i + j
                flat_ref[tap * c : (tap + 1) * c] = sum_ref[i, :, j * c : (j + 1) * c].T
        split_halves(place_ref, flat_ref, sent_ref, kept_ref)


def kernel_grads(places, ends, local, product, x, up, down, half, decays, block, after=None):
    rows, frames, width, p = local.shape
    c = x.shape[-1]
    halo_spec = pl.BlockSpec((None, block, width, c), lambda b: (half, b, 0, 0))
    local_spec = pl.BlockSpec((rows, block, width, p), lambda b: (0, b, 0, 0))
    frame_spec = pl.BlockSpec((block, p), lambda b: (b, 0))
    x_spec = pl.BlockSpec((block, rows, width, c), lambda b: (b, 0, 0, 0))
    lead = [SCALARS, pl.BlockSpec(ends.shape, lambda b: (0, 0, 0)), local_spec, frame_spec]
    tail = [x_spec, halo_spec, halo_spec]
    scratch = [
        pltpu.VMEM((rows + 2, block * width, 3 * c), BF16),
        pltpu.VMEM((rows * width, p), F32),
    ]
    estimate = cost(2 * frames * rows * width * 9 * c * p, 10 * 2**20)
    forward = decays is None
    lines, columns = (9 * p // 2, c) if forward else (9 * c // 2, p)
    grad_specs = [pl.BlockSpec((lines, columns), lambda b: (0, 0))] * 2 + [TOKEN_SPEC]
    grad_shapes = [
        jax.ShapeDtypeStruct((lines, columns), BF16),
        jax.ShapeDtypeStruct((lines, columns), F32),
        TOKEN,
    ]
    if forward:
        line_spec = pl.BlockSpec((block, width, p), lambda b: (b, 0, 0))
        line = jax.ShapeDtypeStruct((frames, width, p), BF16)
        return pl.pallas_call(
            out_grad_kernel,
            grid=(frames // block,),
            in_specs=lead + tail,
            out_specs=[local_spec, line_spec, line_spec] + grad_specs,
            out_shape=[jax.ShapeDtypeStruct(local.shape, BF16), line, line] + grad_shapes,
            scratch_shapes=scratch + [pltpu.VMEM((2 * lines, columns), F32)],
            compiler_params=params(),
            cost_estimate=estimate,
            name="out_grad",
        )(places, ends, local, product, x, up, down)
    return pl.pallas_call(
        in_grad_kernel,
        grid=(frames // block,),
        in_specs=lead + [frame_spec] + tail + [ANYWHERE],
        out_specs=grad_specs,
        out_shape=grad_shapes,
        scratch_shapes=scratch
        + [pltpu.VMEM((3, p, 3 * c), F32), pltpu.VMEM((2 * lines, columns), F32)],
        compiler_params=params(),
        cost_estimate=estimate,
        name="in_grad",
    )(places, ends, local, product, decays, x, up, down, after)


def outputs_kernel(low_ref, up_ref, down_ref, w_ref, x_ref, skip_ref, after_ref, out_ref, token_ref, s_ref):
    token_ref[...] = jnp.zeros_like(token_ref)
    rows, frames, width, p = low_ref.shape
    s_ref[0] = shifted(flat(up_ref[...]), width)
    for r in range(rows):
        s_ref[r + 1] = shifted(flat(low_ref[r]), width)
    s_ref[rows + 1] = shifted(flat(down_ref[...]), width)
    lhs = jnp.concatenate([flat(s_ref[i : i + rows]) for i in range(3)], axis=1)
    mixed = dot(lhs, flat(w_ref[...])).reshape(rows, frames, width, -1)
    skip = skip_ref[...][0:1].reshape(1, 1, -1)
    for r in range(rows):
        out_ref[:, r] = (mixed[r] + skip * x_ref[:, r].astype(F32)).astype(BF16)


def outputs_conv(low, up, down, taps, x, skip, block, after):
    rows, frames, width, p = low.shape
    c = x.shape[-1]
    halo_spec = pl.BlockSpec((block, width, p), lambda b: (b, 0, 0))
    x_spec = pl.BlockSpec((block, rows, width, c), lambda b: (b, 0, 0, 0))
    return pl.pallas_call(
        outputs_kernel,
        grid=(frames // block,),
        in_specs=[
            pl.BlockSpec((rows, block, width, p), lambda b: (0, b, 0, 0)),
            halo_spec,
            halo_spec,
            pl.BlockSpec(taps.shape, lambda b: (0, 0, 0)),
            x_spec,
            pl.BlockSpec((1, c), lambda b: (0, 0)),
            ANYWHERE,
        ],
        out_specs=[x_spec, TOKEN_SPEC],
        out_shape=[jax.ShapeDtypeStruct(x.shape, BF16), TOKEN],
        scratch_shapes=[pltpu.VMEM((rows + 2, block * width, 3 * p), BF16)],
        compiler_params=params(),
        cost_estimate=cost(2 * frames * rows * width * 9 * c * p, 8 * 2**20),
        name="outputs_conv",
    )(low, up, down, taps, x, skip, after)


def edge_rows_kernel(x_ref, cot_ref, first_ref, last_ref, sems):
    rows = x_ref.shape[1]
    copies = []
    for k, ref in enumerate((x_ref, cot_ref)):
        copies.append(pltpu.make_async_copy(ref.at[:, 0], first_ref.at[k], sems.at[k, 0]))
        copies.append(pltpu.make_async_copy(ref.at[:, rows - 1], last_ref.at[k], sems.at[k, 1]))
    for copy in copies:
        copy.start()
    for copy in copies:
        copy.wait()


def edge_rows(x, cot):
    frames, rows, width, c = x.shape
    line = jax.ShapeDtypeStruct((2, frames, width, c), x.dtype)
    return pl.pallas_call(
        edge_rows_kernel,
        in_specs=[ANYWHERE, ANYWHERE],
        out_specs=[ANYWHERE, ANYWHERE],
        out_shape=[line, line],
        scratch_shapes=[pltpu.SemaphoreType.DMA((2, 2))],
        compiler_params=pltpu.CompilerParams(vmem_limit_bytes=2**20),
        cost_estimate=cost(0, 2**22),
        name="edge_rows",
    )(x, cot)


def row_halo(first, last):
    axes = ("y", "core")
    count = lax.axis_size("y") * lax.axis_size("core")
    up = lax.ppermute(last, axes, [(i, i + 1) for i in range(count - 1)])
    down = lax.ppermute(first, axes, [(i + 1, i) for i in range(count - 1)])
    return up, down


CORES = [(0, 1), (1, 0)]


def small_call(body, name, out_shapes, operands, after):
    def kernel(*refs):
        body(*refs[: len(operands)], *refs[len(operands) + 1 : -1])
        refs[-1][...] = jnp.zeros_like(refs[-1])

    return pl.pallas_call(
        kernel,
        in_specs=[pl.BlockSpec(memory_space=pltpu.VMEM)] * len(operands) + [ANYWHERE],
        out_specs=[pl.BlockSpec(memory_space=pltpu.VMEM)] * (len(out_shapes) + 1),
        out_shape=[jax.ShapeDtypeStruct(*shape) for shape in out_shapes] + [TOKEN],
        compiler_params=pltpu.CompilerParams(vmem_limit_bytes=8 * 2**20),
        cost_estimate=cost(0, 2**21),
        name=name,
    )(*operands, after)


def add_kernel(kept_ref, got_ref, out_ref):
    out_ref[...] = (kept_ref[...] + got_ref[...].astype(F32)).astype(out_ref.dtype)


def sum_kernel(parts_ref, out_ref):
    total = parts_ref[0].astype(F32)
    for k in range(1, parts_ref.shape[0]):
        total = total + parts_ref[k].astype(F32)
    out_ref[...] = total.astype(out_ref.dtype)


def total_kernel(scale, parts_ref, out_ref):
    total = parts_ref[0].astype(F32)
    for k in range(1, parts_ref.shape[0]):
        total = total + parts_ref[k].astype(F32)
    total = (total * scale).astype(out_ref.dtype)
    for k in range(out_ref.shape[0]):
        out_ref[k] = total


def repeat_kernel(part_ref, out_ref):
    for k in range(out_ref.shape[0]):
        out_ref[k] = part_ref[...]


def exchange(parts, axes):
    return lax.all_to_all(parts, axes, 0, 0)


def pieces(array, count):
    return array.reshape(count, array.shape[0] // count, array.shape[1])


def merge_kernel(scale, places_ref, own_ref, other_ref, out_ref):
    @pl.when(pl.program_id(0) == 0)
    def _():
        out_ref[...] = own_ref[...].astype(F32) * scale

    @pl.when(pl.program_id(0) == 1)
    def _():
        out_ref[...] = other_ref[...].astype(F32) * scale


def merged(own, other, places, scale):
    half, c = own.shape
    part_spec = pl.BlockSpec((half, c), lambda g, places: (0, 0))
    return pl.pallas_call(
        functools.partial(merge_kernel, scale),
        grid_spec=pltpu.PrefetchScalarGridSpec(
            num_scalar_prefetch=1,
            grid=(2,),
            in_specs=[part_spec, part_spec],
            out_specs=pl.BlockSpec((half, c), lambda g, places: (jnp.bitwise_xor(g, places[1]), 0)),
        ),
        out_shape=jax.ShapeDtypeStruct((2 * half, c), F32),
        compiler_params=params(12),
        cost_estimate=cost(0, 10 * half * c),
        name="merge",
    )(places, own, other)


def per_device(inputs, decays, in_kernel, out_kernel, skip, cotangent):
    clips, frames, rows, width, c = inputs.shape
    p = in_kernel.shape[3]
    block = 16
    devices = math.prod(lax.axis_size(name) for name in ("a", "x", "y", "core"))
    grad_scale = 1.0 / math.sqrt(clips * frames * rows * width * devices)
    x = inputs.reshape(frames, rows, width, c)
    cot = cotangent.reshape(frames, rows, width, c)
    places = jnp.stack([lax.axis_index(("a", "x")), lax.axis_index("core")]).astype(jnp.int32)

    up, down = row_halo(*edge_rows(x, cot))
    x_part, x_taps = interior_conv(x, in_kernel, False, block)
    cot_part, cot_taps = interior_conv(cot, out_kernel, True, block)
    states, running, ends = local_scan(x_part, up, down, 0, x_taps, decays, block)
    adjoint, trailing, messages = local_scan(
        cot_part, up, down, 1, cot_taps, decays, block, places, ends
    )
    carried = exchange(messages, ("a", "x"))

    low, low_first, low_last, sent, out_kept, token = kernel_grads(
        places, carried, states, running, cot, up, down, 1, None, block
    )
    out_got = lax.ppermute(sent, "core", CORES)
    low_up, low_down = row_halo(low_first, low_last)
    sent, in_kept, token = kernel_grads(
        places, carried, adjoint, trailing, x, up, down, 0, decays, block, token
    )
    in_got = lax.ppermute(sent, "core", CORES)
    half, q = in_kept.shape
    out_half, token = small_call(add_kernel, "out_add", [(out_kept.shape, F32)], [out_kept, out_got], token)
    out_half = lax.psum(out_half, ("a", "x", "y"))
    in_half, token = small_call(add_kernel, "in_add", [((half, q), BF16)], [in_kept, in_got], token)
    four = lax.axis_size("x") * lax.axis_size("y")
    deep = lax.axis_size("a")
    parts = exchange(pieces(in_half, four), ("x", "y"))
    outputs, token = outputs_conv(
        low, low_up, low_down, out_kernel.reshape(3, 3 * p, c), x, skip.reshape(1, c), block, token
    )
    part, token = small_call(sum_kernel, "in_sum", [((half // four, q), BF16)], [parts], token)
    parts = exchange(pieces(part, deep), ("a",))
    share = parts.shape[1]
    parts, token = small_call(
        functools.partial(total_kernel, grad_scale), "in_total", [(parts.shape, BF16)], [parts], token
    )
    part = exchange(parts, ("a",)).reshape(deep * share, q)
    parts, token = small_call(
        repeat_kernel, "in_repeat", [((four,) + part.shape, BF16)], [part], token
    )
    in_half = exchange(parts, ("x", "y")).reshape(half, q)
    in_grad = merged(in_half, lax.ppermute(in_half, "core", CORES), places, 1.0)
    out_half = out_half.astype(BF16)
    out_grad = merged(out_half, lax.ppermute(out_half, "core", CORES), places, grad_scale)
    return (
        outputs.reshape(inputs.shape),
        in_grad.reshape(in_kernel.shape),
        out_grad.reshape(out_kernel.shape),
    )


def solution(mesh):
    frames = mesh.shape["tm"]
    rows = mesh.shape["row"]
    fine = jax.sharding.Mesh(
        mesh.devices.reshape(frames // 2, 2, rows // 2, 2), ("a", "x", "y", "core")
    )
    cells = P(None, ("a", "x"), ("y", "core"), None, None)
    return jax.shard_map(
        per_device,
        mesh=fine,
        in_specs=(cells, P(("a", "x"), None), P(), P(), P(), cells),
        out_specs=(cells, P(), P()),
        check_vma=False,
    )
```

```python
import functools
import math

import jax
import jax.numpy as jnp
from jax import lax
from jax.experimental import pallas as pl
from jax.experimental.pallas import tpu as pltpu
from jax.sharding import PartitionSpec as P

BF16 = jnp.bfloat16
F32 = jnp.float32


SCALARS = pl.BlockSpec(memory_space=pltpu.SMEM)
ANYWHERE = pl.BlockSpec(memory_space=pl.ANY)
TOKEN = jax.ShapeDtypeStruct((8, 128), F32)
TOKEN_SPEC = pl.BlockSpec((8, 128), lambda *b: (0, 0))


def params(mib=20):
    return pltpu.CompilerParams(
        dimension_semantics=("arbitrary",), vmem_limit_bytes=mib * 1024 * 1024
    )


def cost(flops, nbytes):
    return pl.CostEstimate(flops=int(flops), bytes_accessed=int(nbytes), transcendentals=0)


def shifted(cells, width):
    count = cells.shape[0]
    wide = cells.astype(F32)
    column = lax.broadcasted_iota(jnp.int32, (count, 1), 0) % width
    left = jnp.where(column == 0, 0.0, pltpu.roll(wide, 1, 0))
    right = jnp.where(column == width - 1, 0.0, pltpu.roll(wide, count - 1, 0))
    return jnp.concatenate([left.astype(BF16), cells, right.astype(BF16)], axis=1)


def flat(block):
    return block.reshape(-1, block.shape[-1])


def dot(a, b):
    return jnp.dot(a, b, preferred_element_type=F32)


def interior_body(x_ref, w_ref, out_ref, s_ref):
    frames, rows, width, _ = x_ref.shape
    lines = frames * width
    for r in range(rows):
        s_ref[r] = shifted(flat(x_ref[:, r]), width)

    def conv(first, count, taps):
        lhs = jnp.concatenate(
            [flat(s_ref[first + i - 1 : first + i - 1 + count]) for i in taps], axis=1
        )
        rhs = w_ref[taps[0] : taps[-1] + 1].reshape(len(taps) * w_ref.shape[1], w_ref.shape[2])
        out_ref[first : first + count] = dot(lhs, rhs).reshape(count, frames, width, -1)

    conv(1, rows - 2, (0, 1, 2))
    conv(0, 1, (1, 2))
    conv(rows - 1, 1, (0, 1))


def interior_plain_kernel(x_ref, w_ref, out_ref, s_ref):
    interior_body(x_ref, w_ref, out_ref, s_ref)


def interior_flipped_kernel(x_ref, w_ref, out_ref, wt_ref, s_ref):
    @pl.when(pl.program_id(0) == 0)
    def _():
        for i in range(3):
            for j in range(3):
                c = w_ref.shape[3]
                wt_ref[i, j * c : (j + 1) * c, :] = w_ref[2 - i, 2 - j].T

    interior_body(x_ref, wt_ref, out_ref, s_ref)


def interior_conv(x, w, flipped, block):
    frames, rows, width, c = x.shape
    p = w.shape[2] if flipped else w.shape[3]
    part_shape = jax.ShapeDtypeStruct((rows, frames, width, p), F32)
    part_spec = pl.BlockSpec((rows, block, width, p), lambda b: (0, b, 0, 0))
    x_spec = pl.BlockSpec((block, rows, width, c), lambda b: (b, 0, 0, 0))
    scratch = [pltpu.VMEM((rows, block * width, 3 * c), BF16)]
    estimate = cost(2 * frames * rows * width * 9 * c * p, 8 * 2**20)
    taps_spec = pl.BlockSpec((3, 3 * c, p), lambda b: (0, 0, 0))
    if flipped:
        return pl.pallas_call(
            interior_flipped_kernel,
            grid=(frames // block,),
            in_specs=[
                x_spec,
                pl.BlockSpec(w.shape, lambda b: (0, 0, 0, 0)),
            ],
            out_specs=[part_spec, taps_spec],
            out_shape=[part_shape, jax.ShapeDtypeStruct((3, 3 * c, p), BF16)],
            scratch_shapes=scratch,
            compiler_params=params(),
            cost_estimate=estimate,
            name="interior_cot",
        )(x, w)
    taps = w.reshape(3, 3 * c, p)
    part = pl.pallas_call(
        interior_plain_kernel,
        grid=(frames // block,),
        in_specs=[x_spec, taps_spec],
        out_specs=part_spec,
        out_shape=part_shape,
        scratch_shapes=scratch,
        compiler_params=params(),
        cost_estimate=estimate,
        name="interior_in",
    )(x, taps)
    return part, taps


def scan_kernel(backward, part_ref, up_ref, down_ref, w_ref, decay_ref, after_ref, local_ref, product_ref, end_ref, carry_ref, run_ref):
    rows, frames, width, p = part_ref.shape
    lines = rows * width

    @pl.when(pl.program_id(0) == 0)
    def _():
        carry_ref[...] = jnp.zeros_like(carry_ref)
        run_ref[...] = jnp.ones_like(run_ref)

    top = dot(shifted(flat(up_ref[...]), width), w_ref[0]).reshape(frames, width, p)
    low = dot(shifted(flat(down_ref[...]), width), w_ref[2]).reshape(frames, width, p)
    decay = decay_ref[...]
    scale = jnp.sqrt((1.0 - decay) * (1.0 + decay))
    state = [carry_ref[r * width : (r + 1) * width] for r in range(rows)]
    run = run_ref[0:1]
    for step in range(frames):
        t = frames - 1 - step if backward else step
        factor = decay[t : t + 1]
        gain = scale[t : t + 1]
        if backward:
            product_ref[t : t + 1] = run
        run = run * factor
        if not backward:
            product_ref[t : t + 1] = run
        for r in range(rows):
            term = part_ref[r, t]
            if r == 0:
                term = term + top[t]
            if r == rows - 1:
                term = term + low[t]
            if backward:
                full = term + state[r]
                local_ref[r, t] = full
                state[r] = factor * full
            else:
                state[r] = factor * state[r] + gain * term
                local_ref[r, t] = state[r]
    for r in range(rows):
        carry_ref[r * width : (r + 1) * width] = state[r]
    run_ref[...] = jnp.broadcast_to(run, run_ref.shape)

    @pl.when(pl.program_id(0) == pl.num_programs(0) - 1)
    def _():
        high = run.astype(BF16).astype(F32)
        products = [jnp.broadcast_to(high, (8, p)), jnp.broadcast_to(run - high, (8, p))]
        message = jnp.concatenate(state + products, axis=0).astype(BF16)
        for k in range(end_ref.shape[0]):
            end_ref[k] = message


def local_scan(part, up, down, half, taps, decays, block, backward, after):
    rows, frames, width, p = part.shape
    c = up.shape[-1]
    blocks = frames // block
    at = (lambda b: blocks - 1 - b) if backward else (lambda b: b)
    halo_spec = pl.BlockSpec((None, block, width, c), lambda b: (half, at(b), 0, 0))
    part_spec = pl.BlockSpec((rows, block, width, p), lambda b: (0, at(b), 0, 0))
    frame_spec = pl.BlockSpec((block, p), lambda b: (at(b), 0))
    lines = rows * width
    count = lax.axis_size("a") * lax.axis_size("x")
    return pl.pallas_call(
        functools.partial(scan_kernel, backward),
        grid=(blocks,),
        in_specs=[
            part_spec,
            halo_spec,
            halo_spec,
            pl.BlockSpec(taps.shape, lambda b: (0, 0, 0)),
            frame_spec,
            ANYWHERE,
        ],
        out_specs=[
            part_spec,
            frame_spec,
            pl.BlockSpec((count, lines + 16, p), lambda b: (0, 0, 0)),
        ],
        out_shape=[
            jax.ShapeDtypeStruct(part.shape, F32),
            jax.ShapeDtypeStruct((frames, p), F32),
            jax.ShapeDtypeStruct((count, lines + 16, p), BF16),
        ],
        scratch_shapes=[pltpu.VMEM((lines, p), F32), pltpu.VMEM((8, p), F32)],
        compiler_params=params(),
        cost_estimate=cost(4 * frames * width * 3 * c * p, 12 * 2**20),
        name="scan_back" if backward else "scan_fwd",
    )(part, up, down, taps, decays, after)


def combine(place_ref, ends_ref, total_ref, backward):
    place = place_ref[0]
    count = ends_ref.shape[0]
    lines = total_ref.shape[0]
    total = jnp.zeros(total_ref.shape, F32)
    order = range(count - 1, -1, -1) if backward else range(count)
    for k in order:
        block = ends_ref[k].astype(F32)
        product = block[lines : lines + 1] + block[lines + 8 : lines + 9]
        passed = product * total + block[0:lines]
        total = jnp.where(k > place if backward else k < place, passed, total)
    total_ref[...] = total


def split_halves(place_ref, sum_ref, sent_ref, kept_ref):
    half = kept_ref.shape[0]
    side = place_ref[1]
    sent_ref[...] = sum_ref[pl.ds(pl.multiple_of((1 - side) * half, 8), half)].astype(BF16)
    kept_ref[...] = sum_ref[pl.ds(pl.multiple_of(side * half, 8), half)]


def fill_rim(s_ref, up_ref, x_ref, down_ref):
    _, rows, width, _ = x_ref.shape
    s_ref[0] = shifted(flat(up_ref[...]), width)
    for r in range(rows):
        s_ref[r + 1] = shifted(flat(x_ref[:, r]), width)
    s_ref[rows + 1] = shifted(flat(down_ref[...]), width)


def out_grad_kernel(place_ref, ends_ref, local_ref, product_ref, cot_ref, up_ref, down_ref, after_ref, low_ref, first_ref, last_ref, sent_ref, kept_ref, token_ref, s_ref, total_ref, sum_ref):
    rows, frames, width, p = local_ref.shape
    c = cot_ref.shape[-1]

    @pl.when(pl.program_id(0) == 0)
    def _():
        combine(place_ref, ends_ref, total_ref, False)
        sum_ref[...] = jnp.zeros_like(sum_ref)
        token_ref[...] = jnp.zeros_like(token_ref)

    fill_rim(s_ref, up_ref, cot_ref, down_ref)
    product = product_ref[...]
    turned = []
    for r in range(rows):
        state = local_ref[r] + product[:, None, :] * total_ref[r * width : (r + 1) * width][None]
        low = state.astype(BF16)
        low_ref[r] = low
        if r == 0:
            first_ref[...] = low
        if r == rows - 1:
            last_ref[...] = low
        turned.append(flat(low).T)
    turned = jnp.concatenate(turned, axis=1)
    for i in range(3):
        gain = dot(turned, flat(s_ref[2 - i : 2 - i + rows]))
        for j in range(3):
            tap = 3 * i + j
            sum_ref[tap * p : (tap + 1) * p] += gain[:, (2 - j) * c : (3 - j) * c]

    @pl.when(pl.program_id(0) == pl.num_programs(0) - 1)
    def _():
        split_halves(place_ref, sum_ref, sent_ref, kept_ref)


def in_grad_kernel(place_ref, ends_ref, local_ref, product_ref, decay_ref, x_ref, up_ref, down_ref, after_ref, sent_ref, kept_ref, token_ref, s_ref, total_ref, sum_ref, flat_ref):
    rows, frames, width, p = local_ref.shape
    c = x_ref.shape[-1]

    @pl.when(pl.program_id(0) == 0)
    def _():
        combine(place_ref, ends_ref, total_ref, True)
        sum_ref[...] = jnp.zeros_like(sum_ref)
        token_ref[...] = jnp.zeros_like(token_ref)

    fill_rim(s_ref, up_ref, x_ref, down_ref)
    product = product_ref[...]
    decay = decay_ref[...]
    scale = jnp.sqrt((1.0 - decay) * (1.0 + decay))[:, None, :]
    turned = []
    for r in range(rows):
        adjoint = local_ref[r] + product[:, None, :] * total_ref[r * width : (r + 1) * width][None]
        turned.append(flat((scale * adjoint).astype(BF16)).T)
    turned = jnp.concatenate(turned, axis=1)
    for i in range(3):
        sum_ref[i] += dot(turned, flat(s_ref[i : i + rows]))

    @pl.when(pl.program_id(0) == pl.num_programs(0) - 1)
    def _():
        for i in range(3):
            for j in range(3):
                tap = 3 * i + j
                flat_ref[tap * c : (tap + 1) * c] = sum_ref[i, :, j * c : (j + 1) * c].T
        split_halves(place_ref, flat_ref, sent_ref, kept_ref)


def kernel_grads(places, ends, local, product, x, up, down, half, decays, block, after):
    rows, frames, width, p = local.shape
    c = x.shape[-1]
    halo_spec = pl.BlockSpec((None, block, width, c), lambda b: (half, b, 0, 0))
    local_spec = pl.BlockSpec((rows, block, width, p), lambda b: (0, b, 0, 0))
    frame_spec = pl.BlockSpec((block, p), lambda b: (b, 0))
    x_spec = pl.BlockSpec((block, rows, width, c), lambda b: (b, 0, 0, 0))
    lead = [SCALARS, pl.BlockSpec(ends.shape, lambda b: (0, 0, 0)), local_spec, frame_spec]
    tail = [x_spec, halo_spec, halo_spec]
    scratch = [
        pltpu.VMEM((rows + 2, block * width, 3 * c), BF16),
        pltpu.VMEM((rows * width, p), F32),
    ]
    estimate = cost(2 * frames * rows * width * 9 * c * p, 10 * 2**20)
    forward = decays is None
    lines, columns = (9 * p // 2, c) if forward else (9 * c // 2, p)
    grad_specs = [pl.BlockSpec((lines, columns), lambda b: (0, 0))] * 2 + [TOKEN_SPEC]
    grad_shapes = [
        jax.ShapeDtypeStruct((lines, columns), BF16),
        jax.ShapeDtypeStruct((lines, columns), F32),
        TOKEN,
    ]
    if forward:
        line_spec = pl.BlockSpec((block, width, p), lambda b: (b, 0, 0))
        line = jax.ShapeDtypeStruct((frames, width, p), BF16)
        return pl.pallas_call(
            out_grad_kernel,
            grid=(frames // block,),
            in_specs=lead + tail + [ANYWHERE],
            out_specs=[local_spec, line_spec, line_spec] + grad_specs,
            out_shape=[jax.ShapeDtypeStruct(local.shape, BF16), line, line] + grad_shapes,
            scratch_shapes=scratch + [pltpu.VMEM((2 * lines, columns), F32)],
            compiler_params=params(),
            cost_estimate=estimate,
            name="out_grad",
        )(places, ends, local, product, x, up, down, after)
    return pl.pallas_call(
        in_grad_kernel,
        grid=(frames // block,),
        in_specs=lead + [frame_spec] + tail + [ANYWHERE],
        out_specs=grad_specs,
        out_shape=grad_shapes,
        scratch_shapes=scratch
        + [pltpu.VMEM((3, p, 3 * c), F32), pltpu.VMEM((2 * lines, columns), F32)],
        compiler_params=params(),
        cost_estimate=estimate,
        name="in_grad",
    )(places, ends, local, product, decays, x, up, down, after)


def outputs_kernel(low_ref, up_ref, down_ref, w_ref, x_ref, skip_ref, after_ref, out_ref, token_ref, s_ref):
    token_ref[...] = jnp.zeros_like(token_ref)
    rows, frames, width, p = low_ref.shape
    s_ref[0] = shifted(flat(up_ref[...]), width)
    for r in range(rows):
        s_ref[r + 1] = shifted(flat(low_ref[r]), width)
    s_ref[rows + 1] = shifted(flat(down_ref[...]), width)
    lhs = jnp.concatenate([flat(s_ref[i : i + rows]) for i in range(3)], axis=1)
    mixed = dot(lhs, flat(w_ref[...])).reshape(rows, frames, width, -1)
    skip = skip_ref[...][0:1].reshape(1, 1, -1)
    for r in range(rows):
        out_ref[:, r] = (mixed[r] + skip * x_ref[:, r].astype(F32)).astype(BF16)


def outputs_conv(low, up, down, taps, x, skip, block, after):
    rows, frames, width, p = low.shape
    c = x.shape[-1]
    halo_spec = pl.BlockSpec((block, width, p), lambda b: (b, 0, 0))
    x_spec = pl.BlockSpec((block, rows, width, c), lambda b: (b, 0, 0, 0))
    return pl.pallas_call(
        outputs_kernel,
        grid=(frames // block,),
        in_specs=[
            pl.BlockSpec((rows, block, width, p), lambda b: (0, b, 0, 0)),
            halo_spec,
            halo_spec,
            pl.BlockSpec(taps.shape, lambda b: (0, 0, 0)),
            x_spec,
            pl.BlockSpec((1, c), lambda b: (0, 0)),
            ANYWHERE,
        ],
        out_specs=[x_spec, TOKEN_SPEC],
        out_shape=[jax.ShapeDtypeStruct(x.shape, BF16), TOKEN],
        scratch_shapes=[pltpu.VMEM((rows + 2, block * width, 3 * p), BF16)],
        compiler_params=params(),
        cost_estimate=cost(2 * frames * rows * width * 9 * c * p, 8 * 2**20),
        name="outputs_conv",
    )(low, up, down, taps, x, skip, after)


def edge_rows_kernel(x_ref, cot_ref, first_ref, last_ref, sems):
    rows = x_ref.shape[1]
    copies = []
    for k, ref in enumerate((x_ref, cot_ref)):
        copies.append(pltpu.make_async_copy(ref.at[:, 0], first_ref.at[k], sems.at[k, 0]))
        copies.append(pltpu.make_async_copy(ref.at[:, rows - 1], last_ref.at[k], sems.at[k, 1]))
    for copy in copies:
        copy.start()
    for copy in copies:
        copy.wait()


def edge_rows(x, cot):
    frames, rows, width, c = x.shape
    line = jax.ShapeDtypeStruct((2, frames, width, c), x.dtype)
    return pl.pallas_call(
        edge_rows_kernel,
        in_specs=[pl.BlockSpec(memory_space=pltpu.HBM)] * 2,
        out_specs=[ANYWHERE, ANYWHERE],
        out_shape=[line, line],
        scratch_shapes=[pltpu.SemaphoreType.DMA((2, 2))],
        compiler_params=pltpu.CompilerParams(vmem_limit_bytes=2**20),
        cost_estimate=cost(0, 2**22),
        name="edge_rows",
    )(x, cot)


def row_halo(first, last):
    axes = ("y", "core")
    count = lax.axis_size("y") * lax.axis_size("core")
    up = lax.ppermute(last, axes, [(i, i + 1) for i in range(count - 1)])
    down = lax.ppermute(first, axes, [(i + 1, i) for i in range(count - 1)])
    return up, down


CORES = [(0, 1), (1, 0)]


def small_call(body, name, out_shapes, operands, after, places=None):
    extra = [] if places is None else [places]

    def kernel(*refs):
        body(*refs[1 : len(extra) + len(operands) + 1], *refs[len(extra) + len(operands) + 1 : -1])
        refs[-1][...] = jnp.zeros_like(refs[-1])

    whole = pl.BlockSpec(memory_space=pltpu.VMEM)
    return pl.pallas_call(
        kernel,
        in_specs=[ANYWHERE] + [SCALARS] * len(extra) + [whole] * len(operands),
        out_specs=[whole] * (len(out_shapes) + 1),
        out_shape=[jax.ShapeDtypeStruct(*shape) for shape in out_shapes] + [TOKEN],
        compiler_params=pltpu.CompilerParams(vmem_limit_bytes=8 * 2**20),
        cost_estimate=cost(0, 2**21),
        name=name,
    )(after, *extra, *operands)


def add_kernel(kept_ref, got_ref, sent_ref, sum_ref):
    total = kept_ref[...] + got_ref[...].astype(F32)
    sum_ref[...] = total
    sent_ref[...] = total.astype(BF16)


def share_kernel(places_ref, kept_ref, parts_ref, out_ref):
    own = places_ref[2]
    total = kept_ref[own]
    for k in range(parts_ref.shape[0]):
        total = total + jnp.where(k == own, 0.0, parts_ref[k].astype(F32))
    total = total.astype(BF16)
    for k in range(out_ref.shape[0]):
        out_ref[k] = total


def total_kernel(scale, parts_ref, out_ref):
    total = parts_ref[0].astype(F32)
    for k in range(1, parts_ref.shape[0]):
        total = total + parts_ref[k].astype(F32)
    total = (total * scale).astype(BF16)
    for k in range(out_ref.shape[0]):
        out_ref[k] = total


def exchange(parts, axes):
    return lax.all_to_all(parts, axes, 0, 0)


def pieces(array, count):
    return array.reshape(count, array.shape[0] // count, array.shape[1])


def merge_kernel(places_ref, own_ref, other_ref, out_ref):
    @pl.when(pl.program_id(0) == 0)
    def _():
        out_ref[...] = own_ref[...].astype(F32)

    @pl.when(pl.program_id(0) == 1)
    def _():
        out_ref[...] = other_ref[...].astype(F32)


def merged(own, other, places):
    half, c = own.shape
    part_spec = pl.BlockSpec((half, c), lambda g, places: (0, 0))
    return pl.pallas_call(
        merge_kernel,
        grid_spec=pltpu.PrefetchScalarGridSpec(
            num_scalar_prefetch=1,
            grid=(2,),
            in_specs=[part_spec, part_spec],
            out_specs=pl.BlockSpec((half, c), lambda g, places: (jnp.bitwise_xor(g, places[1]), 0)),
        ),
        out_shape=jax.ShapeDtypeStruct((2 * half, c), F32),
        compiler_params=params(12),
        cost_estimate=cost(0, 10 * half * c),
        name="merge",
    )(places, own, other)


def per_device(inputs, decays, in_kernel, out_kernel, skip, cotangent):
    clips, frames, rows, width, c = inputs.shape
    p = in_kernel.shape[3]
    block = 16
    devices = math.prod(lax.axis_size(name) for name in ("a", "x", "y", "core"))
    grad_scale = 1.0 / math.sqrt(clips * frames * rows * width * devices)
    x = inputs.reshape(frames, rows, width, c)
    cot = cotangent.reshape(frames, rows, width, c)
    places = jnp.stack(
        [lax.axis_index(("a", "x")), lax.axis_index("core"), lax.axis_index(("x", "y"))]
    ).astype(jnp.int32)
    four = lax.axis_size("x") * lax.axis_size("y")
    deep = lax.axis_size("a")

    up, down = row_halo(*edge_rows(x, cot))
    x_part, x_taps = interior_conv(x, in_kernel, False, block)
    cot_part, cot_taps = interior_conv(cot, out_kernel, True, block)
    states, running, ends = local_scan(x_part, up, down, 0, x_taps, decays, block, False, decays)
    ends_all = exchange(ends, ("a", "x"))
    adjoint, trailing, starts = local_scan(
        cot_part, up, down, 1, cot_taps, decays, block, True, running
    )
    starts_all = exchange(starts, ("a", "x"))

    low, low_first, low_last, sent, kept, token = kernel_grads(
        places, ends_all, states, running, cot, up, down, 1, None, block, trailing
    )
    got = lax.ppermute(sent, "core", CORES)
    low_up, low_down = row_halo(low_first, low_last)

    def add(name, kept, got, token):
        return small_call(
            add_kernel, name, [(kept.shape, BF16), (kept.shape, F32)], [kept, got], token
        )

    def share(name, kept, parts, token):
        shape = (deep,) + parts.shape[1:]
        kept = pieces(kept, four)
        return small_call(share_kernel, name, [(shape, BF16)], [kept, parts], token, places)

    def total(name, parts, token):
        body = functools.partial(total_kernel, grad_scale)
        return small_call(body, name, [((four,) + parts.shape[1:], BF16)], [parts], token)

    sent, out_kept, out_token = add("out_add", kept, got, token)
    out_parts = exchange(pieces(sent, four), ("x", "y"))
    sent, kept, token = kernel_grads(
        places, starts_all, adjoint, trailing, x, up, down, 0, decays, block, out_token
    )
    got = lax.ppermute(sent, "core", CORES)
    out_parts, token = share("out_share", out_kept, out_parts, token)
    out_parts = exchange(out_parts, ("a",))
    sent, in_kept, token = add("in_add", kept, got, token)
    in_parts = exchange(pieces(sent, four), ("x", "y"))
    outputs, token = outputs_conv(
        low, low_up, low_down, out_kernel.reshape(3, 3 * p, c), x, skip.reshape(1, c), block, token
    )
    in_parts, token = share("in_share", in_kept, in_parts, token)
    in_parts = exchange(in_parts, ("a",))
    out_parts, token = total("out_total", out_parts, token)
    out_half = flat(exchange(out_parts, ("x", "y")))
    in_parts, token = total("in_total", in_parts, token)
    in_half = flat(exchange(in_parts, ("x", "y")))
    out_other = lax.ppermute(out_half, "core", CORES)
    in_other = lax.ppermute(in_half, "core", CORES)
    out_grad = merged(out_half, out_other, places)
    in_grad = merged(in_half, in_other, places)
    return (
        outputs.reshape(inputs.shape),
        in_grad.reshape(in_kernel.shape),
        out_grad.reshape(out_kernel.shape),
    )


def solution(mesh):
    frames = mesh.shape["tm"]
    rows = mesh.shape["row"]
    fine = jax.sharding.Mesh(
        mesh.devices.reshape(frames // 2, 2, rows // 2, 2), ("a", "x", "y", "core")
    )
    cells = P(None, ("a", "x"), ("y", "core"), None, None)
    return jax.shard_map(
        per_device,
        mesh=fine,
        in_specs=(cells, P(("a", "x"), None), P(), P(), P(), cells),
        out_specs=(cells, P(), P()),
        check_vma=False,
    )
```

```python
import functools
import math

import jax
import jax.numpy as jnp
from jax import lax
from jax.experimental import pallas as pl
from jax.experimental.pallas import tpu as pltpu
from jax.sharding import PartitionSpec as P

BF16 = jnp.bfloat16
F32 = jnp.float32


SCALARS = pl.BlockSpec(memory_space=pltpu.SMEM)
ANYWHERE = pl.BlockSpec(memory_space=pl.ANY)
TOKEN = jax.ShapeDtypeStruct((8, 128), F32)
TOKEN_SPEC = pl.BlockSpec((8, 128), lambda *b: (0, 0))


def params(mib=20):
    return pltpu.CompilerParams(
        dimension_semantics=("arbitrary",), vmem_limit_bytes=mib * 1024 * 1024
    )


def cost(flops, nbytes):
    return pl.CostEstimate(flops=int(flops), bytes_accessed=int(nbytes), transcendentals=0)


def shifted(cells, width):
    count = cells.shape[0]
    wide = cells.astype(F32)
    column = lax.broadcasted_iota(jnp.int32, (count, 1), 0) % width
    left = jnp.where(column == 0, 0.0, pltpu.roll(wide, 1, 0))
    right = jnp.where(column == width - 1, 0.0, pltpu.roll(wide, count - 1, 0))
    return jnp.concatenate([left.astype(BF16), cells, right.astype(BF16)], axis=1)


def flat(block):
    return block.reshape(-1, block.shape[-1])


def dot(a, b):
    return jnp.dot(a, b, preferred_element_type=F32)


def interior_body(x_ref, w_ref, out_ref, s_ref):
    frames, rows, width, _ = x_ref.shape
    lines = frames * width
    for r in range(rows):
        s_ref[r] = shifted(flat(x_ref[:, r]), width)

    def conv(first, count, taps):
        lhs = jnp.concatenate(
            [flat(s_ref[first + i - 1 : first + i - 1 + count]) for i in taps], axis=1
        )
        rhs = w_ref[taps[0] : taps[-1] + 1].reshape(len(taps) * w_ref.shape[1], w_ref.shape[2])
        out_ref[first : first + count] = dot(lhs, rhs).reshape(count, frames, width, -1)

    conv(1, rows - 2, (0, 1, 2))
    conv(0, 1, (1, 2))
    conv(rows - 1, 1, (0, 1))


def interior_plain_kernel(x_ref, w_ref, out_ref, s_ref):
    interior_body(x_ref, w_ref, out_ref, s_ref)


def interior_flipped_kernel(x_ref, w_ref, out_ref, wt_ref, s_ref):
    @pl.when(pl.program_id(0) == 0)
    def _():
        for i in range(3):
            for j in range(3):
                c = w_ref.shape[3]
                wt_ref[i, j * c : (j + 1) * c, :] = w_ref[2 - i, 2 - j].T

    interior_body(x_ref, wt_ref, out_ref, s_ref)


def interior_conv(x, w, flipped, block):
    frames, rows, width, c = x.shape
    p = w.shape[2] if flipped else w.shape[3]
    part_shape = jax.ShapeDtypeStruct((rows, frames, width, p), F32)
    part_spec = pl.BlockSpec((rows, block, width, p), lambda b: (0, b, 0, 0))
    x_spec = pl.BlockSpec((block, rows, width, c), lambda b: (b, 0, 0, 0))
    scratch = [pltpu.VMEM((rows, block * width, 3 * c), BF16)]
    estimate = cost(2 * frames * rows * width * 9 * c * p, 8 * 2**20)
    taps_spec = pl.BlockSpec((3, 3 * c, p), lambda b: (0, 0, 0))
    if flipped:
        return pl.pallas_call(
            interior_flipped_kernel,
            grid=(frames // block,),
            in_specs=[
                x_spec,
                pl.BlockSpec(w.shape, lambda b: (0, 0, 0, 0)),
            ],
            out_specs=[part_spec, taps_spec],
            out_shape=[part_shape, jax.ShapeDtypeStruct((3, 3 * c, p), BF16)],
            scratch_shapes=scratch,
            compiler_params=params(),
            cost_estimate=estimate,
            name="interior_cot",
        )(x, w)
    taps = w.reshape(3, 3 * c, p)
    part = pl.pallas_call(
        interior_plain_kernel,
        grid=(frames // block,),
        in_specs=[x_spec, taps_spec],
        out_specs=part_spec,
        out_shape=part_shape,
        scratch_shapes=scratch,
        compiler_params=params(),
        cost_estimate=estimate,
        name="interior_in",
    )(x, taps)
    return part, taps


def scan_kernel(backward, part_ref, up_ref, down_ref, w_ref, decay_ref, before_ref, local_ref, product_ref, end_ref, carry_ref, run_ref):
    rows, frames, width, p = part_ref.shape
    lines = rows * width

    @pl.when(pl.program_id(0) == 0)
    def _():
        carry_ref[...] = jnp.zeros_like(carry_ref)
        run_ref[...] = jnp.ones_like(run_ref)

    top = dot(shifted(flat(up_ref[...]), width), w_ref[0]).reshape(frames, width, p)
    low = dot(shifted(flat(down_ref[...]), width), w_ref[2]).reshape(frames, width, p)
    decay = decay_ref[...]
    scale = jnp.sqrt((1.0 - decay) * (1.0 + decay))
    state = [carry_ref[r * width : (r + 1) * width] for r in range(rows)]
    run = run_ref[0:1]
    for step in range(frames):
        t = frames - 1 - step if backward else step
        factor = decay[t : t + 1]
        gain = scale[t : t + 1]
        if backward:
            product_ref[t : t + 1] = run
        run = run * factor
        if not backward:
            product_ref[t : t + 1] = run
        for r in range(rows):
            term = part_ref[r, t]
            if r == 0:
                term = term + top[t]
            if r == rows - 1:
                term = term + low[t]
            if backward:
                full = term + state[r]
                local_ref[r, t] = full
                state[r] = factor * full
            else:
                state[r] = factor * state[r] + gain * term
                local_ref[r, t] = state[r]
    for r in range(rows):
        carry_ref[r * width : (r + 1) * width] = state[r]
    run_ref[...] = jnp.broadcast_to(run, run_ref.shape)

    @pl.when(pl.program_id(0) == pl.num_programs(0) - 1)
    def _():
        if backward:
            message = [before_ref[...]] + state + [jnp.broadcast_to(run, (8, p))]
        else:
            message = state
        end_ref[...] = jnp.concatenate(message, axis=0)


def local_scan(part, up, down, half, taps, decays, block, backward, before):
    rows, frames, width, p = part.shape
    c = up.shape[-1]
    blocks = frames // block
    at = (lambda b: blocks - 1 - b) if backward else (lambda b: b)
    halo_spec = pl.BlockSpec((None, block, width, c), lambda b: (half, at(b), 0, 0))
    part_spec = pl.BlockSpec((rows, block, width, p), lambda b: (0, at(b), 0, 0))
    frame_spec = pl.BlockSpec((block, p), lambda b: (at(b), 0))
    lines = rows * width
    message = 2 * lines + 8 if backward else lines
    return pl.pallas_call(
        functools.partial(scan_kernel, backward),
        grid=(blocks,),
        in_specs=[
            part_spec,
            halo_spec,
            halo_spec,
            pl.BlockSpec(taps.shape, lambda b: (0, 0, 0)),
            frame_spec,
            pl.BlockSpec(before.shape, lambda b: (0, 0)),
        ],
        out_specs=[part_spec, frame_spec, pl.BlockSpec((message, p), lambda b: (0, 0))],
        out_shape=[
            jax.ShapeDtypeStruct(part.shape, F32),
            jax.ShapeDtypeStruct((frames, p), F32),
            jax.ShapeDtypeStruct((message, p), F32),
        ],
        scratch_shapes=[pltpu.VMEM((lines, p), F32), pltpu.VMEM((8, p), F32)],
        compiler_params=params(),
        cost_estimate=cost(4 * frames * width * 3 * c * p, 12 * 2**20),
        name="scan_back" if backward else "scan_fwd",
    )(part, up, down, taps, decays, before)


def pair_kernel(places_ref, own_ref, got_ref, out_ref):
    deep, height, _ = out_ref.shape
    lines = height - 8
    first = places_ref[1] == 0
    own_end, got_end = own_ref[0:lines], got_ref[0:lines]
    own_start, got_start = own_ref[lines : 2 * lines], got_ref[lines : 2 * lines]
    own_product, got_product = own_ref[2 * lines :], got_ref[2 * lines :]
    end = jnp.where(
        first, got_product[0:1] * own_end + got_end, own_product[0:1] * got_end + own_end
    )
    start = jnp.where(
        first, own_product[0:1] * got_start + own_start, got_product[0:1] * own_start + got_start
    )
    product = own_product * got_product
    for k in range(deep):
        out_ref[k, 0:lines] = jnp.where(k > places_ref[0], end, start)
        out_ref[k, lines:] = product


def combine(places_ref, ends_ref, pair_ref, total_ref, backward):
    place = places_ref[0]
    count = ends_ref.shape[0]
    lines = total_ref.shape[0]
    total = jnp.zeros(total_ref.shape, F32)
    order = range(count - 1, -1, -1) if backward else range(count)
    for k in order:
        passed = ends_ref[k, lines : lines + 1] * total + ends_ref[k, 0:lines]
        total = jnp.where(k > place if backward else k < place, passed, total)
    near = pair_ref[lines : 2 * lines] if backward else pair_ref[0:lines]
    passed = pair_ref[2 * lines : 2 * lines + 1] * total + near
    total_ref[...] = jnp.where(places_ref[1] == (0 if backward else 1), passed, total)


def split_halves(place_ref, sum_ref, sent_ref, kept_ref):
    half = kept_ref.shape[0]
    side = place_ref[2]
    sent_ref[...] = sum_ref[pl.ds(pl.multiple_of((1 - side) * half, 8), half)].astype(BF16)
    kept_ref[...] = sum_ref[pl.ds(pl.multiple_of(side * half, 8), half)]


def fill_rim(s_ref, up_ref, x_ref, down_ref):
    _, rows, width, _ = x_ref.shape
    s_ref[0] = shifted(flat(up_ref[...]), width)
    for r in range(rows):
        s_ref[r + 1] = shifted(flat(x_ref[:, r]), width)
    s_ref[rows + 1] = shifted(flat(down_ref[...]), width)


def out_grad_kernel(place_ref, ends_ref, pair_ref, local_ref, product_ref, cot_ref, up_ref, down_ref, low_ref, first_ref, last_ref, sent_ref, kept_ref, token_ref, s_ref, total_ref, sum_ref):
    rows, frames, width, p = local_ref.shape
    c = cot_ref.shape[-1]

    @pl.when(pl.program_id(0) == 0)
    def _():
        combine(place_ref, ends_ref, pair_ref, total_ref, False)
        sum_ref[...] = jnp.zeros_like(sum_ref)
        token_ref[...] = jnp.zeros_like(token_ref)

    fill_rim(s_ref, up_ref, cot_ref, down_ref)
    product = product_ref[...]
    turned = []
    for r in range(rows):
        state = local_ref[r] + product[:, None, :] * total_ref[r * width : (r + 1) * width][None]
        low = state.astype(BF16)
        low_ref[r] = low
        if r == 0:
            first_ref[...] = low
        if r == rows - 1:
            last_ref[...] = low
        turned.append(flat(low).T)
    turned = jnp.concatenate(turned, axis=1)
    for i in range(3):
        gain = dot(turned, flat(s_ref[2 - i : 2 - i + rows]))
        for j in range(3):
            tap = 3 * i + j
            sum_ref[tap * p : (tap + 1) * p] += gain[:, (2 - j) * c : (3 - j) * c]

    @pl.when(pl.program_id(0) == pl.num_programs(0) - 1)
    def _():
        split_halves(place_ref, sum_ref, sent_ref, kept_ref)


def in_grad_kernel(place_ref, ends_ref, pair_ref, local_ref, product_ref, decay_ref, x_ref, up_ref, down_ref, *refs):
    sent_ref, kept_ref, token_ref, s_ref, total_ref, sum_ref, flat_ref = refs[-7:]
    rows, frames, width, p = local_ref.shape
    c = x_ref.shape[-1]

    @pl.when(pl.program_id(0) == 0)
    def _():
        combine(place_ref, ends_ref, pair_ref, total_ref, True)
        sum_ref[...] = jnp.zeros_like(sum_ref)
        token_ref[...] = jnp.zeros_like(token_ref)

    fill_rim(s_ref, up_ref, x_ref, down_ref)
    product = product_ref[...]
    decay = decay_ref[...]
    scale = jnp.sqrt((1.0 - decay) * (1.0 + decay))[:, None, :]
    turned = []
    for r in range(rows):
        adjoint = local_ref[r] + product[:, None, :] * total_ref[r * width : (r + 1) * width][None]
        turned.append(flat((scale * adjoint).astype(BF16)).T)
    turned = jnp.concatenate(turned, axis=1)
    for i in range(3):
        sum_ref[i] += dot(turned, flat(s_ref[i : i + rows]))

    @pl.when(pl.program_id(0) == pl.num_programs(0) - 1)
    def _():
        for i in range(3):
            for j in range(3):
                tap = 3 * i + j
                flat_ref[tap * c : (tap + 1) * c] = sum_ref[i, :, j * c : (j + 1) * c].T
        split_halves(place_ref, flat_ref, sent_ref, kept_ref)


def kernel_grads(places, ends, pair, local, product, x, up, down, half, decays, block, after=None):
    rows, frames, width, p = local.shape
    c = x.shape[-1]
    halo_spec = pl.BlockSpec((None, block, width, c), lambda b: (half, b, 0, 0))
    local_spec = pl.BlockSpec((rows, block, width, p), lambda b: (0, b, 0, 0))
    frame_spec = pl.BlockSpec((block, p), lambda b: (b, 0))
    x_spec = pl.BlockSpec((block, rows, width, c), lambda b: (b, 0, 0, 0))
    lead = [
        SCALARS,
        pl.BlockSpec(ends.shape, lambda b: (0, 0, 0)),
        pl.BlockSpec(pair.shape, lambda b: (0, 0)),
        local_spec,
        frame_spec,
    ]
    tail = [x_spec, halo_spec, halo_spec]
    scratch = [
        pltpu.VMEM((rows + 2, block * width, 3 * c), BF16),
        pltpu.VMEM((rows * width, p), F32),
    ]
    estimate = cost(2 * frames * rows * width * 9 * c * p, 10 * 2**20)
    forward = decays is None
    lines, columns = (9 * p // 2, c) if forward else (9 * c // 2, p)
    grad_specs = [pl.BlockSpec((lines, columns), lambda b: (0, 0))] * 2 + [TOKEN_SPEC]
    grad_shapes = [
        jax.ShapeDtypeStruct((lines, columns), BF16),
        jax.ShapeDtypeStruct((lines, columns), F32),
        TOKEN,
    ]
    if forward:
        line_spec = pl.BlockSpec((block, width, p), lambda b: (b, 0, 0))
        line = jax.ShapeDtypeStruct((frames, width, p), BF16)
        return pl.pallas_call(
            out_grad_kernel,
            grid=(frames // block,),
            in_specs=lead + tail,
            out_specs=[local_spec, line_spec, line_spec] + grad_specs,
            out_shape=[jax.ShapeDtypeStruct(local.shape, BF16), line, line] + grad_shapes,
            scratch_shapes=scratch + [pltpu.VMEM((2 * lines, columns), F32)],
            compiler_params=params(),
            cost_estimate=estimate,
            name="out_grad",
        )(places, ends, pair, local, product, x, up, down)
    return pl.pallas_call(
        in_grad_kernel,
        grid=(frames // block,),
        in_specs=lead + [frame_spec] + tail + [ANYWHERE] * len(after),
        out_specs=grad_specs,
        out_shape=grad_shapes,
        scratch_shapes=scratch
        + [pltpu.VMEM((3, p, 3 * c), F32), pltpu.VMEM((2 * lines, columns), F32)],
        compiler_params=params(),
        cost_estimate=estimate,
        name="in_grad",
    )(places, ends, pair, local, product, decays, x, up, down, *after)


def outputs_kernel(low_ref, up_ref, down_ref, w_ref, x_ref, skip_ref, after_ref, out_ref, token_ref, s_ref):
    token_ref[...] = jnp.zeros_like(token_ref)
    rows, frames, width, p = low_ref.shape
    s_ref[0] = shifted(flat(up_ref[...]), width)
    for r in range(rows):
        s_ref[r + 1] = shifted(flat(low_ref[r]), width)
    s_ref[rows + 1] = shifted(flat(down_ref[...]), width)
    lhs = jnp.concatenate([flat(s_ref[i : i + rows]) for i in range(3)], axis=1)
    mixed = dot(lhs, flat(w_ref[...])).reshape(rows, frames, width, -1)
    skip = skip_ref[...][0:1].reshape(1, 1, -1)
    for r in range(rows):
        out_ref[:, r] = (mixed[r] + skip * x_ref[:, r].astype(F32)).astype(BF16)


def outputs_conv(low, up, down, taps, x, skip, block, after):
    rows, frames, width, p = low.shape
    c = x.shape[-1]
    halo_spec = pl.BlockSpec((block, width, p), lambda b: (b, 0, 0))
    x_spec = pl.BlockSpec((block, rows, width, c), lambda b: (b, 0, 0, 0))
    return pl.pallas_call(
        outputs_kernel,
        grid=(frames // block,),
        in_specs=[
            pl.BlockSpec((rows, block, width, p), lambda b: (0, b, 0, 0)),
            halo_spec,
            halo_spec,
            pl.BlockSpec(taps.shape, lambda b: (0, 0, 0)),
            x_spec,
            pl.BlockSpec((1, c), lambda b: (0, 0)),
            ANYWHERE,
        ],
        out_specs=[x_spec, TOKEN_SPEC],
        out_shape=[jax.ShapeDtypeStruct(x.shape, BF16), TOKEN],
        scratch_shapes=[pltpu.VMEM((rows + 2, block * width, 3 * p), BF16)],
        compiler_params=params(),
        cost_estimate=cost(2 * frames * rows * width * 9 * c * p, 8 * 2**20),
        name="outputs_conv",
    )(low, up, down, taps, x, skip, after)


def edge_rows_kernel(places_ref, x_ref, cot_ref, first_ref, last_ref, sems):
    rows = x_ref.shape[1]
    copies = []
    for k, ref in enumerate((x_ref, cot_ref)):
        copies.append(pltpu.make_async_copy(ref.at[:, 0], first_ref.at[k], sems.at[k, 0]))
        copies.append(pltpu.make_async_copy(ref.at[:, rows - 1], last_ref.at[k], sems.at[k, 1]))
    for copy in copies:
        copy.start()
    for copy in copies:
        copy.wait()


def edge_rows(places, x, cot):
    frames, rows, width, c = x.shape
    line = jax.ShapeDtypeStruct((2, frames, width, c), x.dtype)
    return pl.pallas_call(
        edge_rows_kernel,
        in_specs=[SCALARS, ANYWHERE, ANYWHERE],
        out_specs=[ANYWHERE, ANYWHERE],
        out_shape=[line, line],
        scratch_shapes=[pltpu.SemaphoreType.DMA((2, 2))],
        compiler_params=pltpu.CompilerParams(vmem_limit_bytes=56 * 2**20),
        cost_estimate=cost(0, 2**22),
        name="edge_rows",
    )(places, x, cot)


def row_halo(first, last):
    axes = ("y", "core")
    count = lax.axis_size("y") * lax.axis_size("core")
    up = lax.ppermute(last, axes, [(i, i + 1) for i in range(count - 1)])
    down = lax.ppermute(first, axes, [(i + 1, i) for i in range(count - 1)])
    return up, down


CORES = [(0, 1), (1, 0)]
FAR = 64


def small_call(body, name, out_shapes, operands, after, places=None, mib=2):
    extra = [] if places is None else [places]

    def kernel(*refs):
        body(*refs[len(after) : -1])
        refs[-1][...] = jnp.zeros_like(refs[-1])

    whole = pl.BlockSpec(memory_space=pltpu.VMEM)
    return pl.pallas_call(
        kernel,
        in_specs=[ANYWHERE] * len(after) + [SCALARS] * len(extra) + [whole] * len(operands),
        out_specs=[whole] * (len(out_shapes) + 1),
        out_shape=[jax.ShapeDtypeStruct(*shape) for shape in out_shapes] + [TOKEN],
        compiler_params=pltpu.CompilerParams(vmem_limit_bytes=10 * 2**20),
        cost_estimate=cost(mib * 2**29, 2**21),
        name=name,
    )(*after, *extra, *operands)


def quarter(index, ref):
    size = ref.shape[0] // 4
    return pl.ds(pl.multiple_of(index * size, 16), size)


def add_kernel(places_ref, kept_ref, got_ref, own_ref, *sent_refs):
    for k, ref in enumerate((own_ref,) + sent_refs):
        at = quarter(jnp.bitwise_xor(places_ref[3], k), kept_ref)
        ref[...] = (kept_ref[at] + got_ref[at].astype(F32)).astype(ref.dtype)


def tree(terms):
    while len(terms) > 1:
        terms = [terms[k] + terms[k + 1] for k in range(0, len(terms), 2)]
    return terms[0]


def sum_kernel(scale, *refs):
    total = tree([ref[...].astype(F32) for ref in refs[:-1]])
    if scale is not None:
        total = total * scale
    refs[-1][...] = total.astype(BF16)


def pack_kernel(*refs):
    for k, ref in enumerate(refs[:-1]):
        refs[-1][k] = ref[...]


def merge_kernel(places_ref, own_ref, other_ref, out_ref):
    count, lines, _ = own_ref.shape
    for side, ref in enumerate((own_ref, other_ref)):
        for k in range(count):
            index = jnp.bitwise_xor(places_ref[2], side) * count
            index = index + jnp.bitwise_xor(places_ref[3], k)
            at = pl.ds(pl.multiple_of(index * lines, 16), lines)
            out_ref[at] = ref[k].astype(F32)


def from_others(sent, axes):
    count = math.prod(lax.axis_size(name) for name in axes)
    if not isinstance(sent, list):
        sent = [sent] * (count - 1)
    return [
        lax.ppermute(part, axes, [(i, i ^ k) for i in range(count)])
        for k, part in enumerate(sent, 1)
    ]


def per_device(inputs, decays, in_kernel, out_kernel, skip, cotangent):
    clips, frames, rows, width, c = inputs.shape
    p = in_kernel.shape[3]
    block = 16
    devices = math.prod(lax.axis_size(name) for name in ("a", "x", "y", "core"))
    grad_scale = 1.0 / math.sqrt(clips * frames * rows * width * devices)
    x = inputs.reshape(frames, rows, width, c)
    cot = cotangent.reshape(frames, rows, width, c)
    places = jnp.stack([lax.axis_index(name) for name in ("a", "x", "core", ("x", "y"))])
    places = places.astype(jnp.int32)
    deep = lax.axis_size("a")
    lines = rows * width

    up, down = row_halo(*edge_rows(places, x, cot))
    x_part, x_taps = interior_conv(x, in_kernel, False, block)
    cot_part, cot_taps = interior_conv(cot, out_kernel, True, block)
    states, running, end = local_scan(x_part, up, down, 0, x_taps, decays, block, False, decays)
    adjoint, trailing, message = local_scan(
        cot_part, up, down, 1, cot_taps, decays, block, True, end
    )
    pair = lax.ppermute(message, "x", [(0, 1), (1, 0)])
    ends, token = small_call(
        pair_kernel, "pair", [((deep, lines + 8, p), F32)], [message, pair], [], places
    )
    ends = lax.all_to_all(ends, "a", 0, 0)

    low, low_first, low_last, sent, kept, token = kernel_grads(
        places, ends, pair, states, running, cot, up, down, 1, None, block
    )
    got = lax.ppermute(sent, "core", CORES)
    low_up, low_down = row_halo(low_first, low_last)
    half, q = kept.shape
    part_shape = (half // 4, q)

    def add(name, kept, got, after):
        shapes = [(part_shape, F32)] + [(part_shape, BF16)] * 3
        own, *sent, token = small_call(add_kernel, name, shapes, [kept, got], after, places)
        return own, from_others(sent, ("x", "y")), token

    def sums(name, scale, terms, after, mib=2):
        body = functools.partial(sum_kernel, scale)
        return small_call(body, name, [(part_shape, BF16)], terms, after, None, mib)

    def swapped(part, bit):
        return lax.ppermute(part, "a", [(i, i ^ bit) for i in range(deep)])

    bits = [2**k for k in range(deep.bit_length() - 1)]

    def middle(name, part, other, after):
        for bit in bits[1:]:
            part, token = sums(name, None, [part, other], after)
            other, after = swapped(part, bit), [token]
        return part, other, after[0]

    def pack(name, terms, after):
        packed, token = small_call(pack_kernel, name, [((4,) + part_shape, BF16)], terms, after)
        return packed, lax.ppermute(packed, "core", CORES), token

    def merge(name, packed, other, after):
        return small_call(
            merge_kernel, name, [((2 * half, q), F32)], [packed, other], after, places
        )

    own, others, token = add("out_add", kept, got, [token])
    sent, kept, token = kernel_grads(
        places, ends, pair, adjoint, trailing, x, up, down, 0, decays, block, [token, low_up, low_down]
    )
    got = lax.ppermute(sent, "core", CORES)
    out_part, token = sums("out_share", None, [own] + others, [token], mib=FAR)
    out_other = swapped(out_part, 1)
    own, others, token = add("in_add", kept, got, [token])
    out_part, out_other, token = middle("out_mid", out_part, out_other, [token])
    outputs, token = outputs_conv(
        low, low_up, low_down, out_kernel.reshape(3, 3 * p, c), x, skip.reshape(1, c), block, token
    )
    in_part, token = sums("in_share", None, [own] + others, [token])
    in_other = swapped(in_part, 1)
    out_part, token = sums("out_total", grad_scale, [out_part, out_other], [token])
    out_others = from_others(out_part, ("x", "y"))
    in_part, in_other, token = middle("in_mid", in_part, in_other, [token])
    out_packed, out_other, token = pack("out_pack", [out_part] + out_others, [token])
    in_part, token = sums("in_total", grad_scale, [in_part, in_other], [token])
    in_others = from_others(in_part, ("x", "y"))
    out_grad, token = merge("out_merge", out_packed, out_other, [token])
    in_packed, in_other, token = pack("in_pack", [in_part] + in_others, [token])
    in_grad, _ = merge("in_merge", in_packed, in_other, [token])
    return (
        outputs.reshape(inputs.shape),
        in_grad.reshape(in_kernel.shape),
        out_grad.reshape(out_kernel.shape),
    )


def solution(mesh):
    frames = mesh.shape["tm"]
    rows = mesh.shape["row"]
    fine = jax.sharding.Mesh(
        mesh.devices.reshape(frames // 2, 2, rows // 2, 2), ("a", "x", "y", "core")
    )
    cells = P(None, ("a", "x"), ("y", "core"), None, None)
    return jax.shard_map(
        per_device,
        mesh=fine,
        in_specs=(cells, P(("a", "x"), None), P(), P(), P(), cells),
        out_specs=(cells, P(), P()),
        check_vma=False,
    )
```

```python
import functools
import math

import jax
import jax.numpy as jnp
from jax import lax
from jax.experimental import pallas as pl
from jax.experimental.pallas import tpu as pltpu
from jax.sharding import PartitionSpec as P

BF16 = jnp.bfloat16
F32 = jnp.float32


SCALARS = pl.BlockSpec(memory_space=pltpu.SMEM)
ANYWHERE = pl.BlockSpec(memory_space=pl.ANY)
TOKEN = jax.ShapeDtypeStruct((8, 128), F32)
TOKEN_SPEC = pl.BlockSpec((8, 128), lambda *b: (0, 0))


def params(mib=20):
    return pltpu.CompilerParams(
        dimension_semantics=("arbitrary",), vmem_limit_bytes=mib * 1024 * 1024
    )


def cost(flops, nbytes):
    return pl.CostEstimate(flops=int(flops), bytes_accessed=int(nbytes), transcendentals=0)


def shifted(cells, width):
    count = cells.shape[0]
    wide = cells.astype(F32)
    column = lax.broadcasted_iota(jnp.int32, (count, 1), 0) % width
    left = jnp.where(column == 0, 0.0, pltpu.roll(wide, 1, 0))
    right = jnp.where(column == width - 1, 0.0, pltpu.roll(wide, count - 1, 0))
    return jnp.concatenate([left.astype(BF16), cells, right.astype(BF16)], axis=1)


def flat(block):
    return block.reshape(-1, block.shape[-1])


def dot(a, b):
    return jnp.dot(a, b, preferred_element_type=F32)


def interior_body(x_ref, w_ref, out_ref, s_ref):
    frames, rows, width, _ = x_ref.shape
    lines = frames * width
    for r in range(rows):
        s_ref[r] = shifted(flat(x_ref[:, r]), width)

    def conv(first, count, taps):
        lhs = jnp.concatenate(
            [flat(s_ref[first + i - 1 : first + i - 1 + count]) for i in taps], axis=1
        )
        rhs = w_ref[taps[0] : taps[-1] + 1].reshape(len(taps) * w_ref.shape[1], w_ref.shape[2])
        out_ref[first : first + count] = dot(lhs, rhs).reshape(count, frames, width, -1)

    conv(1, rows - 2, (0, 1, 2))
    conv(0, 1, (1, 2))
    conv(rows - 1, 1, (0, 1))


def interior_plain_kernel(x_ref, w_ref, out_ref, s_ref):
    interior_body(x_ref, w_ref, out_ref, s_ref)


def interior_flipped_kernel(x_ref, w_ref, out_ref, wt_ref, s_ref):
    @pl.when(pl.program_id(0) == 0)
    def _():
        for i in range(3):
            for j in range(3):
                c = w_ref.shape[3]
                wt_ref[i, j * c : (j + 1) * c, :] = w_ref[2 - i, 2 - j].T

    interior_body(x_ref, wt_ref, out_ref, s_ref)


def interior_conv(x, w, flipped, block):
    frames, rows, width, c = x.shape
    p = w.shape[2] if flipped else w.shape[3]
    part_shape = jax.ShapeDtypeStruct((rows, frames, width, p), F32)
    part_spec = pl.BlockSpec((rows, block, width, p), lambda b: (0, b, 0, 0))
    x_spec = pl.BlockSpec((block, rows, width, c), lambda b: (b, 0, 0, 0))
    scratch = [pltpu.VMEM((rows, block * width, 3 * c), BF16)]
    estimate = cost(2 * frames * rows * width * 9 * c * p, 8 * 2**20)
    taps_spec = pl.BlockSpec((3, 3 * c, p), lambda b: (0, 0, 0))
    if flipped:
        return pl.pallas_call(
            interior_flipped_kernel,
            grid=(frames // block,),
            in_specs=[
                x_spec,
                pl.BlockSpec(w.shape, lambda b: (0, 0, 0, 0)),
            ],
            out_specs=[part_spec, taps_spec],
            out_shape=[part_shape, jax.ShapeDtypeStruct((3, 3 * c, p), BF16)],
            scratch_shapes=scratch,
            compiler_params=params(),
            cost_estimate=estimate,
            name="interior_cot",
        )(x, w)
    taps = w.reshape(3, 3 * c, p)
    part = pl.pallas_call(
        interior_plain_kernel,
        grid=(frames // block,),
        in_specs=[x_spec, taps_spec],
        out_specs=part_spec,
        out_shape=part_shape,
        scratch_shapes=scratch,
        compiler_params=params(),
        cost_estimate=estimate,
        name="interior_in",
    )(x, taps)
    return part, taps


def scan_kernel(backward, part_ref, up_ref, down_ref, w_ref, decay_ref, before_ref, local_ref, product_ref, end_ref, carry_ref, run_ref):
    rows, frames, width, p = part_ref.shape
    lines = rows * width

    @pl.when(pl.program_id(0) == 0)
    def _():
        carry_ref[...] = jnp.zeros_like(carry_ref)
        run_ref[...] = jnp.ones_like(run_ref)

    top = dot(shifted(flat(up_ref[...]), width), w_ref[0]).reshape(frames, width, p)
    low = dot(shifted(flat(down_ref[...]), width), w_ref[2]).reshape(frames, width, p)
    decay = decay_ref[...]
    scale = jnp.sqrt((1.0 - decay) * (1.0 + decay))
    state = [carry_ref[r * width : (r + 1) * width] for r in range(rows)]
    run = run_ref[0:1]
    for step in range(frames):
        t = frames - 1 - step if backward else step
        factor = decay[t : t + 1]
        gain = scale[t : t + 1]
        if backward:
            product_ref[t : t + 1] = run
        run = run * factor
        if not backward:
            product_ref[t : t + 1] = run
        for r in range(rows):
            term = part_ref[r, t]
            if r == 0:
                term = term + top[t]
            if r == rows - 1:
                term = term + low[t]
            if backward:
                full = term + state[r]
                local_ref[r, t] = full
                state[r] = factor * full
            else:
                state[r] = factor * state[r] + gain * term
                local_ref[r, t] = state[r]
    for r in range(rows):
        carry_ref[r * width : (r + 1) * width] = state[r]
    run_ref[...] = jnp.broadcast_to(run, run_ref.shape)

    @pl.when(pl.program_id(0) == pl.num_programs(0) - 1)
    def _():
        if backward:
            message = [before_ref[...]] + state + [jnp.broadcast_to(run, (8, p))]
        else:
            message = state
        end_ref[...] = jnp.concatenate(message, axis=0)


def local_scan(part, up, down, half, taps, decays, block, backward, before):
    rows, frames, width, p = part.shape
    c = up.shape[-1]
    blocks = frames // block
    at = (lambda b: blocks - 1 - b) if backward else (lambda b: b)
    halo_spec = pl.BlockSpec((None, block, width, c), lambda b: (half, at(b), 0, 0))
    part_spec = pl.BlockSpec((rows, block, width, p), lambda b: (0, at(b), 0, 0))
    frame_spec = pl.BlockSpec((block, p), lambda b: (at(b), 0))
    lines = rows * width
    message = 2 * lines + 8 if backward else lines
    return pl.pallas_call(
        functools.partial(scan_kernel, backward),
        grid=(blocks,),
        in_specs=[
            part_spec,
            halo_spec,
            halo_spec,
            pl.BlockSpec(taps.shape, lambda b: (0, 0, 0)),
            frame_spec,
            pl.BlockSpec(before.shape, lambda b: (0, 0)),
        ],
        out_specs=[part_spec, frame_spec, pl.BlockSpec((message, p), lambda b: (0, 0))],
        out_shape=[
            jax.ShapeDtypeStruct(part.shape, F32),
            jax.ShapeDtypeStruct((frames, p), F32),
            jax.ShapeDtypeStruct((message, p), F32),
        ],
        scratch_shapes=[pltpu.VMEM((lines, p), F32), pltpu.VMEM((8, p), F32)],
        compiler_params=params(),
        cost_estimate=cost(4 * frames * width * 3 * c * p, 12 * 2**20),
        name="scan_back" if backward else "scan_fwd",
    )(part, up, down, taps, decays, before)


def pair_kernel(places_ref, own_ref, got_ref, out_ref):
    deep, height, _ = out_ref.shape
    lines = height - 8
    first = places_ref[1] == 0
    own_end, got_end = own_ref[0:lines], got_ref[0:lines]
    own_start, got_start = own_ref[lines : 2 * lines], got_ref[lines : 2 * lines]
    own_product, got_product = own_ref[2 * lines :], got_ref[2 * lines :]
    end = jnp.where(
        first, got_product[0:1] * own_end + got_end, own_product[0:1] * got_end + own_end
    )
    start = jnp.where(
        first, own_product[0:1] * got_start + own_start, got_product[0:1] * own_start + got_start
    )
    product = own_product * got_product
    for k in range(deep):
        out_ref[k, 0:lines] = jnp.where(k > places_ref[0], end, start)
        out_ref[k, lines:] = product


def combine(places_ref, ends_ref, pair_ref, total_ref, backward):
    place = places_ref[0]
    count = ends_ref.shape[0]
    lines = total_ref.shape[0]
    total = jnp.zeros(total_ref.shape, F32)
    order = range(count - 1, -1, -1) if backward else range(count)
    for k in order:
        passed = ends_ref[k, lines : lines + 1] * total + ends_ref[k, 0:lines]
        total = jnp.where(k > place if backward else k < place, passed, total)
    near = pair_ref[lines : 2 * lines] if backward else pair_ref[0:lines]
    passed = pair_ref[2 * lines : 2 * lines + 1] * total + near
    total_ref[...] = jnp.where(places_ref[1] == (0 if backward else 1), passed, total)


def split_halves(place_ref, sum_ref, sent_ref, kept_ref):
    half = kept_ref.shape[0]
    side = place_ref[2]
    sent_ref[...] = sum_ref[pl.ds(pl.multiple_of((1 - side) * half, 8), half)].astype(BF16)
    kept_ref[...] = sum_ref[pl.ds(pl.multiple_of(side * half, 8), half)]


def fill_rim(s_ref, up_ref, x_ref, down_ref):
    _, rows, width, _ = x_ref.shape
    s_ref[0] = shifted(flat(up_ref[...]), width)
    for r in range(rows):
        s_ref[r + 1] = shifted(flat(x_ref[:, r]), width)
    s_ref[rows + 1] = shifted(flat(down_ref[...]), width)


def out_grad_kernel(place_ref, ends_ref, pair_ref, local_ref, product_ref, cot_ref, up_ref, down_ref, low_ref, first_ref, last_ref, sent_ref, kept_ref, token_ref, s_ref, total_ref, sum_ref):
    rows, frames, width, p = local_ref.shape
    c = cot_ref.shape[-1]

    @pl.when(pl.program_id(0) == 0)
    def _():
        combine(place_ref, ends_ref, pair_ref, total_ref, False)
        sum_ref[...] = jnp.zeros_like(sum_ref)
        token_ref[...] = jnp.zeros_like(token_ref)

    fill_rim(s_ref, up_ref, cot_ref, down_ref)
    product = product_ref[...]
    turned = []
    for r in range(rows):
        state = local_ref[r] + product[:, None, :] * total_ref[r * width : (r + 1) * width][None]
        low = state.astype(BF16)
        low_ref[r] = low
        if r == 0:
            first_ref[...] = low
        if r == rows - 1:
            last_ref[...] = low
        turned.append(flat(low).T)
    turned = jnp.concatenate(turned, axis=1)
    for i in range(3):
        gain = dot(turned, flat(s_ref[2 - i : 2 - i + rows]))
        for j in range(3):
            tap = 3 * i + j
            sum_ref[tap * p : (tap + 1) * p] += gain[:, (2 - j) * c : (3 - j) * c]

    @pl.when(pl.program_id(0) == pl.num_programs(0) - 1)
    def _():
        split_halves(place_ref, sum_ref, sent_ref, kept_ref)


def in_grad_kernel(place_ref, ends_ref, pair_ref, local_ref, product_ref, decay_ref, x_ref, up_ref, down_ref, *refs):
    sent_ref, kept_ref, token_ref, s_ref, total_ref, sum_ref, flat_ref = refs[-7:]
    rows, frames, width, p = local_ref.shape
    c = x_ref.shape[-1]

    @pl.when(pl.program_id(0) == 0)
    def _():
        combine(place_ref, ends_ref, pair_ref, total_ref, True)
        sum_ref[...] = jnp.zeros_like(sum_ref)
        token_ref[...] = jnp.zeros_like(token_ref)

    fill_rim(s_ref, up_ref, x_ref, down_ref)
    product = product_ref[...]
    decay = decay_ref[...]
    scale = jnp.sqrt((1.0 - decay) * (1.0 + decay))[:, None, :]
    turned = []
    for r in range(rows):
        adjoint = local_ref[r] + product[:, None, :] * total_ref[r * width : (r + 1) * width][None]
        turned.append(flat((scale * adjoint).astype(BF16)).T)
    turned = jnp.concatenate(turned, axis=1)
    for i in range(3):
        sum_ref[i] += dot(turned, flat(s_ref[i : i + rows]))

    @pl.when(pl.program_id(0) == pl.num_programs(0) - 1)
    def _():
        for i in range(3):
            for j in range(3):
                tap = 3 * i + j
                flat_ref[tap * c : (tap + 1) * c] = sum_ref[i, :, j * c : (j + 1) * c].T
        split_halves(place_ref, flat_ref, sent_ref, kept_ref)


def kernel_grads(places, ends, pair, local, product, x, up, down, half, decays, block, after=None):
    rows, frames, width, p = local.shape
    c = x.shape[-1]
    halo_spec = pl.BlockSpec((None, block, width, c), lambda b: (half, b, 0, 0))
    local_spec = pl.BlockSpec((rows, block, width, p), lambda b: (0, b, 0, 0))
    frame_spec = pl.BlockSpec((block, p), lambda b: (b, 0))
    x_spec = pl.BlockSpec((block, rows, width, c), lambda b: (b, 0, 0, 0))
    lead = [
        SCALARS,
        pl.BlockSpec(ends.shape, lambda b: (0, 0, 0)),
        pl.BlockSpec(pair.shape, lambda b: (0, 0)),
        local_spec,
        frame_spec,
    ]
    tail = [x_spec, halo_spec, halo_spec]
    scratch = [
        pltpu.VMEM((rows + 2, block * width, 3 * c), BF16),
        pltpu.VMEM((rows * width, p), F32),
    ]
    estimate = cost(2 * frames * rows * width * 9 * c * p, 10 * 2**20)
    forward = decays is None
    lines, columns = (9 * p // 2, c) if forward else (9 * c // 2, p)
    grad_specs = [pl.BlockSpec((lines, columns), lambda b: (0, 0))] * 2 + [TOKEN_SPEC]
    grad_shapes = [
        jax.ShapeDtypeStruct((lines, columns), BF16),
        jax.ShapeDtypeStruct((lines, columns), F32),
        TOKEN,
    ]
    if forward:
        line_spec = pl.BlockSpec((block, width, p), lambda b: (b, 0, 0))
        line = jax.ShapeDtypeStruct((frames, width, p), BF16)
        return pl.pallas_call(
            out_grad_kernel,
            grid=(frames // block,),
            in_specs=lead + tail,
            out_specs=[local_spec, line_spec, line_spec] + grad_specs,
            out_shape=[jax.ShapeDtypeStruct(local.shape, BF16), line, line] + grad_shapes,
            scratch_shapes=scratch + [pltpu.VMEM((2 * lines, columns), F32)],
            compiler_params=params(),
            cost_estimate=estimate,
            name="out_grad",
        )(places, ends, pair, local, product, x, up, down)
    return pl.pallas_call(
        in_grad_kernel,
        grid=(frames // block,),
        in_specs=lead + [frame_spec] + tail + [ANYWHERE] * len(after),
        out_specs=grad_specs,
        out_shape=grad_shapes,
        scratch_shapes=scratch
        + [pltpu.VMEM((3, p, 3 * c), F32), pltpu.VMEM((2 * lines, columns), F32)],
        compiler_params=params(),
        cost_estimate=estimate,
        name="in_grad",
    )(places, ends, pair, local, product, decays, x, up, down, *after)


def outputs_kernel(low_ref, up_ref, down_ref, w_ref, x_ref, skip_ref, after_ref, out_ref, token_ref, s_ref):
    token_ref[...] = jnp.zeros_like(token_ref)
    rows, frames, width, p = low_ref.shape
    s_ref[0] = shifted(flat(up_ref[...]), width)
    for r in range(rows):
        s_ref[r + 1] = shifted(flat(low_ref[r]), width)
    s_ref[rows + 1] = shifted(flat(down_ref[...]), width)
    lhs = jnp.concatenate([flat(s_ref[i : i + rows]) for i in range(3)], axis=1)
    mixed = dot(lhs, flat(w_ref[...])).reshape(rows, frames, width, -1)
    skip = skip_ref[...][0:1].reshape(1, 1, -1)
    for r in range(rows):
        out_ref[:, r] = (mixed[r] + skip * x_ref[:, r].astype(F32)).astype(BF16)


def outputs_conv(low, up, down, taps, x, skip, block, after):
    rows, frames, width, p = low.shape
    c = x.shape[-1]
    halo_spec = pl.BlockSpec((block, width, p), lambda b: (b, 0, 0))
    x_spec = pl.BlockSpec((block, rows, width, c), lambda b: (b, 0, 0, 0))
    return pl.pallas_call(
        outputs_kernel,
        grid=(frames // block,),
        in_specs=[
            pl.BlockSpec((rows, block, width, p), lambda b: (0, b, 0, 0)),
            halo_spec,
            halo_spec,
            pl.BlockSpec(taps.shape, lambda b: (0, 0, 0)),
            x_spec,
            pl.BlockSpec((1, c), lambda b: (0, 0)),
            ANYWHERE,
        ],
        out_specs=[x_spec, TOKEN_SPEC],
        out_shape=[jax.ShapeDtypeStruct(x.shape, BF16), TOKEN],
        scratch_shapes=[pltpu.VMEM((rows + 2, block * width, 3 * p), BF16)],
        compiler_params=params(),
        cost_estimate=cost(2 * frames * rows * width * 9 * c * p, 8 * 2**20),
        name="outputs_conv",
    )(low, up, down, taps, x, skip, after)


def edge_rows_kernel(places_ref, *refs):
    first_ref, last_ref = refs[4:]
    for k in range(2):
        first_ref[k] = refs[2 * k][:, 0]
        last_ref[k] = refs[2 * k + 1][:, 0]


def edge_rows(places, x, cot, block):
    frames, rows, width, c = x.shape
    line = jax.ShapeDtypeStruct((2, frames, width, c), x.dtype)
    line_spec = pl.BlockSpec((2, block, width, c), lambda b: (0, b, 0, 0))
    first = pl.BlockSpec((block, 1, width, c), lambda b: (b, 0, 0, 0))
    last = pl.BlockSpec((block, 1, width, c), lambda b: (b, rows - 1, 0, 0))
    return pl.pallas_call(
        edge_rows_kernel,
        grid=(frames // block,),
        in_specs=[SCALARS, first, last, first, last],
        out_specs=[line_spec, line_spec],
        out_shape=[line, line],
        compiler_params=params(56),
        cost_estimate=cost(0, 2**22),
        name="edge_rows",
    )(places, x, x, cot, cot)


def row_halo(first, last):
    axes = ("y", "core")
    count = lax.axis_size("y") * lax.axis_size("core")
    up = lax.ppermute(last, axes, [(i, i + 1) for i in range(count - 1)])
    down = lax.ppermute(first, axes, [(i + 1, i) for i in range(count - 1)])
    return up, down


CORES = [(0, 1), (1, 0)]
FAR = 64


def small_call(body, name, out_shapes, operands, after, places=None, mib=2):
    extra = [] if places is None else [places]

    def kernel(*refs):
        body(*refs[len(after) : -1])
        refs[-1][...] = jnp.zeros_like(refs[-1])

    whole = pl.BlockSpec(memory_space=pltpu.VMEM)
    return pl.pallas_call(
        kernel,
        in_specs=[ANYWHERE] * len(after) + [SCALARS] * len(extra) + [whole] * len(operands),
        out_specs=[whole] * (len(out_shapes) + 1),
        out_shape=[jax.ShapeDtypeStruct(*shape) for shape in out_shapes] + [TOKEN],
        compiler_params=pltpu.CompilerParams(vmem_limit_bytes=10 * 2**20),
        cost_estimate=cost(mib * 2**29, 2**21),
        name=name,
    )(*after, *extra, *operands)


def quarter(index, ref):
    size = ref.shape[0] // 4
    return pl.ds(pl.multiple_of(index * size, 16), size)


def add_kernel(places_ref, kept_ref, got_ref, own_ref, *sent_refs):
    for k, ref in enumerate((own_ref,) + sent_refs):
        at = quarter(jnp.bitwise_xor(places_ref[3], k), kept_ref)
        ref[...] = (kept_ref[at] + got_ref[at].astype(F32)).astype(ref.dtype)


def tree(terms):
    while len(terms) > 1:
        terms = [terms[k] + terms[k + 1] for k in range(0, len(terms), 2)]
    return terms[0]


def sum_kernel(scale, *refs):
    total = tree([ref[...].astype(F32) for ref in refs[:-1]])
    if scale is not None:
        total = total * scale
    refs[-1][...] = total.astype(BF16)


def pack_kernel(*refs):
    for k, ref in enumerate(refs[:-1]):
        refs[-1][k] = ref[...]


def merge_kernel(places_ref, own_ref, other_ref, out_ref):
    count, lines, _ = own_ref.shape
    for side, ref in enumerate((own_ref, other_ref)):
        for k in range(count):
            index = jnp.bitwise_xor(places_ref[2], side) * count
            index = index + jnp.bitwise_xor(places_ref[3], k)
            at = pl.ds(pl.multiple_of(index * lines, 16), lines)
            out_ref[at] = ref[k].astype(F32)


def from_others(sent, axes):
    count = math.prod(lax.axis_size(name) for name in axes)
    if not isinstance(sent, list):
        sent = [sent] * (count - 1)
    return [
        lax.ppermute(part, axes, [(i, i ^ k) for i in range(count)])
        for k, part in enumerate(sent, 1)
    ]


def per_device(inputs, decays, in_kernel, out_kernel, skip, cotangent):
    clips, frames, rows, width, c = inputs.shape
    p = in_kernel.shape[3]
    block = 16
    devices = math.prod(lax.axis_size(name) for name in ("a", "x", "y", "core"))
    grad_scale = 1.0 / math.sqrt(clips * frames * rows * width * devices)
    x = inputs.reshape(frames, rows, width, c)
    cot = cotangent.reshape(frames, rows, width, c)
    places = jnp.stack([lax.axis_index(name) for name in ("a", "x", "core", ("x", "y"))])
    places = places.astype(jnp.int32)
    deep = lax.axis_size("a")
    lines = rows * width

    up, down = row_halo(*edge_rows(places, x, cot, block))
    x_part, x_taps = interior_conv(x, in_kernel, False, block)
    cot_part, cot_taps = interior_conv(cot, out_kernel, True, block)
    states, running, end = local_scan(x_part, up, down, 0, x_taps, decays, block, False, decays)
    adjoint, trailing, message = local_scan(
        cot_part, up, down, 1, cot_taps, decays, block, True, end
    )
    pair = lax.ppermute(message, "x", [(0, 1), (1, 0)])
    ends, token = small_call(
        pair_kernel, "pair", [((deep, lines + 8, p), F32)], [message, pair], [], places
    )
    ends = lax.all_to_all(ends, "a", 0, 0)

    low, low_first, low_last, sent, kept, token = kernel_grads(
        places, ends, pair, states, running, cot, up, down, 1, None, block
    )
    got = lax.ppermute(sent, "core", CORES)
    low_up, low_down = row_halo(low_first, low_last)
    half, q = kept.shape
    part_shape = (half // 4, q)

    def add(name, kept, got, after):
        shapes = [(part_shape, F32)] + [(part_shape, BF16)] * 3
        own, *sent, token = small_call(add_kernel, name, shapes, [kept, got], after, places)
        return own, from_others(sent, ("x", "y")), token

    def sums(name, scale, terms, after, mib=2):
        body = functools.partial(sum_kernel, scale)
        return small_call(body, name, [(part_shape, BF16)], terms, after, None, mib)

    def swapped(part, bit):
        return lax.ppermute(part, "a", [(i, i ^ bit) for i in range(deep)])

    bits = [2**k for k in range(deep.bit_length() - 1)]

    def middle(name, part, other, after):
        for bit in bits[1:]:
            part, token = sums(name, None, [part, other], after)
            other, after = swapped(part, bit), [token]
        return part, other, after[0]

    def pack(name, terms, after):
        packed, token = small_call(pack_kernel, name, [((4,) + part_shape, BF16)], terms, after)
        return packed, lax.ppermute(packed, "core", CORES), token

    def merge(name, packed, other, after):
        return small_call(
            merge_kernel, name, [((2 * half, q), F32)], [packed, other], after, places
        )

    own, others, token = add("out_add", kept, got, [token])
    sent, kept, token = kernel_grads(
        places, ends, pair, adjoint, trailing, x, up, down, 0, decays, block, [token]
    )
    got = lax.ppermute(sent, "core", CORES)
    out_part, token = sums("out_share", None, [own] + others, [token, low_up, low_down], mib=FAR)
    out_other = swapped(out_part, 1)
    own, others, token = add("in_add", kept, got, [token])
    out_part, out_other, token = middle("out_mid", out_part, out_other, [token])
    outputs, token = outputs_conv(
        low, low_up, low_down, out_kernel.reshape(3, 3 * p, c), x, skip.reshape(1, c), block, token
    )
    in_part, token = sums("in_share", None, [own] + others, [token])
    in_other = swapped(in_part, 1)
    out_part, token = sums("out_total", grad_scale, [out_part, out_other], [token])
    out_others = from_others(out_part, ("x", "y"))
    in_part, in_other, token = middle("in_mid", in_part, in_other, [token])
    out_packed, out_other, token = pack("out_pack", [out_part] + out_others, [token])
    in_part, token = sums("in_total", grad_scale, [in_part, in_other], [token])
    in_others = from_others(in_part, ("x", "y"))
    out_grad, token = merge("out_merge", out_packed, out_other, [token])
    in_packed, in_other, token = pack("in_pack", [in_part] + in_others, [token])
    in_grad, _ = merge("in_merge", in_packed, in_other, [token])
    return (
        outputs.reshape(inputs.shape),
        in_grad.reshape(in_kernel.shape),
        out_grad.reshape(out_kernel.shape),
    )


def solution(mesh):
    frames = mesh.shape["tm"]
    rows = mesh.shape["row"]
    fine = jax.sharding.Mesh(
        mesh.devices.reshape(frames // 2, 2, rows // 2, 2), ("a", "x", "y", "core")
    )
    cells = P(None, ("a", "x"), ("y", "core"), None, None)
    return jax.shard_map(
        per_device,
        mesh=fine,
        in_specs=(cells, P(("a", "x"), None), P(), P(), P(), cells),
        out_specs=(cells, P(), P()),
        check_vma=False,
    )
```

```python
import functools
import math

import jax
import jax.numpy as jnp
from jax import lax
from jax.experimental import pallas as pl
from jax.experimental.pallas import tpu as pltpu
from jax.sharding import PartitionSpec as P

BF16 = jnp.bfloat16
F32 = jnp.float32


SCALARS = pl.BlockSpec(memory_space=pltpu.SMEM)
ANYWHERE = pl.BlockSpec(memory_space=pl.ANY)
TOKEN = jax.ShapeDtypeStruct((8, 128), F32)
TOKEN_SPEC = pl.BlockSpec((8, 128), lambda *b: (0, 0))


def params(mib=20):
    return pltpu.CompilerParams(
        dimension_semantics=("arbitrary",), vmem_limit_bytes=mib * 1024 * 1024
    )


def cost(flops, nbytes):
    return pl.CostEstimate(flops=int(flops), bytes_accessed=int(nbytes), transcendentals=0)


def shifted(cells, width):
    count = cells.shape[0]
    wide = cells.astype(F32)
    column = lax.broadcasted_iota(jnp.int32, (count, 1), 0) % width
    left = jnp.where(column == 0, 0.0, pltpu.roll(wide, 1, 0))
    right = jnp.where(column == width - 1, 0.0, pltpu.roll(wide, count - 1, 0))
    return jnp.concatenate([left.astype(BF16), cells, right.astype(BF16)], axis=1)


def flat(block):
    return block.reshape(-1, block.shape[-1])


def dot(a, b):
    return jnp.dot(a, b, preferred_element_type=F32)


def interior_body(x_ref, w_ref, out_ref, s_ref):
    frames, rows, width, _ = x_ref.shape
    lines = frames * width
    for r in range(rows):
        s_ref[r] = shifted(flat(x_ref[:, r]), width)

    def conv(first, count, taps):
        lhs = jnp.concatenate(
            [flat(s_ref[first + i - 1 : first + i - 1 + count]) for i in taps], axis=1
        )
        rhs = w_ref[taps[0] : taps[-1] + 1].reshape(len(taps) * w_ref.shape[1], w_ref.shape[2])
        out_ref[first : first + count] = dot(lhs, rhs).reshape(count, frames, width, -1)

    conv(1, rows - 2, (0, 1, 2))
    conv(0, 1, (1, 2))
    conv(rows - 1, 1, (0, 1))


def interior_plain_kernel(x_ref, w_ref, out_ref, s_ref):
    interior_body(x_ref, w_ref, out_ref, s_ref)


def interior_flipped_kernel(x_ref, w_ref, out_ref, wt_ref, s_ref):
    @pl.when(pl.program_id(0) == 0)
    def _():
        for i in range(3):
            for j in range(3):
                c = w_ref.shape[3]
                wt_ref[i, j * c : (j + 1) * c, :] = w_ref[2 - i, 2 - j].T

    interior_body(x_ref, wt_ref, out_ref, s_ref)


def interior_conv(x, w, flipped, block):
    frames, rows, width, c = x.shape
    p = w.shape[2] if flipped else w.shape[3]
    part_shape = jax.ShapeDtypeStruct((rows, frames, width, p), F32)
    part_spec = pl.BlockSpec((rows, block, width, p), lambda b: (0, b, 0, 0))
    x_spec = pl.BlockSpec((block, rows, width, c), lambda b: (b, 0, 0, 0))
    scratch = [pltpu.VMEM((rows, block * width, 3 * c), BF16)]
    estimate = cost(2 * frames * rows * width * 9 * c * p, 8 * 2**20)
    taps_spec = pl.BlockSpec((3, 3 * c, p), lambda b: (0, 0, 0))
    if flipped:
        return pl.pallas_call(
            interior_flipped_kernel,
            grid=(frames // block,),
            in_specs=[
                x_spec,
                pl.BlockSpec(w.shape, lambda b: (0, 0, 0, 0)),
            ],
            out_specs=[part_spec, taps_spec],
            out_shape=[part_shape, jax.ShapeDtypeStruct((3, 3 * c, p), BF16)],
            scratch_shapes=scratch,
            compiler_params=params(),
            cost_estimate=estimate,
            name="interior_cot",
        )(x, w)
    taps = w.reshape(3, 3 * c, p)
    part = pl.pallas_call(
        interior_plain_kernel,
        grid=(frames // block,),
        in_specs=[x_spec, taps_spec],
        out_specs=part_spec,
        out_shape=part_shape,
        scratch_shapes=scratch,
        compiler_params=params(),
        cost_estimate=estimate,
        name="interior_in",
    )(x, taps)
    return part, taps


def scan_kernel(backward, part_ref, up_ref, down_ref, w_ref, decay_ref, before_ref, local_ref, product_ref, end_ref, carry_ref, run_ref):
    rows, frames, width, p = part_ref.shape
    lines = rows * width

    @pl.when(pl.program_id(0) == 0)
    def _():
        carry_ref[...] = jnp.zeros_like(carry_ref)
        run_ref[...] = jnp.ones_like(run_ref)

    top = dot(shifted(flat(up_ref[...]), width), w_ref[0]).reshape(frames, width, p)
    low = dot(shifted(flat(down_ref[...]), width), w_ref[2]).reshape(frames, width, p)
    decay = decay_ref[...]
    scale = jnp.sqrt((1.0 - decay) * (1.0 + decay))
    state = [carry_ref[r * width : (r + 1) * width] for r in range(rows)]
    run = run_ref[0:1]
    for step in range(frames):
        t = frames - 1 - step if backward else step
        factor = decay[t : t + 1]
        gain = scale[t : t + 1]
        if backward:
            product_ref[t : t + 1] = run
        run = run * factor
        if not backward:
            product_ref[t : t + 1] = run
        for r in range(rows):
            term = part_ref[r, t]
            if r == 0:
                term = term + top[t]
            if r == rows - 1:
                term = term + low[t]
            if backward:
                full = term + state[r]
                local_ref[r, t] = full
                state[r] = factor * full
            else:
                state[r] = factor * state[r] + gain * term
                local_ref[r, t] = state[r]
    for r in range(rows):
        carry_ref[r * width : (r + 1) * width] = state[r]
    run_ref[...] = jnp.broadcast_to(run, run_ref.shape)

    @pl.when(pl.program_id(0) == pl.num_programs(0) - 1)
    def _():
        if backward:
            message = [before_ref[...]] + state + [jnp.broadcast_to(run, (8, p))]
        else:
            message = state
        end_ref[...] = jnp.concatenate(message, axis=0)


def local_scan(part, up, down, half, taps, decays, block, backward, before):
    rows, frames, width, p = part.shape
    c = up.shape[-1]
    blocks = frames // block
    at = (lambda b: blocks - 1 - b) if backward else (lambda b: b)
    halo_spec = pl.BlockSpec((None, block, width, c), lambda b: (half, at(b), 0, 0))
    part_spec = pl.BlockSpec((rows, block, width, p), lambda b: (0, at(b), 0, 0))
    frame_spec = pl.BlockSpec((block, p), lambda b: (at(b), 0))
    lines = rows * width
    message = 2 * lines + 8 if backward else lines
    return pl.pallas_call(
        functools.partial(scan_kernel, backward),
        grid=(blocks,),
        in_specs=[
            part_spec,
            halo_spec,
            halo_spec,
            pl.BlockSpec(taps.shape, lambda b: (0, 0, 0)),
            frame_spec,
            pl.BlockSpec(before.shape, lambda b: (0, 0)),
        ],
        out_specs=[part_spec, frame_spec, pl.BlockSpec((message, p), lambda b: (0, 0))],
        out_shape=[
            jax.ShapeDtypeStruct(part.shape, F32),
            jax.ShapeDtypeStruct((frames, p), F32),
            jax.ShapeDtypeStruct((message, p), F32),
        ],
        scratch_shapes=[pltpu.VMEM((lines, p), F32), pltpu.VMEM((8, p), F32)],
        compiler_params=params(),
        cost_estimate=cost(4 * frames * width * 3 * c * p, 12 * 2**20),
        name="scan_back" if backward else "scan_fwd",
    )(part, up, down, taps, decays, before)


def pair_kernel(places_ref, own_ref, got_ref, out_ref):
    deep, height, _ = out_ref.shape
    lines = height - 8
    first = places_ref[1] == 0
    own_end, got_end = own_ref[0:lines], got_ref[0:lines]
    own_start, got_start = own_ref[lines : 2 * lines], got_ref[lines : 2 * lines]
    own_product, got_product = own_ref[2 * lines :], got_ref[2 * lines :]
    end = jnp.where(
        first, got_product[0:1] * own_end + got_end, own_product[0:1] * got_end + own_end
    )
    start = jnp.where(
        first, own_product[0:1] * got_start + own_start, got_product[0:1] * own_start + got_start
    )
    product = own_product * got_product
    for k in range(deep):
        out_ref[k, 0:lines] = jnp.where(k > places_ref[0], end, start)
        out_ref[k, lines:] = product


def combine(places_ref, ends_ref, pair_ref, total_ref, backward):
    place = places_ref[0]
    count = ends_ref.shape[0]
    lines = total_ref.shape[0]
    total = jnp.zeros(total_ref.shape, F32)
    order = range(count - 1, -1, -1) if backward else range(count)
    for k in order:
        passed = ends_ref[k, lines : lines + 1] * total + ends_ref[k, 0:lines]
        total = jnp.where(k > place if backward else k < place, passed, total)
    near = pair_ref[lines : 2 * lines] if backward else pair_ref[0:lines]
    passed = pair_ref[2 * lines : 2 * lines + 1] * total + near
    total_ref[...] = jnp.where(places_ref[1] == (0 if backward else 1), passed, total)


def split_halves(place_ref, sum_ref, sent_ref, kept_ref):
    half = kept_ref.shape[0]
    side = place_ref[2]
    sent_ref[...] = sum_ref[pl.ds(pl.multiple_of((1 - side) * half, 8), half)].astype(BF16)
    kept_ref[...] = sum_ref[pl.ds(pl.multiple_of(side * half, 8), half)]


def fill_rim(s_ref, up_ref, x_ref, down_ref):
    _, rows, width, _ = x_ref.shape
    s_ref[0] = shifted(flat(up_ref[...]), width)
    for r in range(rows):
        s_ref[r + 1] = shifted(flat(x_ref[:, r]), width)
    s_ref[rows + 1] = shifted(flat(down_ref[...]), width)


def out_grad_kernel(place_ref, ends_ref, pair_ref, local_ref, product_ref, cot_ref, up_ref, down_ref, low_ref, first_ref, last_ref, sent_ref, kept_ref, token_ref, s_ref, total_ref, sum_ref):
    rows, frames, width, p = local_ref.shape
    c = cot_ref.shape[-1]

    @pl.when(pl.program_id(0) == 0)
    def _():
        combine(place_ref, ends_ref, pair_ref, total_ref, False)
        sum_ref[...] = jnp.zeros_like(sum_ref)
        token_ref[...] = jnp.zeros_like(token_ref)

    fill_rim(s_ref, up_ref, cot_ref, down_ref)
    product = product_ref[...]
    turned = []
    for r in range(rows):
        state = local_ref[r] + product[:, None, :] * total_ref[r * width : (r + 1) * width][None]
        low = state.astype(BF16)
        low_ref[r] = low
        if r == 0:
            first_ref[...] = low
        if r == rows - 1:
            last_ref[...] = low
        turned.append(flat(low).T)
    turned = jnp.concatenate(turned, axis=1)
    for i in range(3):
        gain = dot(turned, flat(s_ref[2 - i : 2 - i + rows]))
        for j in range(3):
            tap = 3 * i + j
            sum_ref[tap * p : (tap + 1) * p] += gain[:, (2 - j) * c : (3 - j) * c]

    @pl.when(pl.program_id(0) == pl.num_programs(0) - 1)
    def _():
        split_halves(place_ref, sum_ref, sent_ref, kept_ref)


def in_grad_kernel(place_ref, ends_ref, pair_ref, local_ref, product_ref, decay_ref, x_ref, up_ref, down_ref, *refs):
    sent_ref, kept_ref, token_ref, s_ref, total_ref, sum_ref, flat_ref = refs[-7:]
    rows, frames, width, p = local_ref.shape
    c = x_ref.shape[-1]

    @pl.when(pl.program_id(0) == 0)
    def _():
        combine(place_ref, ends_ref, pair_ref, total_ref, True)
        sum_ref[...] = jnp.zeros_like(sum_ref)
        token_ref[...] = jnp.zeros_like(token_ref)

    fill_rim(s_ref, up_ref, x_ref, down_ref)
    product = product_ref[...]
    decay = decay_ref[...]
    scale = jnp.sqrt((1.0 - decay) * (1.0 + decay))[:, None, :]
    turned = []
    for r in range(rows):
        adjoint = local_ref[r] + product[:, None, :] * total_ref[r * width : (r + 1) * width][None]
        turned.append(flat((scale * adjoint).astype(BF16)).T)
    turned = jnp.concatenate(turned, axis=1)
    for i in range(3):
        sum_ref[i] += dot(turned, flat(s_ref[i : i + rows]))

    @pl.when(pl.program_id(0) == pl.num_programs(0) - 1)
    def _():
        for i in range(3):
            for j in range(3):
                tap = 3 * i + j
                flat_ref[tap * c : (tap + 1) * c] = sum_ref[i, :, j * c : (j + 1) * c].T
        split_halves(place_ref, flat_ref, sent_ref, kept_ref)


def kernel_grads(places, ends, pair, local, product, x, up, down, half, decays, block, after=None):
    rows, frames, width, p = local.shape
    c = x.shape[-1]
    halo_spec = pl.BlockSpec((None, block, width, c), lambda b: (half, b, 0, 0))
    local_spec = pl.BlockSpec((rows, block, width, p), lambda b: (0, b, 0, 0))
    frame_spec = pl.BlockSpec((block, p), lambda b: (b, 0))
    x_spec = pl.BlockSpec((block, rows, width, c), lambda b: (b, 0, 0, 0))
    lead = [
        SCALARS,
        pl.BlockSpec(ends.shape, lambda b: (0, 0, 0)),
        pl.BlockSpec(pair.shape, lambda b: (0, 0)),
        local_spec,
        frame_spec,
    ]
    tail = [x_spec, halo_spec, halo_spec]
    scratch = [
        pltpu.VMEM((rows + 2, block * width, 3 * c), BF16),
        pltpu.VMEM((rows * width, p), F32),
    ]
    estimate = cost(2 * frames * rows * width * 9 * c * p, 10 * 2**20)
    forward = decays is None
    lines, columns = (9 * p // 2, c) if forward else (9 * c // 2, p)
    grad_specs = [pl.BlockSpec((lines, columns), lambda b: (0, 0))] * 2 + [TOKEN_SPEC]
    grad_shapes = [
        jax.ShapeDtypeStruct((lines, columns), BF16),
        jax.ShapeDtypeStruct((lines, columns), F32),
        TOKEN,
    ]
    if forward:
        line_spec = pl.BlockSpec((block, width, p), lambda b: (b, 0, 0))
        line = jax.ShapeDtypeStruct((frames, width, p), BF16)
        return pl.pallas_call(
            out_grad_kernel,
            grid=(frames // block,),
            in_specs=lead + tail,
            out_specs=[local_spec, line_spec, line_spec] + grad_specs,
            out_shape=[jax.ShapeDtypeStruct(local.shape, BF16), line, line] + grad_shapes,
            scratch_shapes=scratch + [pltpu.VMEM((2 * lines, columns), F32)],
            compiler_params=params(),
            cost_estimate=estimate,
            name="out_grad",
        )(places, ends, pair, local, product, x, up, down)
    return pl.pallas_call(
        in_grad_kernel,
        grid=(frames // block,),
        in_specs=lead + [frame_spec] + tail + [ANYWHERE] * len(after),
        out_specs=grad_specs,
        out_shape=grad_shapes,
        scratch_shapes=scratch
        + [pltpu.VMEM((3, p, 3 * c), F32), pltpu.VMEM((2 * lines, columns), F32)],
        compiler_params=params(),
        cost_estimate=estimate,
        name="in_grad",
    )(places, ends, pair, local, product, decays, x, up, down, *after)


def outputs_kernel(low_ref, up_ref, down_ref, w_ref, x_ref, skip_ref, after_ref, out_ref, token_ref, s_ref):
    token_ref[...] = jnp.zeros_like(token_ref)
    rows, frames, width, p = low_ref.shape
    s_ref[0] = shifted(flat(up_ref[...]), width)
    for r in range(rows):
        s_ref[r + 1] = shifted(flat(low_ref[r]), width)
    s_ref[rows + 1] = shifted(flat(down_ref[...]), width)
    lhs = jnp.concatenate([flat(s_ref[i : i + rows]) for i in range(3)], axis=1)
    mixed = dot(lhs, flat(w_ref[...])).reshape(rows, frames, width, -1)
    skip = skip_ref[...][0:1].reshape(1, 1, -1)
    for r in range(rows):
        out_ref[:, r] = (mixed[r] + skip * x_ref[:, r].astype(F32)).astype(BF16)


def outputs_conv(low, up, down, taps, x, skip, block, after):
    rows, frames, width, p = low.shape
    c = x.shape[-1]
    halo_spec = pl.BlockSpec((block, width, p), lambda b: (b, 0, 0))
    x_spec = pl.BlockSpec((block, rows, width, c), lambda b: (b, 0, 0, 0))
    return pl.pallas_call(
        outputs_kernel,
        grid=(frames // block,),
        in_specs=[
            pl.BlockSpec((rows, block, width, p), lambda b: (0, b, 0, 0)),
            halo_spec,
            halo_spec,
            pl.BlockSpec(taps.shape, lambda b: (0, 0, 0)),
            x_spec,
            pl.BlockSpec((1, c), lambda b: (0, 0)),
            ANYWHERE,
        ],
        out_specs=[x_spec, TOKEN_SPEC],
        out_shape=[jax.ShapeDtypeStruct(x.shape, BF16), TOKEN],
        scratch_shapes=[pltpu.VMEM((rows + 2, block * width, 3 * p), BF16)],
        compiler_params=params(),
        cost_estimate=cost(2 * frames * rows * width * 9 * c * p, 8 * 2**20),
        name="outputs_conv",
    )(low, up, down, taps, x, skip, after)


def edge_rows_kernel(places_ref, *refs):
    first_ref, last_ref = refs[2:]
    for k in range(2):
        first_ref[k] = refs[k][:, 0]
        last_ref[k] = refs[k][:, refs[k].shape[1] - 1]


def edge_rows(places, x, cot, block):
    frames, rows, width, c = x.shape
    line = jax.ShapeDtypeStruct((2, frames, width, c), x.dtype)
    line_spec = pl.BlockSpec((2, block, width, c), lambda b: (0, b, 0, 0))
    x_spec = pl.BlockSpec((block, rows, width, c), lambda b: (b, 0, 0, 0))
    return pl.pallas_call(
        edge_rows_kernel,
        grid=(frames // block,),
        in_specs=[SCALARS, x_spec, x_spec],
        out_specs=[line_spec, line_spec],
        out_shape=[line, line],
        compiler_params=params(56),
        cost_estimate=cost(0, 2**22),
        name="edge_rows",
    )(places, x, cot)


def row_halo(first, last):
    axes = ("y", "core")
    count = lax.axis_size("y") * lax.axis_size("core")
    up = lax.ppermute(last, axes, [(i, i + 1) for i in range(count - 1)])
    down = lax.ppermute(first, axes, [(i + 1, i) for i in range(count - 1)])
    return up, down


CORES = [(0, 1), (1, 0)]
FAR = 64


def small_call(body, name, out_shapes, operands, after, places=None, mib=2):
    extra = [] if places is None else [places]

    def kernel(*refs):
        body(*refs[len(after) : -1])
        refs[-1][...] = jnp.zeros_like(refs[-1])

    whole = pl.BlockSpec(memory_space=pltpu.VMEM)
    return pl.pallas_call(
        kernel,
        in_specs=[ANYWHERE] * len(after) + [SCALARS] * len(extra) + [whole] * len(operands),
        out_specs=[whole] * (len(out_shapes) + 1),
        out_shape=[jax.ShapeDtypeStruct(*shape) for shape in out_shapes] + [TOKEN],
        compiler_params=pltpu.CompilerParams(vmem_limit_bytes=10 * 2**20),
        cost_estimate=cost(mib * 2**29, 2**21),
        name=name,
    )(*after, *extra, *operands)


def quarter(index, ref):
    size = ref.shape[0] // 4
    return pl.ds(pl.multiple_of(index * size, 16), size)


def add_kernel(places_ref, kept_ref, got_ref, own_ref, *sent_refs):
    for k, ref in enumerate((own_ref,) + sent_refs):
        at = quarter(jnp.bitwise_xor(places_ref[3], k), kept_ref)
        ref[...] = (kept_ref[at] + got_ref[at].astype(F32)).astype(ref.dtype)


def tree(terms):
    while len(terms) > 1:
        terms = [terms[k] + terms[k + 1] for k in range(0, len(terms), 2)]
    return terms[0]


def sum_kernel(scale, *refs):
    total = tree([ref[...].astype(F32) for ref in refs[:-1]])
    if scale is not None:
        total = total * scale
    refs[-1][...] = total.astype(BF16)


def pack_kernel(*refs):
    for k, ref in enumerate(refs[:-1]):
        refs[-1][k] = ref[...]


def merge_kernel(places_ref, own_ref, other_ref, out_ref):
    count, lines, _ = own_ref.shape
    for side, ref in enumerate((own_ref, other_ref)):
        for k in range(count):
            index = jnp.bitwise_xor(places_ref[2], side) * count
            index = index + jnp.bitwise_xor(places_ref[3], k)
            at = pl.ds(pl.multiple_of(index * lines, 16), lines)
            out_ref[at] = ref[k].astype(F32)


def from_others(sent, axes):
    count = math.prod(lax.axis_size(name) for name in axes)
    if not isinstance(sent, list):
        sent = [sent] * (count - 1)
    return [
        lax.ppermute(part, axes, [(i, i ^ k) for i in range(count)])
        for k, part in enumerate(sent, 1)
    ]


def per_device(inputs, decays, in_kernel, out_kernel, skip, cotangent):
    clips, frames, rows, width, c = inputs.shape
    p = in_kernel.shape[3]
    block = 16
    devices = math.prod(lax.axis_size(name) for name in ("a", "x", "y", "core"))
    grad_scale = 1.0 / math.sqrt(clips * frames * rows * width * devices)
    x = inputs.reshape(frames, rows, width, c)
    cot = cotangent.reshape(frames, rows, width, c)
    places = jnp.stack([lax.axis_index(name) for name in ("a", "x", "core", ("x", "y"))])
    places = places.astype(jnp.int32)
    deep = lax.axis_size("a")
    lines = rows * width

    up, down = row_halo(*edge_rows(places, x, cot, block))
    x_part, x_taps = interior_conv(x, in_kernel, False, block)
    cot_part, cot_taps = interior_conv(cot, out_kernel, True, block)
    states, running, end = local_scan(x_part, up, down, 0, x_taps, decays, block, False, decays)
    adjoint, trailing, message = local_scan(
        cot_part, up, down, 1, cot_taps, decays, block, True, end
    )
    pair = lax.ppermute(message, "x", [(0, 1), (1, 0)])
    ends, token = small_call(
        pair_kernel, "pair", [((deep, lines + 8, p), F32)], [message, pair], [], places
    )
    ends = lax.all_to_all(ends, "a", 0, 0)

    low, low_first, low_last, sent, kept, token = kernel_grads(
        places, ends, pair, states, running, cot, up, down, 1, None, block
    )
    got = lax.ppermute(sent, "core", CORES)
    low_up, low_down = row_halo(low_first, low_last)
    half, q = kept.shape
    part_shape = (half // 4, q)

    def add(name, kept, got, after):
        shapes = [(part_shape, F32)] + [(part_shape, BF16)] * 3
        own, *sent, token = small_call(add_kernel, name, shapes, [kept, got], after, places)
        return own, from_others(sent, ("x", "y")), token

    def sums(name, scale, terms, after, mib=2):
        body = functools.partial(sum_kernel, scale)
        return small_call(body, name, [(part_shape, BF16)], terms, after, None, mib)

    def swapped(part, bit):
        return lax.ppermute(part, "a", [(i, i ^ bit) for i in range(deep)])

    bits = [2**k for k in range(deep.bit_length() - 1)]

    def middle(name, part, other, after):
        for bit in bits[1:]:
            part, token = sums(name, None, [part, other], after)
            other, after = swapped(part, bit), [token]
        return part, other, after[0]

    def pack(name, terms, after, mib=2):
        shape = (4,) + part_shape
        packed, token = small_call(pack_kernel, name, [(shape, BF16)], terms, after, None, mib)
        return packed, lax.ppermute(packed, "core", CORES), token

    def merge(name, packed, other, after):
        return small_call(
            merge_kernel, name, [((2 * half, q), F32)], [packed, other], after, places
        )

    own, others, token = add("out_add", kept, got, [token])
    sent, kept, token = kernel_grads(
        places, ends, pair, adjoint, trailing, x, up, down, 0, decays, block, [token]
    )
    got = lax.ppermute(sent, "core", CORES)
    out_part, token = sums("out_share", None, [own] + others, [token, low_up, low_down], mib=FAR)
    out_other = swapped(out_part, 1)
    own, others, token = add("in_add", kept, got, [token])
    outputs, token = outputs_conv(
        low, low_up, low_down, out_kernel.reshape(3, 3 * p, c), x, skip.reshape(1, c), block, token
    )
    out_part, out_other, token = middle("out_mid", out_part, out_other, [token])
    in_part, token = sums("in_share", None, [own] + others, [token])
    in_other = swapped(in_part, 1)
    in_part, in_other, token = middle("in_mid", in_part, in_other, [token])
    out_part, token = sums("out_total", grad_scale, [out_part, out_other], [token], mib=FAR)
    out_others = from_others(out_part, ("x", "y"))
    in_part, token = sums("in_total", grad_scale, [in_part, in_other], [token])
    in_others = from_others(in_part, ("x", "y"))
    out_packed, out_other, token = pack("out_pack", [out_part] + out_others, [token], FAR)
    out_grad, token = merge("out_merge", out_packed, out_other, [token])
    in_packed, in_other, token = pack("in_pack", [in_part] + in_others, [token])
    in_grad, _ = merge("in_merge", in_packed, in_other, [token])
    return (
        outputs.reshape(inputs.shape),
        in_grad.reshape(in_kernel.shape),
        out_grad.reshape(out_kernel.shape),
    )


def solution(mesh):
    frames = mesh.shape["tm"]
    rows = mesh.shape["row"]
    fine = jax.sharding.Mesh(
        mesh.devices.reshape(frames // 2, 2, rows // 2, 2), ("a", "x", "y", "core")
    )
    cells = P(None, ("a", "x"), ("y", "core"), None, None)
    return jax.shard_map(
        per_device,
        mesh=fine,
        in_specs=(cells, P(("a", "x"), None), P(), P(), P(), cells),
        out_specs=(cells, P(), P()),
        check_vma=False,
    )
```

```python
import functools
import math

import jax
import jax.numpy as jnp
from jax import lax
from jax.experimental import pallas as pl
from jax.experimental.pallas import tpu as pltpu
from jax.sharding import PartitionSpec as P

BF16 = jnp.bfloat16
F32 = jnp.float32


SCALARS = pl.BlockSpec(memory_space=pltpu.SMEM)
ANYWHERE = pl.BlockSpec(memory_space=pl.ANY)
TOKEN = jax.ShapeDtypeStruct((8, 128), F32)
TOKEN_SPEC = pl.BlockSpec((8, 128), lambda *b: (0, 0))


def params(mib=20):
    return pltpu.CompilerParams(
        dimension_semantics=("arbitrary",), vmem_limit_bytes=mib * 1024 * 1024
    )


def cost(flops, nbytes):
    return pl.CostEstimate(flops=int(flops), bytes_accessed=int(nbytes), transcendentals=0)


def shifted(cells, width):
    count = cells.shape[0]
    wide = cells.astype(F32)
    column = lax.broadcasted_iota(jnp.int32, (count, 1), 0) % width
    left = jnp.where(column == 0, 0.0, pltpu.roll(wide, 1, 0))
    right = jnp.where(column == width - 1, 0.0, pltpu.roll(wide, count - 1, 0))
    return jnp.concatenate([left.astype(BF16), cells, right.astype(BF16)], axis=1)


def flat(block):
    return block.reshape(-1, block.shape[-1])


def dot(a, b):
    return jnp.dot(a, b, preferred_element_type=F32)


def interior_body(x_ref, w_ref, out_ref, s_ref):
    frames, rows, width, _ = x_ref.shape
    lines = frames * width
    for r in range(rows):
        s_ref[r] = shifted(flat(x_ref[:, r]), width)

    def conv(first, count, taps):
        lhs = jnp.concatenate(
            [flat(s_ref[first + i - 1 : first + i - 1 + count]) for i in taps], axis=1
        )
        rhs = w_ref[taps[0] : taps[-1] + 1].reshape(len(taps) * w_ref.shape[1], w_ref.shape[2])
        out_ref[first : first + count] = dot(lhs, rhs).reshape(count, frames, width, -1)

    conv(1, rows - 2, (0, 1, 2))
    conv(0, 1, (1, 2))
    conv(rows - 1, 1, (0, 1))


def interior_plain_kernel(x_ref, w_ref, out_ref, s_ref):
    interior_body(x_ref, w_ref, out_ref, s_ref)


def interior_flipped_kernel(x_ref, w_ref, out_ref, wt_ref, s_ref):
    @pl.when(pl.program_id(0) == 0)
    def _():
        for i in range(3):
            for j in range(3):
                c = w_ref.shape[3]
                wt_ref[i, j * c : (j + 1) * c, :] = w_ref[2 - i, 2 - j].T

    interior_body(x_ref, wt_ref, out_ref, s_ref)


def interior_conv(x, w, flipped, block):
    frames, rows, width, c = x.shape
    p = w.shape[2] if flipped else w.shape[3]
    part_shape = jax.ShapeDtypeStruct((rows, frames, width, p), F32)
    part_spec = pl.BlockSpec((rows, block, width, p), lambda b: (0, b, 0, 0))
    x_spec = pl.BlockSpec((block, rows, width, c), lambda b: (b, 0, 0, 0))
    scratch = [pltpu.VMEM((rows, block * width, 3 * c), BF16)]
    estimate = cost(2 * frames * rows * width * 9 * c * p, 8 * 2**20)
    taps_spec = pl.BlockSpec((3, 3 * c, p), lambda b: (0, 0, 0))
    if flipped:
        return pl.pallas_call(
            interior_flipped_kernel,
            grid=(frames // block,),
            in_specs=[
                x_spec,
                pl.BlockSpec(w.shape, lambda b: (0, 0, 0, 0)),
            ],
            out_specs=[part_spec, taps_spec],
            out_shape=[part_shape, jax.ShapeDtypeStruct((3, 3 * c, p), BF16)],
            scratch_shapes=scratch,
            compiler_params=params(),
            cost_estimate=estimate,
            name="interior_cot",
        )(x, w)
    taps = w.reshape(3, 3 * c, p)
    part = pl.pallas_call(
        interior_plain_kernel,
        grid=(frames // block,),
        in_specs=[x_spec, taps_spec],
        out_specs=part_spec,
        out_shape=part_shape,
        scratch_shapes=scratch,
        compiler_params=params(),
        cost_estimate=estimate,
        name="interior_in",
    )(x, taps)
    return part, taps


def scan_kernel(backward, part_ref, up_ref, down_ref, w_ref, decay_ref, before_ref, local_ref, product_ref, end_ref, carry_ref, run_ref):
    rows, frames, width, p = part_ref.shape
    lines = rows * width

    @pl.when(pl.program_id(0) == 0)
    def _():
        carry_ref[...] = jnp.zeros_like(carry_ref)
        run_ref[...] = jnp.ones_like(run_ref)

    top = dot(shifted(flat(up_ref[...]), width), w_ref[0]).reshape(frames, width, p)
    low = dot(shifted(flat(down_ref[...]), width), w_ref[2]).reshape(frames, width, p)
    decay = decay_ref[...]
    scale = jnp.sqrt((1.0 - decay) * (1.0 + decay))
    state = [carry_ref[r * width : (r + 1) * width] for r in range(rows)]
    run = run_ref[0:1]
    for step in range(frames):
        t = frames - 1 - step if backward else step
        factor = decay[t : t + 1]
        gain = scale[t : t + 1]
        if backward:
            product_ref[t : t + 1] = run
        run = run * factor
        if not backward:
            product_ref[t : t + 1] = run
        for r in range(rows):
            term = part_ref[r, t]
            if r == 0:
                term = term + top[t]
            if r == rows - 1:
                term = term + low[t]
            if backward:
                full = term + state[r]
                local_ref[r, t] = full
                state[r] = factor * full
            else:
                state[r] = factor * state[r] + gain * term
                local_ref[r, t] = state[r]
    for r in range(rows):
        carry_ref[r * width : (r + 1) * width] = state[r]
    run_ref[...] = jnp.broadcast_to(run, run_ref.shape)

    @pl.when(pl.program_id(0) == pl.num_programs(0) - 1)
    def _():
        if backward:
            message = [before_ref[...]] + state + [jnp.broadcast_to(run, (8, p))]
        else:
            message = state
        end_ref[...] = jnp.concatenate(message, axis=0)


def local_scan(part, up, down, half, taps, decays, block, backward, before):
    rows, frames, width, p = part.shape
    c = up.shape[-1]
    blocks = frames // block
    at = (lambda b: blocks - 1 - b) if backward else (lambda b: b)
    halo_spec = pl.BlockSpec((None, block, width, c), lambda b: (half, at(b), 0, 0))
    part_spec = pl.BlockSpec((rows, block, width, p), lambda b: (0, at(b), 0, 0))
    frame_spec = pl.BlockSpec((block, p), lambda b: (at(b), 0))
    lines = rows * width
    message = 2 * lines + 8 if backward else lines
    return pl.pallas_call(
        functools.partial(scan_kernel, backward),
        grid=(blocks,),
        in_specs=[
            part_spec,
            halo_spec,
            halo_spec,
            pl.BlockSpec(taps.shape, lambda b: (0, 0, 0)),
            frame_spec,
            pl.BlockSpec(before.shape, lambda b: (0, 0)),
        ],
        out_specs=[part_spec, frame_spec, pl.BlockSpec((message, p), lambda b: (0, 0))],
        out_shape=[
            jax.ShapeDtypeStruct(part.shape, F32),
            jax.ShapeDtypeStruct((frames, p), F32),
            jax.ShapeDtypeStruct((message, p), F32),
        ],
        scratch_shapes=[pltpu.VMEM((lines, p), F32), pltpu.VMEM((8, p), F32)],
        compiler_params=params(),
        cost_estimate=cost(4 * frames * width * 3 * c * p, 12 * 2**20),
        name="scan_back" if backward else "scan_fwd",
    )(part, up, down, taps, decays, before)


def pair_kernel(places_ref, own_ref, got_ref, out_ref):
    deep, height, _ = out_ref.shape
    lines = height - 8
    first = places_ref[1] == 0
    own_end, got_end = own_ref[0:lines], got_ref[0:lines]
    own_start, got_start = own_ref[lines : 2 * lines], got_ref[lines : 2 * lines]
    own_product, got_product = own_ref[2 * lines :], got_ref[2 * lines :]
    end = jnp.where(
        first, got_product[0:1] * own_end + got_end, own_product[0:1] * got_end + own_end
    )
    start = jnp.where(
        first, own_product[0:1] * got_start + own_start, got_product[0:1] * own_start + got_start
    )
    product = own_product * got_product
    for k in range(deep):
        out_ref[k, 0:lines] = jnp.where(k > places_ref[0], end, start)
        out_ref[k, lines:] = product


def combine(places_ref, ends_ref, pair_ref, total_ref, backward):
    place = places_ref[0]
    count = ends_ref.shape[0]
    lines = total_ref.shape[0]
    total = jnp.zeros(total_ref.shape, F32)
    order = range(count - 1, -1, -1) if backward else range(count)
    for k in order:
        passed = ends_ref[k, lines : lines + 1] * total + ends_ref[k, 0:lines]
        total = jnp.where(k > place if backward else k < place, passed, total)
    near = pair_ref[lines : 2 * lines] if backward else pair_ref[0:lines]
    passed = pair_ref[2 * lines : 2 * lines + 1] * total + near
    total_ref[...] = jnp.where(places_ref[1] == (0 if backward else 1), passed, total)


def split_halves(place_ref, sum_ref, sent_ref, kept_ref):
    half = kept_ref.shape[0]
    side = place_ref[2]
    sent_ref[...] = sum_ref[pl.ds(pl.multiple_of((1 - side) * half, 8), half)].astype(BF16)
    kept_ref[...] = sum_ref[pl.ds(pl.multiple_of(side * half, 8), half)]


def fill_rim(s_ref, up_ref, x_ref, down_ref):
    _, rows, width, _ = x_ref.shape
    s_ref[0] = shifted(flat(up_ref[...]), width)
    for r in range(rows):
        s_ref[r + 1] = shifted(flat(x_ref[:, r]), width)
    s_ref[rows + 1] = shifted(flat(down_ref[...]), width)


def out_grad_kernel(place_ref, ends_ref, pair_ref, local_ref, product_ref, cot_ref, up_ref, down_ref, low_ref, first_ref, last_ref, sent_ref, kept_ref, token_ref, s_ref, total_ref, sum_ref):
    rows, frames, width, p = local_ref.shape
    c = cot_ref.shape[-1]

    @pl.when(pl.program_id(0) == 0)
    def _():
        combine(place_ref, ends_ref, pair_ref, total_ref, False)
        sum_ref[...] = jnp.zeros_like(sum_ref)
        token_ref[...] = jnp.zeros_like(token_ref)

    fill_rim(s_ref, up_ref, cot_ref, down_ref)
    product = product_ref[...]
    turned = []
    for r in range(rows):
        state = local_ref[r] + product[:, None, :] * total_ref[r * width : (r + 1) * width][None]
        low = state.astype(BF16)
        low_ref[r] = low
        if r == 0:
            first_ref[...] = low
        if r == rows - 1:
            last_ref[...] = low
        turned.append(flat(low).T)
    turned = jnp.concatenate(turned, axis=1)
    for i in range(3):
        gain = dot(turned, flat(s_ref[2 - i : 2 - i + rows]))
        for j in range(3):
            tap = 3 * i + j
            sum_ref[tap * p : (tap + 1) * p] += gain[:, (2 - j) * c : (3 - j) * c]

    @pl.when(pl.program_id(0) == pl.num_programs(0) - 1)
    def _():
        split_halves(place_ref, sum_ref, sent_ref, kept_ref)


def in_grad_kernel(place_ref, ends_ref, pair_ref, local_ref, product_ref, decay_ref, x_ref, up_ref, down_ref, *refs):
    sent_ref, kept_ref, token_ref, s_ref, total_ref, sum_ref, flat_ref = refs[-7:]
    rows, frames, width, p = local_ref.shape
    c = x_ref.shape[-1]

    @pl.when(pl.program_id(0) == 0)
    def _():
        combine(place_ref, ends_ref, pair_ref, total_ref, True)
        sum_ref[...] = jnp.zeros_like(sum_ref)
        token_ref[...] = jnp.zeros_like(token_ref)

    fill_rim(s_ref, up_ref, x_ref, down_ref)
    product = product_ref[...]
    decay = decay_ref[...]
    scale = jnp.sqrt((1.0 - decay) * (1.0 + decay))[:, None, :]
    turned = []
    for r in range(rows):
        adjoint = local_ref[r] + product[:, None, :] * total_ref[r * width : (r + 1) * width][None]
        turned.append(flat((scale * adjoint).astype(BF16)).T)
    turned = jnp.concatenate(turned, axis=1)
    for i in range(3):
        sum_ref[i] += dot(turned, flat(s_ref[i : i + rows]))

    @pl.when(pl.program_id(0) == pl.num_programs(0) - 1)
    def _():
        for i in range(3):
            for j in range(3):
                tap = 3 * i + j
                flat_ref[tap * c : (tap + 1) * c] = sum_ref[i, :, j * c : (j + 1) * c].T
        split_halves(place_ref, flat_ref, sent_ref, kept_ref)


def kernel_grads(places, ends, pair, local, product, x, up, down, half, decays, block, after=None):
    rows, frames, width, p = local.shape
    c = x.shape[-1]
    halo_spec = pl.BlockSpec((None, block, width, c), lambda b: (half, b, 0, 0))
    local_spec = pl.BlockSpec((rows, block, width, p), lambda b: (0, b, 0, 0))
    frame_spec = pl.BlockSpec((block, p), lambda b: (b, 0))
    x_spec = pl.BlockSpec((block, rows, width, c), lambda b: (b, 0, 0, 0))
    lead = [
        SCALARS,
        pl.BlockSpec(ends.shape, lambda b: (0, 0, 0)),
        pl.BlockSpec(pair.shape, lambda b: (0, 0)),
        local_spec,
        frame_spec,
    ]
    tail = [x_spec, halo_spec, halo_spec]
    scratch = [
        pltpu.VMEM((rows + 2, block * width, 3 * c), BF16),
        pltpu.VMEM((rows * width, p), F32),
    ]
    estimate = cost(2 * frames * rows * width * 9 * c * p, 10 * 2**20)
    forward = decays is None
    lines, columns = (9 * p // 2, c) if forward else (9 * c // 2, p)
    grad_specs = [pl.BlockSpec((lines, columns), lambda b: (0, 0))] * 2 + [TOKEN_SPEC]
    grad_shapes = [
        jax.ShapeDtypeStruct((lines, columns), BF16),
        jax.ShapeDtypeStruct((lines, columns), F32),
        TOKEN,
    ]
    if forward:
        line_spec = pl.BlockSpec((block, width, p), lambda b: (b, 0, 0))
        line = jax.ShapeDtypeStruct((frames, width, p), BF16)
        return pl.pallas_call(
            out_grad_kernel,
            grid=(frames // block,),
            in_specs=lead + tail,
            out_specs=[local_spec, line_spec, line_spec] + grad_specs,
            out_shape=[jax.ShapeDtypeStruct(local.shape, BF16), line, line] + grad_shapes,
            scratch_shapes=scratch + [pltpu.VMEM((2 * lines, columns), F32)],
            compiler_params=params(),
            cost_estimate=estimate,
            name="out_grad",
        )(places, ends, pair, local, product, x, up, down)
    return pl.pallas_call(
        in_grad_kernel,
        grid=(frames // block,),
        in_specs=lead + [frame_spec] + tail + [ANYWHERE] * len(after),
        out_specs=grad_specs,
        out_shape=grad_shapes,
        scratch_shapes=scratch
        + [pltpu.VMEM((3, p, 3 * c), F32), pltpu.VMEM((2 * lines, columns), F32)],
        compiler_params=params(),
        cost_estimate=estimate,
        name="in_grad",
    )(places, ends, pair, local, product, decays, x, up, down, *after)


def outputs_kernel(low_ref, up_ref, down_ref, w_ref, x_ref, skip_ref, after_ref, out_ref, token_ref, s_ref):
    token_ref[...] = jnp.zeros_like(token_ref)
    rows, frames, width, p = low_ref.shape
    s_ref[0] = shifted(flat(up_ref[...]), width)
    for r in range(rows):
        s_ref[r + 1] = shifted(flat(low_ref[r]), width)
    s_ref[rows + 1] = shifted(flat(down_ref[...]), width)
    lhs = jnp.concatenate([flat(s_ref[i : i + rows]) for i in range(3)], axis=1)
    mixed = dot(lhs, flat(w_ref[...])).reshape(rows, frames, width, -1)
    skip = skip_ref[...][0:1].reshape(1, 1, -1)
    for r in range(rows):
        out_ref[:, r] = (mixed[r] + skip * x_ref[:, r].astype(F32)).astype(BF16)


def outputs_conv(low, up, down, taps, x, skip, block, after):
    rows, frames, width, p = low.shape
    c = x.shape[-1]
    halo_spec = pl.BlockSpec((block, width, p), lambda b: (b, 0, 0))
    x_spec = pl.BlockSpec((block, rows, width, c), lambda b: (b, 0, 0, 0))
    return pl.pallas_call(
        outputs_kernel,
        grid=(frames // block,),
        in_specs=[
            pl.BlockSpec((rows, block, width, p), lambda b: (0, b, 0, 0)),
            halo_spec,
            halo_spec,
            pl.BlockSpec(taps.shape, lambda b: (0, 0, 0)),
            x_spec,
            pl.BlockSpec((1, c), lambda b: (0, 0)),
            ANYWHERE,
        ],
        out_specs=[x_spec, TOKEN_SPEC],
        out_shape=[jax.ShapeDtypeStruct(x.shape, BF16), TOKEN],
        scratch_shapes=[pltpu.VMEM((rows + 2, block * width, 3 * p), BF16)],
        compiler_params=params(),
        cost_estimate=cost(2 * frames * rows * width * 9 * c * p, 8 * 2**20),
        name="outputs_conv",
    )(low, up, down, taps, x, skip, after)


def edge_rows_kernel(places_ref, *refs):
    first_ref, last_ref = refs[4:]
    for k in range(2):
        first_ref[k] = refs[2 * k][:, 0]
        last_ref[k] = refs[2 * k + 1][:, 0]


def edge_rows(places, x, cot, block):
    frames, rows, width, c = x.shape
    line = jax.ShapeDtypeStruct((2, frames, width, c), x.dtype)
    line_spec = pl.BlockSpec((2, block, width, c), lambda b: (0, b, 0, 0))
    first = pl.BlockSpec((block, 1, width, c), lambda b: (b, 0, 0, 0))
    last = pl.BlockSpec((block, 1, width, c), lambda b: (b, rows - 1, 0, 0))
    return pl.pallas_call(
        edge_rows_kernel,
        grid=(frames // block,),
        in_specs=[SCALARS, first, last, first, last],
        out_specs=[line_spec, line_spec],
        out_shape=[line, line],
        compiler_params=params(56),
        cost_estimate=cost(0, 2**22),
        name="edge_rows",
    )(places, x, x, cot, cot)


def row_halo(first, last):
    axes = ("y", "core")
    count = lax.axis_size("y") * lax.axis_size("core")
    up = lax.ppermute(last, axes, [(i, i + 1) for i in range(count - 1)])
    down = lax.ppermute(first, axes, [(i + 1, i) for i in range(count - 1)])
    return up, down


CORES = [(0, 1), (1, 0)]
FAR = 64


def small_call(body, name, out_shapes, operands, after, places=None, mib=2):
    extra = [] if places is None else [places]

    def kernel(*refs):
        body(*refs[len(after) : -1])
        refs[-1][...] = jnp.zeros_like(refs[-1])

    whole = pl.BlockSpec(memory_space=pltpu.VMEM)
    return pl.pallas_call(
        kernel,
        in_specs=[ANYWHERE] * len(after) + [SCALARS] * len(extra) + [whole] * len(operands),
        out_specs=[whole] * (len(out_shapes) + 1),
        out_shape=[jax.ShapeDtypeStruct(*shape) for shape in out_shapes] + [TOKEN],
        compiler_params=pltpu.CompilerParams(vmem_limit_bytes=10 * 2**20),
        cost_estimate=cost(mib * 2**29, 2**21),
        name=name,
    )(*after, *extra, *operands)


def quarter(index, ref):
    size = ref.shape[0] // 4
    return pl.ds(pl.multiple_of(index * size, 16), size)


def add_kernel(places_ref, kept_ref, got_ref, own_ref, *sent_refs):
    for k, ref in enumerate((own_ref,) + sent_refs):
        at = quarter(jnp.bitwise_xor(places_ref[3], k), kept_ref)
        ref[...] = (kept_ref[at] + got_ref[at].astype(F32)).astype(ref.dtype)


def tree(terms):
    while len(terms) > 1:
        terms = [terms[k] + terms[k + 1] for k in range(0, len(terms), 2)]
    return terms[0]


def sum_kernel(scale, *refs):
    total = tree([ref[...].astype(F32) for ref in refs[:-1]])
    if scale is not None:
        total = total * scale
    refs[-1][...] = total.astype(BF16)


def pack_kernel(*refs):
    for k, ref in enumerate(refs[:-1]):
        refs[-1][k] = ref[...]


def merge_kernel(places_ref, own_ref, other_ref, out_ref):
    count, lines, _ = own_ref.shape
    for side, ref in enumerate((own_ref, other_ref)):
        for k in range(count):
            index = jnp.bitwise_xor(places_ref[2], side) * count
            index = index + jnp.bitwise_xor(places_ref[3], k)
            at = pl.ds(pl.multiple_of(index * lines, 16), lines)
            out_ref[at] = ref[k].astype(F32)


def from_others(sent, axes):
    count = math.prod(lax.axis_size(name) for name in axes)
    if not isinstance(sent, list):
        sent = [sent] * (count - 1)
    return [
        lax.ppermute(part, axes, [(i, i ^ k) for i in range(count)])
        for k, part in enumerate(sent, 1)
    ]


def per_device(inputs, decays, in_kernel, out_kernel, skip, cotangent):
    clips, frames, rows, width, c = inputs.shape
    p = in_kernel.shape[3]
    block = 16
    devices = math.prod(lax.axis_size(name) for name in ("a", "x", "y", "core"))
    grad_scale = 1.0 / math.sqrt(clips * frames * rows * width * devices)
    x = inputs.reshape(frames, rows, width, c)
    cot = cotangent.reshape(frames, rows, width, c)
    places = jnp.stack([lax.axis_index(name) for name in ("a", "x", "core", ("x", "y"))])
    places = places.astype(jnp.int32)
    deep = lax.axis_size("a")
    lines = rows * width

    up, down = row_halo(*edge_rows(places, x, cot, block))
    x_part, x_taps = interior_conv(x, in_kernel, False, block)
    cot_part, cot_taps = interior_conv(cot, out_kernel, True, block)
    states, running, end = local_scan(x_part, up, down, 0, x_taps, decays, block, False, decays)
    adjoint, trailing, message = local_scan(
        cot_part, up, down, 1, cot_taps, decays, block, True, end
    )
    pair = lax.ppermute(message, "x", [(0, 1), (1, 0)])
    ends, token = small_call(
        pair_kernel, "pair", [((deep, lines + 8, p), F32)], [message, pair], [], places
    )
    ends = lax.all_to_all(ends, "a", 0, 0)

    low, low_first, low_last, sent, kept, token = kernel_grads(
        places, ends, pair, states, running, cot, up, down, 1, None, block
    )
    got = lax.ppermute(sent, "core", CORES)
    low_up, low_down = row_halo(low_first, low_last)
    half, q = kept.shape
    part_shape = (half // 4, q)

    def add(name, kept, got, after):
        shapes = [(part_shape, F32)] + [(part_shape, BF16)] * 3
        own, *sent, token = small_call(add_kernel, name, shapes, [kept, got], after, places)
        return own, from_others(sent, ("x", "y")), token

    def sums(name, scale, terms, after, mib=2):
        body = functools.partial(sum_kernel, scale)
        return small_call(body, name, [(part_shape, BF16)], terms, after, None, mib)

    def swapped(part, bit):
        return lax.ppermute(part, "a", [(i, i ^ bit) for i in range(deep)])

    bits = [2**k for k in range(deep.bit_length() - 1)]

    def middle(name, part, other, after, mib=2):
        for bit in bits[1:]:
            part, token = sums(name, None, [part, other], after, mib)
            other, after = swapped(part, bit), [token]
        return part, other, after[0]

    def pack(name, terms, after, mib=2):
        shape = (4,) + part_shape
        packed, token = small_call(pack_kernel, name, [(shape, BF16)], terms, after, None, mib)
        return packed, lax.ppermute(packed, "core", CORES), token

    def merge(name, packed, other, after, mib=2):
        shapes = [((2 * half, q), F32)]
        return small_call(merge_kernel, name, shapes, [packed, other], after, places, mib)

    own, others, token = add("out_add", kept, got, [token])
    sent, kept, token = kernel_grads(
        places, ends, pair, adjoint, trailing, x, up, down, 0, decays, block, [token]
    )
    got = lax.ppermute(sent, "core", CORES)
    out_part, token = sums("out_share", None, [own] + others, [token, low_up, low_down], mib=FAR)
    out_other = swapped(out_part, 1)
    own, others, token = add("in_add", kept, got, [token])
    out_part, out_other, token = middle("out_mid", out_part, out_other, [token], FAR)
    in_part, token = sums("in_share", None, [own] + others, [token])
    in_other = swapped(in_part, 1)
    out_part, token = sums("out_total", grad_scale, [out_part, out_other], [token], mib=FAR)
    out_others = from_others(out_part, ("x", "y"))
    in_part, in_other, token = middle("in_mid", in_part, in_other, [token])
    outputs, token = outputs_conv(
        low, low_up, low_down, out_kernel.reshape(3, 3 * p, c), x, skip.reshape(1, c), block, token
    )
    in_part, token = sums("in_total", grad_scale, [in_part, in_other], [token])
    in_others = from_others(in_part, ("x", "y"))
    out_packed, out_other, token = pack("out_pack", [out_part] + out_others, [token])
    out_grad, token = merge("out_merge", out_packed, out_other, [token], FAR)
    in_packed, in_other, token = pack("in_pack", [in_part] + in_others, [token])
    in_grad, _ = merge("in_merge", in_packed, in_other, [token])
    return (
        outputs.reshape(inputs.shape),
        in_grad.reshape(in_kernel.shape),
        out_grad.reshape(out_kernel.shape),
    )


def solution(mesh):
    frames = mesh.shape["tm"]
    rows = mesh.shape["row"]
    fine = jax.sharding.Mesh(
        mesh.devices.reshape(frames // 2, 2, rows // 2, 2), ("a", "x", "y", "core")
    )
    cells = P(None, ("a", "x"), ("y", "core"), None, None)
    return jax.shard_map(
        per_device,
        mesh=fine,
        in_specs=(cells, P(("a", "x"), None), P(), P(), P(), cells),
        out_specs=(cells, P(), P()),
        check_vma=False,
    )
```

```python
import functools
import math

import jax
import jax.numpy as jnp
from jax import lax
from jax.experimental import pallas as pl
from jax.experimental.pallas import tpu as pltpu
from jax.sharding import PartitionSpec as P

BF16 = jnp.bfloat16
F32 = jnp.float32


SCALARS = pl.BlockSpec(memory_space=pltpu.SMEM)
ANYWHERE = pl.BlockSpec(memory_space=pl.ANY)
TOKEN = jax.ShapeDtypeStruct((8, 128), F32)
TOKEN_SPEC = pl.BlockSpec((8, 128), lambda *b: (0, 0))


def params(mib=30):
    return pltpu.CompilerParams(
        dimension_semantics=("arbitrary",), vmem_limit_bytes=mib * 1024 * 1024
    )


def cost(flops, nbytes):
    return pl.CostEstimate(flops=int(flops), bytes_accessed=int(nbytes), transcendentals=0)


def shifted(cells, width):
    count = cells.shape[0]
    wide = cells.astype(F32)
    column = lax.broadcasted_iota(jnp.int32, (count, 1), 0) % width
    left = jnp.where(column == 0, 0.0, pltpu.roll(wide, 1, 0))
    right = jnp.where(column == width - 1, 0.0, pltpu.roll(wide, count - 1, 0))
    return jnp.concatenate([left.astype(BF16), cells, right.astype(BF16)], axis=1)


def flat(block):
    return block.reshape(-1, block.shape[-1])


def dot(a, b):
    return jnp.dot(a, b, preferred_element_type=F32)


def interior_body(x_ref, w_ref, out_ref, s_ref):
    frames, rows, width, _ = x_ref.shape
    lines = frames * width
    for r in range(rows):
        s_ref[r] = shifted(flat(x_ref[:, r]), width)

    def conv(first, count, taps):
        lhs = jnp.concatenate(
            [flat(s_ref[first + i - 1 : first + i - 1 + count]) for i in taps], axis=1
        )
        rhs = w_ref[taps[0] : taps[-1] + 1].reshape(len(taps) * w_ref.shape[1], w_ref.shape[2])
        out_ref[first : first + count] = dot(lhs, rhs).reshape(count, frames, width, -1)

    conv(1, rows - 2, (0, 1, 2))
    conv(0, 1, (1, 2))
    conv(rows - 1, 1, (0, 1))


def interior_plain_kernel(x_ref, w_ref, out_ref, s_ref):
    interior_body(x_ref, w_ref, out_ref, s_ref)


def interior_flipped_kernel(x_ref, w_ref, out_ref, wt_ref, s_ref):
    @pl.when(pl.program_id(0) == 0)
    def _():
        for i in range(3):
            for j in range(3):
                c = w_ref.shape[3]
                wt_ref[i, j * c : (j + 1) * c, :] = w_ref[2 - i, 2 - j].T

    interior_body(x_ref, wt_ref, out_ref, s_ref)


def interior_conv(x, w, flipped, block):
    frames, rows, width, c = x.shape
    p = w.shape[2] if flipped else w.shape[3]
    part_shape = jax.ShapeDtypeStruct((rows, frames, width, p), F32)
    part_spec = pl.BlockSpec((rows, block, width, p), lambda b: (0, b, 0, 0))
    x_spec = pl.BlockSpec((block, rows, width, c), lambda b: (b, 0, 0, 0))
    scratch = [pltpu.VMEM((rows, block * width, 3 * c), BF16)]
    estimate = cost(2 * frames * rows * width * 9 * c * p, 8 * 2**20)
    taps_spec = pl.BlockSpec((3, 3 * c, p), lambda b: (0, 0, 0))
    if flipped:
        return pl.pallas_call(
            interior_flipped_kernel,
            grid=(frames // block,),
            in_specs=[
                x_spec,
                pl.BlockSpec(w.shape, lambda b: (0, 0, 0, 0)),
            ],
            out_specs=[part_spec, taps_spec],
            out_shape=[part_shape, jax.ShapeDtypeStruct((3, 3 * c, p), BF16)],
            scratch_shapes=scratch,
            compiler_params=params(),
            cost_estimate=estimate,
            name="interior_cot",
        )(x, w)
    taps = w.reshape(3, 3 * c, p)
    part = pl.pallas_call(
        interior_plain_kernel,
        grid=(frames // block,),
        in_specs=[x_spec, taps_spec],
        out_specs=part_spec,
        out_shape=part_shape,
        scratch_shapes=scratch,
        compiler_params=params(),
        cost_estimate=estimate,
        name="interior_in",
    )(x, taps)
    return part, taps


def scan_kernel(backward, part_ref, up_ref, down_ref, w_ref, decay_ref, before_ref, local_ref, product_ref, end_ref, carry_ref, run_ref):
    rows, frames, width, p = part_ref.shape
    lines = rows * width

    @pl.when(pl.program_id(0) == 0)
    def _():
        carry_ref[...] = jnp.zeros_like(carry_ref)
        run_ref[...] = jnp.ones_like(run_ref)

    top = dot(shifted(flat(up_ref[...]), width), w_ref[0]).reshape(frames, width, p)
    low = dot(shifted(flat(down_ref[...]), width), w_ref[2]).reshape(frames, width, p)
    decay = decay_ref[...]
    scale = jnp.sqrt((1.0 - decay) * (1.0 + decay))
    state = [carry_ref[r * width : (r + 1) * width] for r in range(rows)]
    run = run_ref[0:1]
    for step in range(frames):
        t = frames - 1 - step if backward else step
        factor = decay[t : t + 1]
        gain = scale[t : t + 1]
        if backward:
            product_ref[t : t + 1] = run
        run = run * factor
        if not backward:
            product_ref[t : t + 1] = run
        for r in range(rows):
            term = part_ref[r, t]
            if r == 0:
                term = term + top[t]
            if r == rows - 1:
                term = term + low[t]
            if backward:
                full = term + state[r]
                local_ref[r, t] = full
                state[r] = factor * full
            else:
                state[r] = factor * state[r] + gain * term
                local_ref[r, t] = state[r]
    for r in range(rows):
        carry_ref[r * width : (r + 1) * width] = state[r]
    run_ref[...] = jnp.broadcast_to(run, run_ref.shape)

    @pl.when(pl.program_id(0) == pl.num_programs(0) - 1)
    def _():
        if backward:
            message = [before_ref[...]] + state + [jnp.broadcast_to(run, (8, p))]
        else:
            message = state
        end_ref[...] = jnp.concatenate(message, axis=0)


def local_scan(part, up, down, half, taps, decays, block, backward, before):
    rows, frames, width, p = part.shape
    c = up.shape[-1]
    blocks = frames // block
    at = (lambda b: blocks - 1 - b) if backward else (lambda b: b)
    halo_spec = pl.BlockSpec((None, block, width, c), lambda b: (half, at(b), 0, 0))
    part_spec = pl.BlockSpec((rows, block, width, p), lambda b: (0, at(b), 0, 0))
    frame_spec = pl.BlockSpec((block, p), lambda b: (at(b), 0))
    lines = rows * width
    message = 2 * lines + 8 if backward else lines
    return pl.pallas_call(
        functools.partial(scan_kernel, backward),
        grid=(blocks,),
        in_specs=[
            part_spec,
            halo_spec,
            halo_spec,
            pl.BlockSpec(taps.shape, lambda b: (0, 0, 0)),
            frame_spec,
            pl.BlockSpec(before.shape, lambda b: (0, 0)),
        ],
        out_specs=[part_spec, frame_spec, pl.BlockSpec((message, p), lambda b: (0, 0))],
        out_shape=[
            jax.ShapeDtypeStruct(part.shape, F32),
            jax.ShapeDtypeStruct((frames, p), F32),
            jax.ShapeDtypeStruct((message, p), F32),
        ],
        scratch_shapes=[pltpu.VMEM((lines, p), F32), pltpu.VMEM((8, p), F32)],
        compiler_params=params(),
        cost_estimate=cost(4 * frames * width * 3 * c * p, 12 * 2**20),
        name="scan_back" if backward else "scan_fwd",
    )(part, up, down, taps, decays, before)


def pair_kernel(places_ref, own_ref, got_ref, out_ref):
    deep, height, _ = out_ref.shape
    lines = height - 8
    first = places_ref[1] == 0
    own_end, got_end = own_ref[0:lines], got_ref[0:lines]
    own_start, got_start = own_ref[lines : 2 * lines], got_ref[lines : 2 * lines]
    own_product, got_product = own_ref[2 * lines :], got_ref[2 * lines :]
    end = jnp.where(
        first, got_product[0:1] * own_end + got_end, own_product[0:1] * got_end + own_end
    )
    start = jnp.where(
        first, own_product[0:1] * got_start + own_start, got_product[0:1] * own_start + got_start
    )
    product = own_product * got_product
    for k in range(deep):
        out_ref[k, 0:lines] = jnp.where(k > places_ref[0], end, start)
        out_ref[k, lines:] = product


def combine(places_ref, ends_ref, pair_ref, total_ref, backward):
    place = places_ref[0]
    count = ends_ref.shape[0]
    lines = total_ref.shape[0]
    total = jnp.zeros(total_ref.shape, F32)
    order = range(count - 1, -1, -1) if backward else range(count)
    for k in order:
        passed = ends_ref[k, lines : lines + 1] * total + ends_ref[k, 0:lines]
        total = jnp.where(k > place if backward else k < place, passed, total)
    near = pair_ref[lines : 2 * lines] if backward else pair_ref[0:lines]
    passed = pair_ref[2 * lines : 2 * lines + 1] * total + near
    total_ref[...] = jnp.where(places_ref[1] == (0 if backward else 1), passed, total)


def split_halves(place_ref, sum_ref, sent_ref, kept_ref):
    half = kept_ref.shape[0]
    side = place_ref[2]
    sent_ref[...] = sum_ref[pl.ds(pl.multiple_of((1 - side) * half, 8), half)].astype(BF16)
    kept_ref[...] = sum_ref[pl.ds(pl.multiple_of(side * half, 8), half)]


def fill_rim(s_ref, up_ref, x_ref, down_ref):
    _, rows, width, _ = x_ref.shape
    s_ref[0] = shifted(flat(up_ref[...]), width)
    for r in range(rows):
        s_ref[r + 1] = shifted(flat(x_ref[:, r]), width)
    s_ref[rows + 1] = shifted(flat(down_ref[...]), width)


def out_grad_kernel(place_ref, ends_ref, pair_ref, local_ref, product_ref, cot_ref, up_ref, down_ref, low_ref, first_ref, last_ref, sent_ref, kept_ref, token_ref, s_ref, total_ref, sum_ref):
    rows, frames, width, p = local_ref.shape
    c = cot_ref.shape[-1]

    @pl.when(pl.program_id(0) == 0)
    def _():
        combine(place_ref, ends_ref, pair_ref, total_ref, False)
        sum_ref[...] = jnp.zeros_like(sum_ref)
        token_ref[...] = jnp.zeros_like(token_ref)

    fill_rim(s_ref, up_ref, cot_ref, down_ref)
    product = product_ref[...]
    turned = []
    for r in range(rows):
        state = local_ref[r] + product[:, None, :] * total_ref[r * width : (r + 1) * width][None]
        low = state.astype(BF16)
        low_ref[r] = low
        if r == 0:
            first_ref[...] = low
        if r == rows - 1:
            last_ref[...] = low
        turned.append(flat(low).T)
    turned = jnp.concatenate(turned, axis=1)
    for i in range(3):
        gain = dot(turned, flat(s_ref[2 - i : 2 - i + rows]))
        for j in range(3):
            tap = 3 * i + j
            sum_ref[tap * p : (tap + 1) * p] += gain[:, (2 - j) * c : (3 - j) * c]

    @pl.when(pl.program_id(0) == pl.num_programs(0) - 1)
    def _():
        split_halves(place_ref, sum_ref, sent_ref, kept_ref)


def in_grad_kernel(place_ref, ends_ref, pair_ref, local_ref, product_ref, decay_ref, x_ref, up_ref, down_ref, *refs):
    sent_ref, kept_ref, token_ref, s_ref, total_ref, sum_ref, flat_ref = refs[-7:]
    rows, frames, width, p = local_ref.shape
    c = x_ref.shape[-1]

    @pl.when(pl.program_id(0) == 0)
    def _():
        combine(place_ref, ends_ref, pair_ref, total_ref, True)
        sum_ref[...] = jnp.zeros_like(sum_ref)
        token_ref[...] = jnp.zeros_like(token_ref)

    fill_rim(s_ref, up_ref, x_ref, down_ref)
    product = product_ref[...]
    decay = decay_ref[...]
    scale = jnp.sqrt((1.0 - decay) * (1.0 + decay))[:, None, :]
    turned = []
    for r in range(rows):
        adjoint = local_ref[r] + product[:, None, :] * total_ref[r * width : (r + 1) * width][None]
        turned.append(flat((scale * adjoint).astype(BF16)).T)
    turned = jnp.concatenate(turned, axis=1)
    for i in range(3):
        sum_ref[i] += dot(turned, flat(s_ref[i : i + rows]))

    @pl.when(pl.program_id(0) == pl.num_programs(0) - 1)
    def _():
        for i in range(3):
            for j in range(3):
                tap = 3 * i + j
                flat_ref[tap * c : (tap + 1) * c] = sum_ref[i, :, j * c : (j + 1) * c].T
        split_halves(place_ref, flat_ref, sent_ref, kept_ref)


def kernel_grads(places, ends, pair, local, product, x, up, down, half, decays, block, after=None):
    rows, frames, width, p = local.shape
    c = x.shape[-1]
    halo_spec = pl.BlockSpec((None, block, width, c), lambda b: (half, b, 0, 0))
    local_spec = pl.BlockSpec((rows, block, width, p), lambda b: (0, b, 0, 0))
    frame_spec = pl.BlockSpec((block, p), lambda b: (b, 0))
    x_spec = pl.BlockSpec((block, rows, width, c), lambda b: (b, 0, 0, 0))
    lead = [
        SCALARS,
        pl.BlockSpec(ends.shape, lambda b: (0, 0, 0)),
        pl.BlockSpec(pair.shape, lambda b: (0, 0)),
        local_spec,
        frame_spec,
    ]
    tail = [x_spec, halo_spec, halo_spec]
    scratch = [
        pltpu.VMEM((rows + 2, block * width, 3 * c), BF16),
        pltpu.VMEM((rows * width, p), F32),
    ]
    estimate = cost(2 * frames * rows * width * 9 * c * p, 10 * 2**20)
    forward = decays is None
    lines, columns = (9 * p // 2, c) if forward else (9 * c // 2, p)
    grad_specs = [pl.BlockSpec((lines, columns), lambda b: (0, 0))] * 2 + [TOKEN_SPEC]
    grad_shapes = [
        jax.ShapeDtypeStruct((lines, columns), BF16),
        jax.ShapeDtypeStruct((lines, columns), F32),
        TOKEN,
    ]
    if forward:
        line_spec = pl.BlockSpec((block, width, p), lambda b: (b, 0, 0))
        line = jax.ShapeDtypeStruct((frames, width, p), BF16)
        return pl.pallas_call(
            out_grad_kernel,
            grid=(frames // block,),
            in_specs=lead + tail,
            out_specs=[local_spec, line_spec, line_spec] + grad_specs,
            out_shape=[jax.ShapeDtypeStruct(local.shape, BF16), line, line] + grad_shapes,
            scratch_shapes=scratch + [pltpu.VMEM((2 * lines, columns), F32)],
            compiler_params=params(),
            cost_estimate=estimate,
            name="out_grad",
        )(places, ends, pair, local, product, x, up, down)
    return pl.pallas_call(
        in_grad_kernel,
        grid=(frames // block,),
        in_specs=lead + [frame_spec] + tail + [ANYWHERE] * len(after),
        out_specs=grad_specs,
        out_shape=grad_shapes,
        scratch_shapes=scratch
        + [pltpu.VMEM((3, p, 3 * c), F32), pltpu.VMEM((2 * lines, columns), F32)],
        compiler_params=params(),
        cost_estimate=estimate,
        name="in_grad",
    )(places, ends, pair, local, product, decays, x, up, down, *after)


def outputs_kernel(low_ref, up_ref, down_ref, w_ref, x_ref, skip_ref, after_ref, out_ref, token_ref, s_ref):
    token_ref[...] = jnp.zeros_like(token_ref)
    rows, frames, width, p = low_ref.shape
    s_ref[0] = shifted(flat(up_ref[...]), width)
    for r in range(rows):
        s_ref[r + 1] = shifted(flat(low_ref[r]), width)
    s_ref[rows + 1] = shifted(flat(down_ref[...]), width)
    lhs = jnp.concatenate([flat(s_ref[i : i + rows]) for i in range(3)], axis=1)
    mixed = dot(lhs, flat(w_ref[...])).reshape(rows, frames, width, -1)
    skip = skip_ref[...][0:1].reshape(1, 1, -1)
    for r in range(rows):
        out_ref[:, r] = (mixed[r] + skip * x_ref[:, r].astype(F32)).astype(BF16)


def outputs_conv(low, up, down, taps, x, skip, block, after):
    rows, frames, width, p = low.shape
    c = x.shape[-1]
    halo_spec = pl.BlockSpec((block, width, p), lambda b: (b, 0, 0))
    x_spec = pl.BlockSpec((block, rows, width, c), lambda b: (b, 0, 0, 0))
    return pl.pallas_call(
        outputs_kernel,
        grid=(frames // block,),
        in_specs=[
            pl.BlockSpec((rows, block, width, p), lambda b: (0, b, 0, 0)),
            halo_spec,
            halo_spec,
            pl.BlockSpec(taps.shape, lambda b: (0, 0, 0)),
            x_spec,
            pl.BlockSpec((1, c), lambda b: (0, 0)),
            ANYWHERE,
        ],
        out_specs=[x_spec, TOKEN_SPEC],
        out_shape=[jax.ShapeDtypeStruct(x.shape, BF16), TOKEN],
        scratch_shapes=[pltpu.VMEM((rows + 2, block * width, 3 * p), BF16)],
        compiler_params=params(),
        cost_estimate=cost(2 * frames * rows * width * 9 * c * p, 8 * 2**20),
        name="outputs_conv",
    )(low, up, down, taps, x, skip, after)


def edge_rows_kernel(places_ref, *refs):
    first_ref, last_ref = refs[4:]
    for k in range(2):
        first_ref[k] = refs[2 * k][:, 0]
        last_ref[k] = refs[2 * k + 1][:, 0]


def edge_rows(places, x, cot, block):
    frames, rows, width, c = x.shape
    line = jax.ShapeDtypeStruct((2, frames, width, c), x.dtype)
    line_spec = pl.BlockSpec((2, block, width, c), lambda b: (0, b, 0, 0))
    first = pl.BlockSpec((block, 1, width, c), lambda b: (b, 0, 0, 0))
    last = pl.BlockSpec((block, 1, width, c), lambda b: (b, rows - 1, 0, 0))
    return pl.pallas_call(
        edge_rows_kernel,
        grid=(frames // block,),
        in_specs=[SCALARS, first, last, first, last],
        out_specs=[line_spec, line_spec],
        out_shape=[line, line],
        compiler_params=params(56),
        cost_estimate=cost(0, 2**22),
        name="edge_rows",
    )(places, x, x, cot, cot)


def row_halo(first, last):
    axes = ("y", "core")
    count = lax.axis_size("y") * lax.axis_size("core")
    up = lax.ppermute(last, axes, [(i, i + 1) for i in range(count - 1)])
    down = lax.ppermute(first, axes, [(i + 1, i) for i in range(count - 1)])
    return up, down


CORES = [(0, 1), (1, 0)]
FAR = 64


def small_call(body, name, out_shapes, operands, after, places=None, mib=2):
    extra = [] if places is None else [places]

    def kernel(*refs):
        body(*refs[len(after) : -1])
        refs[-1][...] = jnp.zeros_like(refs[-1])

    whole = pl.BlockSpec(memory_space=pltpu.VMEM)
    return pl.pallas_call(
        kernel,
        in_specs=[ANYWHERE] * len(after) + [SCALARS] * len(extra) + [whole] * len(operands),
        out_specs=[whole] * (len(out_shapes) + 1),
        out_shape=[jax.ShapeDtypeStruct(*shape) for shape in out_shapes] + [TOKEN],
        compiler_params=pltpu.CompilerParams(vmem_limit_bytes=10 * 2**20),
        cost_estimate=cost(mib * 2**29, 2**21),
        name=name,
    )(*after, *extra, *operands)


def quarter(index, ref):
    size = ref.shape[0] // 4
    return pl.ds(pl.multiple_of(index * size, 16), size)


def add_kernel(places_ref, kept_ref, got_ref, own_ref, *sent_refs):
    for k, ref in enumerate((own_ref,) + sent_refs):
        at = quarter(jnp.bitwise_xor(places_ref[3], k), kept_ref)
        ref[...] = (kept_ref[at] + got_ref[at].astype(F32)).astype(ref.dtype)


def tree(terms):
    while len(terms) > 1:
        terms = [terms[k] + terms[k + 1] for k in range(0, len(terms), 2)]
    return terms[0]


def sum_kernel(scale, *refs):
    total = tree([ref[...].astype(F32) for ref in refs[:-1]])
    if scale is not None:
        total = total * scale
    refs[-1][...] = total.astype(BF16)


def pack_kernel(*refs):
    for k, ref in enumerate(refs[:-1]):
        refs[-1][k] = ref[...]


def merge_kernel(places_ref, own_ref, other_ref, out_ref):
    count, lines, _ = own_ref.shape
    for side, ref in enumerate((own_ref, other_ref)):
        for k in range(count):
            index = jnp.bitwise_xor(places_ref[2], side) * count
            index = index + jnp.bitwise_xor(places_ref[3], k)
            at = pl.ds(pl.multiple_of(index * lines, 16), lines)
            out_ref[at] = ref[k].astype(F32)


def from_others(sent, axes):
    count = math.prod(lax.axis_size(name) for name in axes)
    if not isinstance(sent, list):
        sent = [sent] * (count - 1)
    return [
        lax.ppermute(part, axes, [(i, i ^ k) for i in range(count)])
        for k, part in enumerate(sent, 1)
    ]


def per_device(inputs, decays, in_kernel, out_kernel, skip, cotangent):
    clips, frames, rows, width, c = inputs.shape
    p = in_kernel.shape[3]
    block = 32
    devices = math.prod(lax.axis_size(name) for name in ("a", "x", "y", "core"))
    grad_scale = 1.0 / math.sqrt(clips * frames * rows * width * devices)
    x = inputs.reshape(frames, rows, width, c)
    cot = cotangent.reshape(frames, rows, width, c)
    places = jnp.stack([lax.axis_index(name) for name in ("a", "x", "core", ("x", "y"))])
    places = places.astype(jnp.int32)
    deep = lax.axis_size("a")
    lines = rows * width

    up, down = row_halo(*edge_rows(places, x, cot, block))
    x_part, x_taps = interior_conv(x, in_kernel, False, block)
    cot_part, cot_taps = interior_conv(cot, out_kernel, True, block)
    states, running, end = local_scan(x_part, up, down, 0, x_taps, decays, block, False, decays)
    adjoint, trailing, message = local_scan(
        cot_part, up, down, 1, cot_taps, decays, block, True, end
    )
    pair = lax.ppermute(message, "x", [(0, 1), (1, 0)])
    ends, token = small_call(
        pair_kernel, "pair", [((deep, lines + 8, p), F32)], [message, pair], [], places
    )
    ends = lax.all_to_all(ends, "a", 0, 0)

    low, low_first, low_last, sent, kept, token = kernel_grads(
        places, ends, pair, states, running, cot, up, down, 1, None, block
    )
    got = lax.ppermute(sent, "core", CORES)
    low_up, low_down = row_halo(low_first, low_last)
    half, q = kept.shape
    part_shape = (half // 4, q)

    def add(name, kept, got, after):
        shapes = [(part_shape, F32)] + [(part_shape, BF16)] * 3
        own, *sent, token = small_call(add_kernel, name, shapes, [kept, got], after, places)
        return own, from_others(sent, ("x", "y")), token

    def sums(name, scale, terms, after, mib=2):
        body = functools.partial(sum_kernel, scale)
        return small_call(body, name, [(part_shape, BF16)], terms, after, None, mib)

    def swapped(part, bit):
        return lax.ppermute(part, "a", [(i, i ^ bit) for i in range(deep)])

    bits = [2**k for k in range(deep.bit_length() - 1)]

    def middle(name, part, other, after, mib=2):
        for bit in bits[1:]:
            part, token = sums(name, None, [part, other], after, mib)
            other, after = swapped(part, bit), [token]
        return part, other, after[0]

    def pack(name, terms, after, mib=2):
        shape = (4,) + part_shape
        packed, token = small_call(pack_kernel, name, [(shape, BF16)], terms, after, None, mib)
        return packed, lax.ppermute(packed, "core", CORES), token

    def merge(name, packed, other, after, mib=2):
        shapes = [((2 * half, q), F32)]
        return small_call(merge_kernel, name, shapes, [packed, other], after, places, mib)

    own, others, token = add("out_add", kept, got, [token])
    sent, kept, token = kernel_grads(
        places, ends, pair, adjoint, trailing, x, up, down, 0, decays, block, [token]
    )
    got = lax.ppermute(sent, "core", CORES)
    out_part, token = sums("out_share", None, [own] + others, [token, low_up, low_down], mib=FAR)
    out_other = swapped(out_part, 1)
    own, others, token = add("in_add", kept, got, [token])
    out_part, out_other, token = middle("out_mid", out_part, out_other, [token], FAR)
    in_part, token = sums("in_share", None, [own] + others, [token])
    in_other = swapped(in_part, 1)
    out_part, token = sums("out_total", grad_scale, [out_part, out_other], [token], mib=FAR)
    out_others = from_others(out_part, ("x", "y"))
    in_part, in_other, token = middle("in_mid", in_part, in_other, [token])
    outputs, token = outputs_conv(
        low, low_up, low_down, out_kernel.reshape(3, 3 * p, c), x, skip.reshape(1, c), block, token
    )
    in_part, token = sums("in_total", grad_scale, [in_part, in_other], [token])
    in_others = from_others(in_part, ("x", "y"))
    out_packed, out_other, token = pack("out_pack", [out_part] + out_others, [token])
    out_grad, token = merge("out_merge", out_packed, out_other, [token], FAR)
    in_packed, in_other, token = pack("in_pack", [in_part] + in_others, [token])
    in_grad, _ = merge("in_merge", in_packed, in_other, [token])
    return (
        outputs.reshape(inputs.shape),
        in_grad.reshape(in_kernel.shape),
        out_grad.reshape(out_kernel.shape),
    )


def solution(mesh):
    frames = mesh.shape["tm"]
    rows = mesh.shape["row"]
    fine = jax.sharding.Mesh(
        mesh.devices.reshape(frames // 2, 2, rows // 2, 2), ("a", "x", "y", "core")
    )
    cells = P(None, ("a", "x"), ("y", "core"), None, None)
    return jax.shard_map(
        per_device,
        mesh=fine,
        in_specs=(cells, P(("a", "x"), None), P(), P(), P(), cells),
        out_specs=(cells, P(), P()),
        check_vma=False,
    )
```

```python
import functools
import math

import jax
import jax.numpy as jnp
from jax import lax
from jax.experimental import pallas as pl
from jax.experimental.pallas import tpu as pltpu
from jax.sharding import PartitionSpec as P

BF16 = jnp.bfloat16
F32 = jnp.float32


SCALARS = pl.BlockSpec(memory_space=pltpu.SMEM)
ANYWHERE = pl.BlockSpec(memory_space=pl.ANY)
TOKEN = jax.ShapeDtypeStruct((8, 128), F32)
TOKEN_SPEC = pl.BlockSpec((8, 128), lambda *b: (0, 0))


def params(mib=30):
    return pltpu.CompilerParams(
        dimension_semantics=("arbitrary",), vmem_limit_bytes=mib * 1024 * 1024
    )


def cost(flops, nbytes):
    return pl.CostEstimate(flops=int(flops), bytes_accessed=int(nbytes), transcendentals=0)


def shifted(cells, width):
    count = cells.shape[0]
    wide = cells.astype(F32)
    column = lax.broadcasted_iota(jnp.int32, (count, 1), 0) % width
    left = jnp.where(column == 0, 0.0, pltpu.roll(wide, 1, 0))
    right = jnp.where(column == width - 1, 0.0, pltpu.roll(wide, count - 1, 0))
    return jnp.concatenate([left.astype(BF16), cells, right.astype(BF16)], axis=1)


def flat(block):
    return block.reshape(-1, block.shape[-1])


def dot(a, b):
    return jnp.dot(a, b, preferred_element_type=F32)


def interior_body(x_ref, w_ref, out_ref, s_ref):
    frames, rows, width, _ = x_ref.shape
    lines = frames * width
    for r in range(rows):
        s_ref[r] = shifted(flat(x_ref[:, r]), width)

    def conv(first, count, taps):
        lhs = jnp.concatenate(
            [flat(s_ref[first + i - 1 : first + i - 1 + count]) for i in taps], axis=1
        )
        rhs = w_ref[taps[0] : taps[-1] + 1].reshape(len(taps) * w_ref.shape[1], w_ref.shape[2])
        out_ref[first : first + count] = dot(lhs, rhs).reshape(count, frames, width, -1)

    conv(1, rows - 2, (0, 1, 2))
    conv(0, 1, (1, 2))
    conv(rows - 1, 1, (0, 1))


def interior_plain_kernel(x_ref, w_ref, out_ref, s_ref):
    interior_body(x_ref, w_ref, out_ref, s_ref)


def interior_flipped_kernel(x_ref, w_ref, out_ref, wt_ref, s_ref):
    @pl.when(pl.program_id(0) == 0)
    def _():
        for i in range(3):
            for j in range(3):
                c = w_ref.shape[3]
                wt_ref[i, j * c : (j + 1) * c, :] = w_ref[2 - i, 2 - j].T

    interior_body(x_ref, wt_ref, out_ref, s_ref)


def interior_conv(x, w, flipped, block):
    frames, rows, width, c = x.shape
    p = w.shape[2] if flipped else w.shape[3]
    part_shape = jax.ShapeDtypeStruct((rows, frames, width, p), F32)
    part_spec = pl.BlockSpec((rows, block, width, p), lambda b: (0, b, 0, 0))
    x_spec = pl.BlockSpec((block, rows, width, c), lambda b: (b, 0, 0, 0))
    scratch = [pltpu.VMEM((rows, block * width, 3 * c), BF16)]
    estimate = cost(2 * frames * rows * width * 9 * c * p, 8 * 2**20)
    taps_spec = pl.BlockSpec((3, 3 * c, p), lambda b: (0, 0, 0))
    if flipped:
        return pl.pallas_call(
            interior_flipped_kernel,
            grid=(frames // block,),
            in_specs=[
                x_spec,
                pl.BlockSpec(w.shape, lambda b: (0, 0, 0, 0)),
            ],
            out_specs=[part_spec, taps_spec],
            out_shape=[part_shape, jax.ShapeDtypeStruct((3, 3 * c, p), BF16)],
            scratch_shapes=scratch,
            compiler_params=params(),
            cost_estimate=estimate,
            name="interior_cot",
        )(x, w)
    taps = w.reshape(3, 3 * c, p)
    part = pl.pallas_call(
        interior_plain_kernel,
        grid=(frames // block,),
        in_specs=[x_spec, taps_spec],
        out_specs=part_spec,
        out_shape=part_shape,
        scratch_shapes=scratch,
        compiler_params=params(),
        cost_estimate=estimate,
        name="interior_in",
    )(x, taps)
    return part, taps


def scan_kernel(backward, part_ref, up_ref, down_ref, w_ref, decay_ref, before_ref, local_ref, product_ref, end_ref, carry_ref, run_ref):
    rows, frames, width, p = part_ref.shape
    lines = rows * width

    @pl.when(pl.program_id(0) == 0)
    def _():
        carry_ref[...] = jnp.zeros_like(carry_ref)
        run_ref[...] = jnp.ones_like(run_ref)

    top = dot(shifted(flat(up_ref[...]), width), w_ref[0]).reshape(frames, width, p)
    low = dot(shifted(flat(down_ref[...]), width), w_ref[2]).reshape(frames, width, p)
    decay = decay_ref[...]
    scale = jnp.sqrt((1.0 - decay) * (1.0 + decay))
    state = [carry_ref[r * width : (r + 1) * width] for r in range(rows)]
    run = run_ref[0:1]
    for step in range(frames):
        t = frames - 1 - step if backward else step
        factor = decay[t : t + 1]
        gain = scale[t : t + 1]
        if backward:
            product_ref[t : t + 1] = run
        run = run * factor
        if not backward:
            product_ref[t : t + 1] = run
        for r in range(rows):
            term = part_ref[r, t]
            if r == 0:
                term = term + top[t]
            if r == rows - 1:
                term = term + low[t]
            if backward:
                full = term + state[r]
                local_ref[r, t] = full
                state[r] = factor * full
            else:
                state[r] = factor * state[r] + gain * term
                local_ref[r, t] = state[r]
    for r in range(rows):
        carry_ref[r * width : (r + 1) * width] = state[r]
    run_ref[...] = jnp.broadcast_to(run, run_ref.shape)

    @pl.when(pl.program_id(0) == pl.num_programs(0) - 1)
    def _():
        if backward:
            message = [before_ref[...]] + state + [jnp.broadcast_to(run, (8, p))]
        else:
            message = state
        end_ref[...] = jnp.concatenate(message, axis=0)


def local_scan(part, up, down, half, taps, decays, block, backward, before):
    rows, frames, width, p = part.shape
    c = up.shape[-1]
    blocks = frames // block
    at = (lambda b: blocks - 1 - b) if backward else (lambda b: b)
    halo_spec = pl.BlockSpec((None, block, width, c), lambda b: (half, at(b), 0, 0))
    part_spec = pl.BlockSpec((rows, block, width, p), lambda b: (0, at(b), 0, 0))
    frame_spec = pl.BlockSpec((block, p), lambda b: (at(b), 0))
    lines = rows * width
    message = 2 * lines + 8 if backward else lines
    return pl.pallas_call(
        functools.partial(scan_kernel, backward),
        grid=(blocks,),
        in_specs=[
            part_spec,
            halo_spec,
            halo_spec,
            pl.BlockSpec(taps.shape, lambda b: (0, 0, 0)),
            frame_spec,
            pl.BlockSpec(before.shape, lambda b: (0, 0)),
        ],
        out_specs=[part_spec, frame_spec, pl.BlockSpec((message, p), lambda b: (0, 0))],
        out_shape=[
            jax.ShapeDtypeStruct(part.shape, F32),
            jax.ShapeDtypeStruct((frames, p), F32),
            jax.ShapeDtypeStruct((message, p), F32),
        ],
        scratch_shapes=[pltpu.VMEM((lines, p), F32), pltpu.VMEM((8, p), F32)],
        compiler_params=params(),
        cost_estimate=cost(4 * frames * width * 3 * c * p, 12 * 2**20),
        name="scan_back" if backward else "scan_fwd",
    )(part, up, down, taps, decays, before)


def pair_kernel(places_ref, own_ref, got_ref, out_ref):
    deep, height, _ = out_ref.shape
    lines = height - 8
    first = places_ref[1] == 0
    own_end, got_end = own_ref[0:lines], got_ref[0:lines]
    own_start, got_start = own_ref[lines : 2 * lines], got_ref[lines : 2 * lines]
    own_product, got_product = own_ref[2 * lines :], got_ref[2 * lines :]
    end = jnp.where(
        first, got_product[0:1] * own_end + got_end, own_product[0:1] * got_end + own_end
    )
    start = jnp.where(
        first, own_product[0:1] * got_start + own_start, got_product[0:1] * own_start + got_start
    )
    product = own_product * got_product
    for k in range(deep):
        out_ref[k, 0:lines] = jnp.where(k > places_ref[0], end, start)
        out_ref[k, lines:] = product


def combine(places_ref, ends_ref, pair_ref, total_ref, backward):
    place = places_ref[0]
    count = ends_ref.shape[0]
    lines = total_ref.shape[0]
    total = jnp.zeros(total_ref.shape, F32)
    order = range(count - 1, -1, -1) if backward else range(count)
    for k in order:
        passed = ends_ref[k, lines : lines + 1] * total + ends_ref[k, 0:lines]
        total = jnp.where(k > place if backward else k < place, passed, total)
    near = pair_ref[lines : 2 * lines] if backward else pair_ref[0:lines]
    passed = pair_ref[2 * lines : 2 * lines + 1] * total + near
    total_ref[...] = jnp.where(places_ref[1] == (0 if backward else 1), passed, total)


def split_halves(place_ref, sum_ref, sent_ref, kept_ref):
    half = kept_ref.shape[0]
    side = place_ref[2]
    sent_ref[...] = sum_ref[pl.ds(pl.multiple_of((1 - side) * half, 8), half)].astype(BF16)
    kept_ref[...] = sum_ref[pl.ds(pl.multiple_of(side * half, 8), half)]


def fill_rim(s_ref, up_ref, x_ref, down_ref):
    _, rows, width, _ = x_ref.shape
    s_ref[0] = shifted(flat(up_ref[...]), width)
    for r in range(rows):
        s_ref[r + 1] = shifted(flat(x_ref[:, r]), width)
    s_ref[rows + 1] = shifted(flat(down_ref[...]), width)


def out_grad_kernel(place_ref, ends_ref, pair_ref, local_ref, product_ref, cot_ref, up_ref, down_ref, low_ref, first_ref, last_ref, sent_ref, kept_ref, token_ref, s_ref, total_ref, sum_ref):
    rows, frames, width, p = local_ref.shape
    c = cot_ref.shape[-1]

    @pl.when(pl.program_id(0) == 0)
    def _():
        combine(place_ref, ends_ref, pair_ref, total_ref, False)
        sum_ref[...] = jnp.zeros_like(sum_ref)
        token_ref[...] = jnp.zeros_like(token_ref)

    fill_rim(s_ref, up_ref, cot_ref, down_ref)
    product = product_ref[...]
    turned = []
    for r in range(rows):
        state = local_ref[r] + product[:, None, :] * total_ref[r * width : (r + 1) * width][None]
        low = state.astype(BF16)
        low_ref[r] = low
        if r == 0:
            first_ref[...] = low
        if r == rows - 1:
            last_ref[...] = low
        turned.append(flat(low).T)
    turned = jnp.concatenate(turned, axis=1)
    for i in range(3):
        gain = dot(turned, flat(s_ref[2 - i : 2 - i + rows]))
        for j in range(3):
            tap = 3 * i + j
            sum_ref[tap * p : (tap + 1) * p] += gain[:, (2 - j) * c : (3 - j) * c]

    @pl.when(pl.program_id(0) == pl.num_programs(0) - 1)
    def _():
        split_halves(place_ref, sum_ref, sent_ref, kept_ref)


def in_grad_kernel(place_ref, ends_ref, pair_ref, local_ref, product_ref, decay_ref, x_ref, up_ref, down_ref, *refs):
    sent_ref, kept_ref, token_ref, s_ref, total_ref, sum_ref, flat_ref = refs[-7:]
    rows, frames, width, p = local_ref.shape
    c = x_ref.shape[-1]

    @pl.when(pl.program_id(0) == 0)
    def _():
        combine(place_ref, ends_ref, pair_ref, total_ref, True)
        sum_ref[...] = jnp.zeros_like(sum_ref)
        token_ref[...] = jnp.zeros_like(token_ref)

    fill_rim(s_ref, up_ref, x_ref, down_ref)
    product = product_ref[...]
    decay = decay_ref[...]
    scale = jnp.sqrt((1.0 - decay) * (1.0 + decay))[:, None, :]
    turned = []
    for r in range(rows):
        adjoint = local_ref[r] + product[:, None, :] * total_ref[r * width : (r + 1) * width][None]
        turned.append(flat((scale * adjoint).astype(BF16)).T)
    turned = jnp.concatenate(turned, axis=1)
    for i in range(3):
        sum_ref[i] += dot(turned, flat(s_ref[i : i + rows]))

    @pl.when(pl.program_id(0) == pl.num_programs(0) - 1)
    def _():
        for i in range(3):
            for j in range(3):
                tap = 3 * i + j
                flat_ref[tap * c : (tap + 1) * c] = sum_ref[i, :, j * c : (j + 1) * c].T
        split_halves(place_ref, flat_ref, sent_ref, kept_ref)


def kernel_grads(places, ends, pair, local, product, x, up, down, half, decays, block, after=None):
    rows, frames, width, p = local.shape
    c = x.shape[-1]
    halo_spec = pl.BlockSpec((None, block, width, c), lambda b: (half, b, 0, 0))
    local_spec = pl.BlockSpec((rows, block, width, p), lambda b: (0, b, 0, 0))
    frame_spec = pl.BlockSpec((block, p), lambda b: (b, 0))
    x_spec = pl.BlockSpec((block, rows, width, c), lambda b: (b, 0, 0, 0))
    lead = [
        SCALARS,
        pl.BlockSpec(ends.shape, lambda b: (0, 0, 0)),
        pl.BlockSpec(pair.shape, lambda b: (0, 0)),
        local_spec,
        frame_spec,
    ]
    tail = [x_spec, halo_spec, halo_spec]
    scratch = [
        pltpu.VMEM((rows + 2, block * width, 3 * c), BF16),
        pltpu.VMEM((rows * width, p), F32),
    ]
    estimate = cost(2 * frames * rows * width * 9 * c * p, 10 * 2**20)
    forward = decays is None
    lines, columns = (9 * p // 2, c) if forward else (9 * c // 2, p)
    grad_specs = [pl.BlockSpec((lines, columns), lambda b: (0, 0))] * 2 + [TOKEN_SPEC]
    grad_shapes = [
        jax.ShapeDtypeStruct((lines, columns), BF16),
        jax.ShapeDtypeStruct((lines, columns), F32),
        TOKEN,
    ]
    if forward:
        line_spec = pl.BlockSpec((block, width, p), lambda b: (b, 0, 0))
        line = jax.ShapeDtypeStruct((frames, width, p), BF16)
        return pl.pallas_call(
            out_grad_kernel,
            grid=(frames // block,),
            in_specs=lead + tail,
            out_specs=[local_spec, line_spec, line_spec] + grad_specs,
            out_shape=[jax.ShapeDtypeStruct(local.shape, BF16), line, line] + grad_shapes,
            scratch_shapes=scratch + [pltpu.VMEM((2 * lines, columns), F32)],
            compiler_params=params(),
            cost_estimate=estimate,
            name="out_grad",
        )(places, ends, pair, local, product, x, up, down)
    return pl.pallas_call(
        in_grad_kernel,
        grid=(frames // block,),
        in_specs=lead + [frame_spec] + tail + [ANYWHERE] * len(after),
        out_specs=grad_specs,
        out_shape=grad_shapes,
        scratch_shapes=scratch
        + [pltpu.VMEM((3, p, 3 * c), F32), pltpu.VMEM((2 * lines, columns), F32)],
        compiler_params=params(),
        cost_estimate=estimate,
        name="in_grad",
    )(places, ends, pair, local, product, decays, x, up, down, *after)


def outputs_kernel(low_ref, up_ref, down_ref, w_ref, x_ref, skip_ref, after_ref, out_ref, token_ref, s_ref):
    token_ref[...] = jnp.zeros_like(token_ref)
    rows, frames, width, p = low_ref.shape
    s_ref[0] = shifted(flat(up_ref[...]), width)
    for r in range(rows):
        s_ref[r + 1] = shifted(flat(low_ref[r]), width)
    s_ref[rows + 1] = shifted(flat(down_ref[...]), width)
    lhs = jnp.concatenate([flat(s_ref[i : i + rows]) for i in range(3)], axis=1)
    mixed = dot(lhs, flat(w_ref[...])).reshape(rows, frames, width, -1)
    skip = skip_ref[...][0:1].reshape(1, 1, -1)
    for r in range(rows):
        out_ref[:, r] = (mixed[r] + skip * x_ref[:, r].astype(F32)).astype(BF16)


def outputs_conv(low, up, down, taps, x, skip, block, after):
    rows, frames, width, p = low.shape
    c = x.shape[-1]
    halo_spec = pl.BlockSpec((block, width, p), lambda b: (b, 0, 0))
    x_spec = pl.BlockSpec((block, rows, width, c), lambda b: (b, 0, 0, 0))
    return pl.pallas_call(
        outputs_kernel,
        grid=(frames // block,),
        in_specs=[
            pl.BlockSpec((rows, block, width, p), lambda b: (0, b, 0, 0)),
            halo_spec,
            halo_spec,
            pl.BlockSpec(taps.shape, lambda b: (0, 0, 0)),
            x_spec,
            pl.BlockSpec((1, c), lambda b: (0, 0)),
            ANYWHERE,
        ],
        out_specs=[x_spec, TOKEN_SPEC],
        out_shape=[jax.ShapeDtypeStruct(x.shape, BF16), TOKEN],
        scratch_shapes=[pltpu.VMEM((rows + 2, block * width, 3 * p), BF16)],
        compiler_params=params(),
        cost_estimate=cost(2 * frames * rows * width * 9 * c * p, 8 * 2**20),
        name="outputs_conv",
    )(low, up, down, taps, x, skip, after)


def edge_rows_kernel(places_ref, *refs):
    first_ref, last_ref = refs[4:]
    for k in range(2):
        first_ref[k] = refs[2 * k][:, 0]
        last_ref[k] = refs[2 * k + 1][:, 0]


def edge_rows(places, x, cot, block):
    frames, rows, width, c = x.shape
    line = jax.ShapeDtypeStruct((2, frames, width, c), x.dtype)
    line_spec = pl.BlockSpec((2, block, width, c), lambda b: (0, b, 0, 0))
    first = pl.BlockSpec((block, 1, width, c), lambda b: (b, 0, 0, 0))
    last = pl.BlockSpec((block, 1, width, c), lambda b: (b, rows - 1, 0, 0))
    return pl.pallas_call(
        edge_rows_kernel,
        grid=(frames // block,),
        in_specs=[SCALARS, first, last, first, last],
        out_specs=[line_spec, line_spec],
        out_shape=[line, line],
        compiler_params=params(56),
        cost_estimate=cost(0, 2**22),
        name="edge_rows",
    )(places, x, x, cot, cot)


def row_halo(first, last):
    axes = ("y", "core")
    count = lax.axis_size("y") * lax.axis_size("core")
    up = lax.ppermute(last, axes, [(i, i + 1) for i in range(count - 1)])
    down = lax.ppermute(first, axes, [(i + 1, i) for i in range(count - 1)])
    return up, down


CORES = [(0, 1), (1, 0)]
FAR = 64


def small_call(body, name, out_shapes, operands, after, places=None, mib=2):
    extra = [] if places is None else [places]

    def kernel(*refs):
        body(*refs[len(after) : -1])
        refs[-1][...] = jnp.zeros_like(refs[-1])

    whole = pl.BlockSpec(memory_space=pltpu.VMEM)
    return pl.pallas_call(
        kernel,
        in_specs=[ANYWHERE] * len(after) + [SCALARS] * len(extra) + [whole] * len(operands),
        out_specs=[whole] * (len(out_shapes) + 1),
        out_shape=[jax.ShapeDtypeStruct(*shape) for shape in out_shapes] + [TOKEN],
        compiler_params=pltpu.CompilerParams(vmem_limit_bytes=10 * 2**20),
        cost_estimate=cost(mib * 2**29, 2**21),
        name=name,
    )(*after, *extra, *operands)


def quarter(index, ref):
    size = ref.shape[0] // 4
    return pl.ds(pl.multiple_of(index * size, 16), size)


def add_kernel(places_ref, kept_ref, got_ref, own_ref, *sent_refs):
    for k, ref in enumerate((own_ref,) + sent_refs):
        at = quarter(jnp.bitwise_xor(places_ref[3], k), kept_ref)
        ref[...] = (kept_ref[at] + got_ref[at].astype(F32)).astype(ref.dtype)


def tree(terms):
    while len(terms) > 1:
        terms = [terms[k] + terms[k + 1] for k in range(0, len(terms), 2)]
    return terms[0]


def sum_kernel(scale, *refs):
    total = tree([ref[...].astype(F32) for ref in refs[:-1]])
    if scale is not None:
        total = total * scale
    refs[-1][...] = total.astype(BF16)


def copy_kernel(first_ref, last_ref, first_out_ref, last_out_ref):
    first_out_ref[...] = first_ref[...]
    last_out_ref[...] = last_ref[...]


def pack_kernel(*refs):
    for k, ref in enumerate(refs[:-1]):
        refs[-1][k] = ref[...]


def merge_kernel(places_ref, own_ref, other_ref, out_ref):
    count, lines, _ = own_ref.shape
    for side, ref in enumerate((own_ref, other_ref)):
        for k in range(count):
            index = jnp.bitwise_xor(places_ref[2], side) * count
            index = index + jnp.bitwise_xor(places_ref[3], k)
            at = pl.ds(pl.multiple_of(index * lines, 16), lines)
            out_ref[at] = ref[k].astype(F32)


def from_others(sent, axes):
    count = math.prod(lax.axis_size(name) for name in axes)
    if not isinstance(sent, list):
        sent = [sent] * (count - 1)
    return [
        lax.ppermute(part, axes, [(i, i ^ k) for i in range(count)])
        for k, part in enumerate(sent, 1)
    ]


def per_device(inputs, decays, in_kernel, out_kernel, skip, cotangent):
    clips, frames, rows, width, c = inputs.shape
    p = in_kernel.shape[3]
    block = 32
    devices = math.prod(lax.axis_size(name) for name in ("a", "x", "y", "core"))
    grad_scale = 1.0 / math.sqrt(clips * frames * rows * width * devices)
    x = inputs.reshape(frames, rows, width, c)
    cot = cotangent.reshape(frames, rows, width, c)
    places = jnp.stack([lax.axis_index(name) for name in ("a", "x", "core", ("x", "y"))])
    places = places.astype(jnp.int32)
    deep = lax.axis_size("a")
    lines = rows * width

    up, down = row_halo(*edge_rows(places, x, cot, frames))
    x_part, x_taps = interior_conv(x, in_kernel, False, block)
    cot_part, cot_taps = interior_conv(cot, out_kernel, True, block)
    states, running, end = local_scan(x_part, up, down, 0, x_taps, decays, block, False, decays)
    adjoint, trailing, message = local_scan(
        cot_part, up, down, 1, cot_taps, decays, block, True, end
    )
    pair = lax.ppermute(message, "x", [(0, 1), (1, 0)])
    ends, token = small_call(
        pair_kernel, "pair", [((deep, lines + 8, p), F32)], [message, pair], [], places
    )
    ends = lax.all_to_all(ends, "a", 0, 0)

    low, low_first, low_last, sent, kept, token = kernel_grads(
        places, ends, pair, states, running, cot, up, down, 1, None, block
    )
    got = lax.ppermute(sent, "core", CORES)
    half, q = kept.shape
    part_shape = (half // 4, q)

    def add(name, kept, got, after):
        shapes = [(part_shape, F32)] + [(part_shape, BF16)] * 3
        own, *sent, token = small_call(add_kernel, name, shapes, [kept, got], after, places)
        return own, from_others(sent, ("x", "y")), token

    def sums(name, scale, terms, after, mib=2):
        body = functools.partial(sum_kernel, scale)
        return small_call(body, name, [(part_shape, BF16)], terms, after, None, mib)

    def swapped(part, bit):
        return lax.ppermute(part, "a", [(i, i ^ bit) for i in range(deep)])

    bits = [2**k for k in range(deep.bit_length() - 1)]

    def middle(name, part, other, after, mib=2):
        for bit in bits[1:]:
            part, token = sums(name, None, [part, other], after, mib)
            other, after = swapped(part, bit), [token]
        return part, other, after[0]

    def pack(name, terms, after, mib=2):
        shape = (4,) + part_shape
        packed, token = small_call(pack_kernel, name, [(shape, BF16)], terms, after, None, mib)
        return packed, lax.ppermute(packed, "core", CORES), token

    def merge(name, packed, other, after, mib=2):
        shapes = [((2 * half, q), F32)]
        return small_call(merge_kernel, name, shapes, [packed, other], after, places, mib)

    own, others, token = add("out_add", kept, got, [token])
    sent, kept, token = kernel_grads(
        places, ends, pair, adjoint, trailing, x, up, down, 0, decays, block, [token]
    )
    got = lax.ppermute(sent, "core", CORES)
    out_part, token = sums("out_share", None, [own] + others, [token], mib=FAR)
    out_other = swapped(out_part, 1)
    own, others, token = add("in_add", kept, got, [token])
    out_part, out_other, token = middle("out_mid", out_part, out_other, [token], FAR)
    line = (low_first.shape, BF16)
    low_first, low_last, _ = small_call(
        copy_kernel, "low_edges", [line, line], [low_first, low_last], [token]
    )
    low_up, low_down = row_halo(low_first, low_last)
    in_part, token = sums("in_share", None, [own] + others, [token])
    in_other = swapped(in_part, 1)
    out_part, token = sums(
        "out_total", grad_scale, [out_part, out_other], [token], mib=FAR
    )
    out_others = from_others(out_part, ("x", "y"))
    in_part, in_other, token = middle("in_mid", in_part, in_other, [token])
    outputs, token = outputs_conv(
        low, low_up, low_down, out_kernel.reshape(3, 3 * p, c), x, skip.reshape(1, c), block, token
    )
    in_part, token = sums("in_total", grad_scale, [in_part, in_other], [token])
    in_others = from_others(in_part, ("x", "y"))
    out_packed, out_other, token = pack("out_pack", [out_part] + out_others, [token])
    out_grad, token = merge("out_merge", out_packed, out_other, [token], FAR)
    in_packed, in_other, token = pack("in_pack", [in_part] + in_others, [token])
    in_grad, _ = merge("in_merge", in_packed, in_other, [token])
    return (
        outputs.reshape(inputs.shape),
        in_grad.reshape(in_kernel.shape),
        out_grad.reshape(out_kernel.shape),
    )


def solution(mesh):
    frames = mesh.shape["tm"]
    rows = mesh.shape["row"]
    fine = jax.sharding.Mesh(
        mesh.devices.reshape(frames // 2, 2, rows // 2, 2), ("a", "x", "y", "core")
    )
    cells = P(None, ("a", "x"), ("y", "core"), None, None)
    return jax.shard_map(
        per_device,
        mesh=fine,
        in_specs=(cells, P(("a", "x"), None), P(), P(), P(), cells),
        out_specs=(cells, P(), P()),
        check_vma=False,
    )
```

```python
import functools
import math

import jax
import jax.numpy as jnp
from jax import lax
from jax.experimental import pallas as pl
from jax.experimental.pallas import tpu as pltpu
from jax.sharding import PartitionSpec as P

BF16 = jnp.bfloat16
F32 = jnp.float32


SCALARS = pl.BlockSpec(memory_space=pltpu.SMEM)
ANYWHERE = pl.BlockSpec(memory_space=pl.ANY)
TOKEN = jax.ShapeDtypeStruct((8, 128), F32)
TOKEN_SPEC = pl.BlockSpec((8, 128), lambda *b: (0, 0))


def params(mib=30):
    return pltpu.CompilerParams(
        dimension_semantics=("arbitrary",), vmem_limit_bytes=mib * 1024 * 1024
    )


def cost(flops, nbytes):
    return pl.CostEstimate(flops=int(flops), bytes_accessed=int(nbytes), transcendentals=0)


def shifted(cells, width):
    count = cells.shape[0]
    wide = cells.astype(F32)
    column = lax.broadcasted_iota(jnp.int32, (count, 1), 0) % width
    left = jnp.where(column == 0, 0.0, pltpu.roll(wide, 1, 0))
    right = jnp.where(column == width - 1, 0.0, pltpu.roll(wide, count - 1, 0))
    return jnp.concatenate([left.astype(BF16), cells, right.astype(BF16)], axis=1)


def flat(block):
    return block.reshape(-1, block.shape[-1])


def dot(a, b):
    return jnp.dot(a, b, preferred_element_type=F32)


def interior_body(x_ref, w_ref, out_ref, s_ref):
    frames, rows, width, _ = x_ref.shape
    lines = frames * width
    for r in range(rows):
        s_ref[r] = shifted(flat(x_ref[:, r]), width)

    def conv(first, count, taps):
        lhs = jnp.concatenate(
            [flat(s_ref[first + i - 1 : first + i - 1 + count]) for i in taps], axis=1
        )
        rhs = w_ref[taps[0] : taps[-1] + 1].reshape(len(taps) * w_ref.shape[1], w_ref.shape[2])
        out_ref[first : first + count] = dot(lhs, rhs).reshape(count, frames, width, -1)

    conv(1, rows - 2, (0, 1, 2))
    conv(0, 1, (1, 2))
    conv(rows - 1, 1, (0, 1))


def interior_plain_kernel(x_ref, w_ref, out_ref, s_ref):
    interior_body(x_ref, w_ref, out_ref, s_ref)


def interior_flipped_kernel(x_ref, w_ref, out_ref, wt_ref, s_ref):
    @pl.when(pl.program_id(0) == 0)
    def _():
        for i in range(3):
            for j in range(3):
                c = w_ref.shape[3]
                wt_ref[i, j * c : (j + 1) * c, :] = w_ref[2 - i, 2 - j].T

    interior_body(x_ref, wt_ref, out_ref, s_ref)


def interior_conv(x, w, flipped, block):
    frames, rows, width, c = x.shape
    p = w.shape[2] if flipped else w.shape[3]
    part_shape = jax.ShapeDtypeStruct((rows, frames, width, p), F32)
    part_spec = pl.BlockSpec((rows, block, width, p), lambda b: (0, b, 0, 0))
    x_spec = pl.BlockSpec((block, rows, width, c), lambda b: (b, 0, 0, 0))
    scratch = [pltpu.VMEM((rows, block * width, 3 * c), BF16)]
    estimate = cost(2 * frames * rows * width * 9 * c * p, 8 * 2**20)
    taps_spec = pl.BlockSpec((3, 3 * c, p), lambda b: (0, 0, 0))
    if flipped:
        return pl.pallas_call(
            interior_flipped_kernel,
            grid=(frames // block,),
            in_specs=[
                x_spec,
                pl.BlockSpec(w.shape, lambda b: (0, 0, 0, 0)),
            ],
            out_specs=[part_spec, taps_spec],
            out_shape=[part_shape, jax.ShapeDtypeStruct((3, 3 * c, p), BF16)],
            scratch_shapes=scratch,
            compiler_params=params(),
            cost_estimate=estimate,
            name="interior_cot",
        )(x, w)
    taps = w.reshape(3, 3 * c, p)
    part = pl.pallas_call(
        interior_plain_kernel,
        grid=(frames // block,),
        in_specs=[x_spec, taps_spec],
        out_specs=part_spec,
        out_shape=part_shape,
        scratch_shapes=scratch,
        compiler_params=params(),
        cost_estimate=estimate,
        name="interior_in",
    )(x, taps)
    return part, taps


def scan_kernel(backward, part_ref, up_ref, down_ref, w_ref, decay_ref, before_ref, local_ref, product_ref, end_ref, carry_ref, run_ref):
    rows, frames, width, p = part_ref.shape
    lines = rows * width

    @pl.when(pl.program_id(0) == 0)
    def _():
        carry_ref[...] = jnp.zeros_like(carry_ref)
        run_ref[...] = jnp.ones_like(run_ref)

    top = dot(shifted(flat(up_ref[...]), width), w_ref[0]).reshape(frames, width, p)
    low = dot(shifted(flat(down_ref[...]), width), w_ref[2]).reshape(frames, width, p)
    decay = decay_ref[...]
    scale = jnp.sqrt((1.0 - decay) * (1.0 + decay))
    state = [carry_ref[r * width : (r + 1) * width] for r in range(rows)]
    run = run_ref[0:1]
    for step in range(frames):
        t = frames - 1 - step if backward else step
        factor = decay[t : t + 1]
        gain = scale[t : t + 1]
        if backward:
            product_ref[t : t + 1] = run
        run = run * factor
        if not backward:
            product_ref[t : t + 1] = run
        for r in range(rows):
            term = part_ref[r, t]
            if r == 0:
                term = term + top[t]
            if r == rows - 1:
                term = term + low[t]
            if backward:
                full = term + state[r]
                local_ref[r, t] = full
                state[r] = factor * full
            else:
                state[r] = factor * state[r] + gain * term
                local_ref[r, t] = state[r]
    for r in range(rows):
        carry_ref[r * width : (r + 1) * width] = state[r]
    run_ref[...] = jnp.broadcast_to(run, run_ref.shape)

    @pl.when(pl.program_id(0) == pl.num_programs(0) - 1)
    def _():
        if backward:
            message = [before_ref[...]] + state + [jnp.broadcast_to(run, (8, p))]
        else:
            message = state
        end_ref[...] = jnp.concatenate(message, axis=0)


def local_scan(part, up, down, half, taps, decays, block, backward, before):
    rows, frames, width, p = part.shape
    c = up.shape[-1]
    blocks = frames // block
    at = (lambda b: blocks - 1 - b) if backward else (lambda b: b)
    halo_spec = pl.BlockSpec((None, block, width, c), lambda b: (half, at(b), 0, 0))
    part_spec = pl.BlockSpec((rows, block, width, p), lambda b: (0, at(b), 0, 0))
    frame_spec = pl.BlockSpec((block, p), lambda b: (at(b), 0))
    lines = rows * width
    message = 2 * lines + 8 if backward else lines
    return pl.pallas_call(
        functools.partial(scan_kernel, backward),
        grid=(blocks,),
        in_specs=[
            part_spec,
            halo_spec,
            halo_spec,
            pl.BlockSpec(taps.shape, lambda b: (0, 0, 0)),
            frame_spec,
            pl.BlockSpec(before.shape, lambda b: (0, 0)),
        ],
        out_specs=[part_spec, frame_spec, pl.BlockSpec((message, p), lambda b: (0, 0))],
        out_shape=[
            jax.ShapeDtypeStruct(part.shape, F32),
            jax.ShapeDtypeStruct((frames, p), F32),
            jax.ShapeDtypeStruct((message, p), F32),
        ],
        scratch_shapes=[pltpu.VMEM((lines, p), F32), pltpu.VMEM((8, p), F32)],
        compiler_params=params(),
        cost_estimate=cost(4 * frames * width * 3 * c * p, 12 * 2**20),
        name="scan_back" if backward else "scan_fwd",
    )(part, up, down, taps, decays, before)


def pair_kernel(places_ref, own_ref, got_ref, out_ref):
    deep, height, _ = out_ref.shape
    lines = height - 8
    first = places_ref[1] == 0
    own_end, got_end = own_ref[0:lines], got_ref[0:lines]
    own_start, got_start = own_ref[lines : 2 * lines], got_ref[lines : 2 * lines]
    own_product, got_product = own_ref[2 * lines :], got_ref[2 * lines :]
    end = jnp.where(
        first, got_product[0:1] * own_end + got_end, own_product[0:1] * got_end + own_end
    )
    start = jnp.where(
        first, own_product[0:1] * got_start + own_start, got_product[0:1] * own_start + got_start
    )
    product = own_product * got_product
    for k in range(deep):
        out_ref[k, 0:lines] = jnp.where(k > places_ref[0], end, start)
        out_ref[k, lines:] = product


def combine(places_ref, ends_ref, pair_ref, total_ref, backward):
    place = places_ref[0]
    count = ends_ref.shape[0]
    lines = total_ref.shape[0]
    total = jnp.zeros(total_ref.shape, F32)
    order = range(count - 1, -1, -1) if backward else range(count)
    for k in order:
        passed = ends_ref[k, lines : lines + 1] * total + ends_ref[k, 0:lines]
        total = jnp.where(k > place if backward else k < place, passed, total)
    near = pair_ref[lines : 2 * lines] if backward else pair_ref[0:lines]
    passed = pair_ref[2 * lines : 2 * lines + 1] * total + near
    total_ref[...] = jnp.where(places_ref[1] == (0 if backward else 1), passed, total)


def split_halves(place_ref, sum_ref, sent_ref, kept_ref):
    half = kept_ref.shape[0]
    side = place_ref[2]
    sent_ref[...] = sum_ref[pl.ds(pl.multiple_of((1 - side) * half, 8), half)].astype(BF16)
    kept_ref[...] = sum_ref[pl.ds(pl.multiple_of(side * half, 8), half)]


def fill_rim(s_ref, up_ref, x_ref, down_ref):
    _, rows, width, _ = x_ref.shape
    s_ref[0] = shifted(flat(up_ref[...]), width)
    for r in range(rows):
        s_ref[r + 1] = shifted(flat(x_ref[:, r]), width)
    s_ref[rows + 1] = shifted(flat(down_ref[...]), width)


def out_grad_kernel(place_ref, ends_ref, pair_ref, local_ref, product_ref, cot_ref, up_ref, down_ref, low_ref, first_ref, last_ref, sent_ref, kept_ref, token_ref, s_ref, total_ref, sum_ref):
    rows, frames, width, p = local_ref.shape
    c = cot_ref.shape[-1]

    @pl.when(pl.program_id(0) == 0)
    def _():
        combine(place_ref, ends_ref, pair_ref, total_ref, False)
        sum_ref[...] = jnp.zeros_like(sum_ref)
        token_ref[...] = jnp.zeros_like(token_ref)

    fill_rim(s_ref, up_ref, cot_ref, down_ref)
    product = product_ref[...]
    turned = []
    for r in range(rows):
        state = local_ref[r] + product[:, None, :] * total_ref[r * width : (r + 1) * width][None]
        low = state.astype(BF16)
        low_ref[r] = low
        if r == 0:
            first_ref[...] = low
        if r == rows - 1:
            last_ref[...] = low
        turned.append(flat(low).T)
    turned = jnp.concatenate(turned, axis=1)
    for i in range(3):
        gain = dot(turned, flat(s_ref[2 - i : 2 - i + rows]))
        for j in range(3):
            tap = 3 * i + j
            sum_ref[tap * p : (tap + 1) * p] += gain[:, (2 - j) * c : (3 - j) * c]

    @pl.when(pl.program_id(0) == pl.num_programs(0) - 1)
    def _():
        split_halves(place_ref, sum_ref, sent_ref, kept_ref)


def in_grad_kernel(place_ref, ends_ref, pair_ref, local_ref, product_ref, decay_ref, x_ref, up_ref, down_ref, *refs):
    sent_ref, kept_ref, token_ref, s_ref, total_ref, sum_ref, flat_ref = refs[-7:]
    rows, frames, width, p = local_ref.shape
    c = x_ref.shape[-1]

    @pl.when(pl.program_id(0) == 0)
    def _():
        combine(place_ref, ends_ref, pair_ref, total_ref, True)
        sum_ref[...] = jnp.zeros_like(sum_ref)
        token_ref[...] = jnp.zeros_like(token_ref)

    fill_rim(s_ref, up_ref, x_ref, down_ref)
    product = product_ref[...]
    decay = decay_ref[...]
    scale = jnp.sqrt((1.0 - decay) * (1.0 + decay))[:, None, :]
    turned = []
    for r in range(rows):
        adjoint = local_ref[r] + product[:, None, :] * total_ref[r * width : (r + 1) * width][None]
        turned.append(flat((scale * adjoint).astype(BF16)).T)
    turned = jnp.concatenate(turned, axis=1)
    for i in range(3):
        sum_ref[i] += dot(turned, flat(s_ref[i : i + rows]))

    @pl.when(pl.program_id(0) == pl.num_programs(0) - 1)
    def _():
        for i in range(3):
            for j in range(3):
                tap = 3 * i + j
                flat_ref[tap * c : (tap + 1) * c] = sum_ref[i, :, j * c : (j + 1) * c].T
        split_halves(place_ref, flat_ref, sent_ref, kept_ref)


def kernel_grads(places, ends, pair, local, product, x, up, down, half, decays, block, after=None):
    rows, frames, width, p = local.shape
    c = x.shape[-1]
    halo_spec = pl.BlockSpec((None, block, width, c), lambda b: (half, b, 0, 0))
    local_spec = pl.BlockSpec((rows, block, width, p), lambda b: (0, b, 0, 0))
    frame_spec = pl.BlockSpec((block, p), lambda b: (b, 0))
    x_spec = pl.BlockSpec((block, rows, width, c), lambda b: (b, 0, 0, 0))
    lead = [
        SCALARS,
        pl.BlockSpec(ends.shape, lambda b: (0, 0, 0)),
        pl.BlockSpec(pair.shape, lambda b: (0, 0)),
        local_spec,
        frame_spec,
    ]
    tail = [x_spec, halo_spec, halo_spec]
    scratch = [
        pltpu.VMEM((rows + 2, block * width, 3 * c), BF16),
        pltpu.VMEM((rows * width, p), F32),
    ]
    estimate = cost(2 * frames * rows * width * 9 * c * p, 10 * 2**20)
    forward = decays is None
    lines, columns = (9 * p // 2, c) if forward else (9 * c // 2, p)
    grad_specs = [pl.BlockSpec((lines, columns), lambda b: (0, 0))] * 2 + [TOKEN_SPEC]
    grad_shapes = [
        jax.ShapeDtypeStruct((lines, columns), BF16),
        jax.ShapeDtypeStruct((lines, columns), F32),
        TOKEN,
    ]
    if forward:
        line_spec = pl.BlockSpec((block, width, p), lambda b: (b, 0, 0))
        line = jax.ShapeDtypeStruct((frames, width, p), BF16)
        return pl.pallas_call(
            out_grad_kernel,
            grid=(frames // block,),
            in_specs=lead + tail,
            out_specs=[local_spec, line_spec, line_spec] + grad_specs,
            out_shape=[jax.ShapeDtypeStruct(local.shape, BF16), line, line] + grad_shapes,
            scratch_shapes=scratch + [pltpu.VMEM((2 * lines, columns), F32)],
            compiler_params=params(),
            cost_estimate=estimate,
            name="out_grad",
        )(places, ends, pair, local, product, x, up, down)
    return pl.pallas_call(
        in_grad_kernel,
        grid=(frames // block,),
        in_specs=lead + [frame_spec] + tail + [ANYWHERE] * len(after),
        out_specs=grad_specs,
        out_shape=grad_shapes,
        scratch_shapes=scratch
        + [pltpu.VMEM((3, p, 3 * c), F32), pltpu.VMEM((2 * lines, columns), F32)],
        compiler_params=params(),
        cost_estimate=estimate,
        name="in_grad",
    )(places, ends, pair, local, product, decays, x, up, down, *after)


def outputs_kernel(low_ref, up_ref, down_ref, w_ref, x_ref, skip_ref, after_ref, out_ref, token_ref, s_ref):
    token_ref[...] = jnp.zeros_like(token_ref)
    rows, frames, width, p = low_ref.shape
    s_ref[0] = shifted(flat(up_ref[...]), width)
    for r in range(rows):
        s_ref[r + 1] = shifted(flat(low_ref[r]), width)
    s_ref[rows + 1] = shifted(flat(down_ref[...]), width)
    lhs = jnp.concatenate([flat(s_ref[i : i + rows]) for i in range(3)], axis=1)
    mixed = dot(lhs, flat(w_ref[...])).reshape(rows, frames, width, -1)
    skip = skip_ref[...][0:1].reshape(1, 1, -1)
    for r in range(rows):
        out_ref[:, r] = (mixed[r] + skip * x_ref[:, r].astype(F32)).astype(BF16)


def outputs_conv(low, up, down, taps, x, skip, block, after):
    rows, frames, width, p = low.shape
    c = x.shape[-1]
    halo_spec = pl.BlockSpec((block, width, p), lambda b: (b, 0, 0))
    x_spec = pl.BlockSpec((block, rows, width, c), lambda b: (b, 0, 0, 0))
    return pl.pallas_call(
        outputs_kernel,
        grid=(frames // block,),
        in_specs=[
            pl.BlockSpec((rows, block, width, p), lambda b: (0, b, 0, 0)),
            halo_spec,
            halo_spec,
            pl.BlockSpec(taps.shape, lambda b: (0, 0, 0)),
            x_spec,
            pl.BlockSpec((1, c), lambda b: (0, 0)),
            ANYWHERE,
        ],
        out_specs=[x_spec, TOKEN_SPEC],
        out_shape=[jax.ShapeDtypeStruct(x.shape, BF16), TOKEN],
        scratch_shapes=[pltpu.VMEM((rows + 2, block * width, 3 * p), BF16)],
        compiler_params=params(),
        cost_estimate=cost(2 * frames * rows * width * 9 * c * p, 8 * 2**20),
        name="outputs_conv",
    )(low, up, down, taps, x, skip, after)


def edge_rows_kernel(places_ref, *refs):
    first_ref, last_ref = refs[4:]
    for k in range(2):
        first_ref[k] = refs[2 * k][:, 0]
        last_ref[k] = refs[2 * k + 1][:, 0]


def edge_rows(places, x, cot, block):
    frames, rows, width, c = x.shape
    line = jax.ShapeDtypeStruct((2, frames, width, c), x.dtype)
    line_spec = pl.BlockSpec((2, block, width, c), lambda b: (0, b, 0, 0))
    first = pl.BlockSpec((block, 1, width, c), lambda b: (b, 0, 0, 0))
    last = pl.BlockSpec((block, 1, width, c), lambda b: (b, rows - 1, 0, 0))
    return pl.pallas_call(
        edge_rows_kernel,
        grid=(frames // block,),
        in_specs=[SCALARS, first, last, first, last],
        out_specs=[line_spec, line_spec],
        out_shape=[line, line],
        compiler_params=params(56),
        cost_estimate=cost(0, 2**22),
        name="edge_rows",
    )(places, x, x, cot, cot)


def row_halo(first, last):
    axes = ("y", "core")
    count = lax.axis_size("y") * lax.axis_size("core")
    up = lax.ppermute(last, axes, [(i, i + 1) for i in range(count - 1)])
    down = lax.ppermute(first, axes, [(i + 1, i) for i in range(count - 1)])
    return up, down


CORES = [(0, 1), (1, 0)]
FAR = 64


def small_call(body, name, out_shapes, operands, after, places=None, mib=2):
    extra = [] if places is None else [places]

    def kernel(*refs):
        body(*refs[len(after) : -1])
        refs[-1][...] = jnp.zeros_like(refs[-1])

    whole = pl.BlockSpec(memory_space=pltpu.VMEM)
    return pl.pallas_call(
        kernel,
        in_specs=[ANYWHERE] * len(after) + [SCALARS] * len(extra) + [whole] * len(operands),
        out_specs=[whole] * (len(out_shapes) + 1),
        out_shape=[jax.ShapeDtypeStruct(*shape) for shape in out_shapes] + [TOKEN],
        compiler_params=pltpu.CompilerParams(vmem_limit_bytes=10 * 2**20),
        cost_estimate=cost(mib * 2**29, 2**21),
        name=name,
    )(*after, *extra, *operands)


def quarter(index, ref):
    size = ref.shape[0] // 4
    return pl.ds(pl.multiple_of(index * size, 16), size)


def add_kernel(places_ref, kept_ref, got_ref, own_ref, *sent_refs):
    for k, ref in enumerate((own_ref,) + sent_refs):
        at = quarter(jnp.bitwise_xor(places_ref[3], k), kept_ref)
        ref[...] = (kept_ref[at] + got_ref[at].astype(F32)).astype(ref.dtype)


def tree(terms):
    while len(terms) > 1:
        terms = [terms[k] + terms[k + 1] for k in range(0, len(terms), 2)]
    return terms[0]


def sum_kernel(scale, *refs):
    total = tree([ref[...].astype(F32) for ref in refs[:-1]])
    if scale is not None:
        total = total * scale
    refs[-1][...] = total.astype(BF16)


def copy_kernel(first_ref, last_ref, first_out_ref, last_out_ref):
    first_out_ref[...] = first_ref[...]
    last_out_ref[...] = last_ref[...]


def pack_kernel(*refs):
    for k, ref in enumerate(refs[:-1]):
        refs[-1][k] = ref[...]


def merge_kernel(places_ref, own_ref, other_ref, out_ref):
    count, lines, _ = own_ref.shape
    for side, ref in enumerate((own_ref, other_ref)):
        for k in range(count):
            index = jnp.bitwise_xor(places_ref[2], side) * count
            index = index + jnp.bitwise_xor(places_ref[3], k)
            at = pl.ds(pl.multiple_of(index * lines, 16), lines)
            out_ref[at] = ref[k].astype(F32)


def from_others(sent, axes):
    count = math.prod(lax.axis_size(name) for name in axes)
    if not isinstance(sent, list):
        sent = [sent] * (count - 1)
    return [
        lax.ppermute(part, axes, [(i, i ^ k) for i in range(count)])
        for k, part in enumerate(sent, 1)
    ]


def per_device(inputs, decays, in_kernel, out_kernel, skip, cotangent):
    clips, frames, rows, width, c = inputs.shape
    p = in_kernel.shape[3]
    block = 32
    devices = math.prod(lax.axis_size(name) for name in ("a", "x", "y", "core"))
    grad_scale = 1.0 / math.sqrt(clips * frames * rows * width * devices)
    x = inputs.reshape(frames, rows, width, c)
    cot = cotangent.reshape(frames, rows, width, c)
    places = jnp.stack([lax.axis_index(name) for name in ("a", "x", "core", ("x", "y"))])
    places = places.astype(jnp.int32)
    deep = lax.axis_size("a")
    lines = rows * width

    up, down = row_halo(*edge_rows(places, x, cot, frames))
    x_part, x_taps = interior_conv(x, in_kernel, False, block)
    cot_part, cot_taps = interior_conv(cot, out_kernel, True, block)
    states, running, end = local_scan(x_part, up, down, 0, x_taps, decays, block, False, decays)
    adjoint, trailing, message = local_scan(
        cot_part, up, down, 1, cot_taps, decays, block, True, end
    )
    pair = lax.ppermute(message, "x", [(0, 1), (1, 0)])
    ends, token = small_call(
        pair_kernel, "pair", [((deep, lines + 8, p), F32)], [message, pair], [], places
    )
    ends = lax.all_to_all(ends, "a", 0, 0)

    low, low_first, low_last, sent, kept, token = kernel_grads(
        places, ends, pair, states, running, cot, up, down, 1, None, block
    )
    got = lax.ppermute(sent, "core", CORES)
    half, q = kept.shape
    part_shape = (half // 4, q)

    def add(name, kept, got, after):
        shapes = [(part_shape, F32)] + [(part_shape, BF16)] * 3
        own, *sent, token = small_call(add_kernel, name, shapes, [kept, got], after, places)
        return own, from_others(sent, ("x", "y")), token

    def sums(name, scale, terms, after, mib=2):
        body = functools.partial(sum_kernel, scale)
        return small_call(body, name, [(part_shape, BF16)], terms, after, None, mib)

    def swapped(part, bit):
        return lax.ppermute(part, "a", [(i, i ^ bit) for i in range(deep)])

    bits = [2**k for k in range(deep.bit_length() - 1)]

    def middle(name, part, other, after, mib=2):
        for bit in bits[1:]:
            part, token = sums(name, None, [part, other], after, mib)
            other, after = swapped(part, bit), [token]
        return part, other, after[0]

    def pack(name, terms, after, mib=2):
        shape = (4,) + part_shape
        packed, token = small_call(pack_kernel, name, [(shape, BF16)], terms, after, None, mib)
        return packed, lax.ppermute(packed, "core", CORES), token

    def merge(name, packed, other, after, mib=2):
        shapes = [((2 * half, q), F32)]
        return small_call(merge_kernel, name, shapes, [packed, other], after, places, mib)

    own, others, token = add("out_add", kept, got, [token])
    sent, kept, token = kernel_grads(
        places, ends, pair, adjoint, trailing, x, up, down, 0, decays, block, [token]
    )
    got = lax.ppermute(sent, "core", CORES)
    out_part, token = sums("out_share", None, [own] + others, [token], mib=FAR)
    out_other = swapped(out_part, 1)
    own, others, token = add("in_add", kept, got, [token])
    out_part, out_other, token = middle("out_mid", out_part, out_other, [token], FAR)
    line = (low_first.shape, BF16)
    low_first, low_last, _ = small_call(
        copy_kernel, "low_edges", [line, line], [low_first, low_last], [token]
    )
    low_up, low_down = row_halo(low_first, low_last)
    in_part, token = sums("in_share", None, [own] + others, [token])
    in_other = swapped(in_part, 1)
    out_part, token = sums(
        "out_total", grad_scale, [out_part, out_other], [token], mib=FAR
    )
    out_others = from_others(out_part, ("x", "y"))
    in_part, in_other, token = middle("in_mid", in_part, in_other, [token])
    in_part, token = sums("in_total", grad_scale, [in_part, in_other], [token])
    in_others = from_others(in_part, ("x", "y"))
    out_packed, out_other, token = pack("out_pack", [out_part] + out_others, [token])
    outputs, token = outputs_conv(
        low, low_up, low_down, out_kernel.reshape(3, 3 * p, c), x, skip.reshape(1, c), block, token
    )
    in_packed, in_other, token = pack("in_pack", [in_part] + in_others, [token])
    out_grad, token = merge("out_merge", out_packed, out_other, [token], FAR)
    in_grad, _ = merge("in_merge", in_packed, in_other, [token])
    return (
        outputs.reshape(inputs.shape),
        in_grad.reshape(in_kernel.shape),
        out_grad.reshape(out_kernel.shape),
    )


def solution(mesh):
    frames = mesh.shape["tm"]
    rows = mesh.shape["row"]
    fine = jax.sharding.Mesh(
        mesh.devices.reshape(frames // 2, 2, rows // 2, 2), ("a", "x", "y", "core")
    )
    cells = P(None, ("a", "x"), ("y", "core"), None, None)
    return jax.shard_map(
        per_device,
        mesh=fine,
        in_specs=(cells, P(("a", "x"), None), P(), P(), P(), cells),
        out_specs=(cells, P(), P()),
        check_vma=False,
    )
```
